128 devices in a mesh: dp: 16 (over x, z), seq: 8 (over y, core).
Axes of the slice: x: 4, y: 4, z: 4, core: 2. Of those that a mesh axis runs over, the one named last changes fastest.
Arguments:
- hidden: bfloat16 [16384, 4096], P(('dp', 'seq')), may hold values from -6 to 6
- w_query: bfloat16 [4096, 2048], P('dp'), may hold values from -0.09375 to 0.09375
- nbr_keys: bfloat16 [512, 128, 2048], P(('dp', 'seq')), may hold values from -50 to 50
- nbr_values: bfloat16 [512, 128, 2048], P(('dp', 'seq')), may hold values from -6 to 6
- nbr_ids: int32 [256, 2], P(('dp', 'seq')), may hold values from 0 to 31, as said below
- d_attended: bfloat16 [16384, 2048], P(('dp', 'seq')), may hold values from -6 to 6
Outputs:
- attended: bfloat16 [16384, 2048], P(('dp', 'seq'))
- d_hidden: bfloat16 [16384, 4096], P(('dp', 'seq'))
- d_wq: float32 [4096, 2048], P('seq', 'dp')
- d_keys: float32 [512, 128, 2048], P(('dp', 'seq'))
- d_values: float32 [512, 128, 2048], P(('dp', 'seq'))
The draws below stay inside these ranges and needn't reach their ends.
Inputs may be any that keep to these rules, and one draw needn't show every extreme that they name: `nbr_ids`: the 4 ids held by one device (2 blocks × 2 neighbours) are distinct and lie in 4 different seq shards of the group (the shard of an id is id // 4).
All inputs are finite; a program needn't handle non-finite values.
Results may differ from the reference program's by a relative error of at most 0.019.
The reference program's roundings to bfloat16 on the way (of `query`, `probs_low`, `d_scores` and `d_query`) count: a program that leaves them out, or rounds other values in their place, can miss the bound.
Values may be sent and summed in bfloat16 or wider, within the bound.
A program may use at most 128 MiB of HBM per device.

```python
import jax
import jax.numpy as jnp
from jax import lax

D = 4096
HEADS = 16
HEAD_DIM = 128
BLOCK = 64
NEIGH = 2
NLEN = 128
C_DEV = 2
NB_DEV = 4
HD = 2048
TOKENS = 16384
POOL = 512
N_DP = 16
N_SEQ = 8


def draw_nbr_keys(key, part):
    key = jax.random.fold_in(key, 11)
    first = jax.random.fold_in(key, 0)
    return jax.random.normal(first, (POOL, NLEN, HD), jnp.float32).astype(jnp.bfloat16)


def draw_nbr_ids(key, part):
    key = jax.random.fold_in(key, 5)
    first, second, third, fourth = jax.random.split(key, 4)
    requests = NEIGH * C_DEV
    capacity = (requests + N_SEQ - 1) // N_SEQ
    devices = N_DP * N_SEQ
    slots = N_SEQ * capacity
    ranking = jax.random.permutation(first, N_SEQ).astype(jnp.int32)
    slot_shard = jnp.arange(slots, dtype=jnp.int32) // capacity
    slot_repeat = jnp.arange(slots, dtype=jnp.int32) % capacity
    noise = jax.random.randint(second, (devices, slots), 0, 256, dtype=jnp.int32)
    scores = (noise + 64 * ranking[slot_shard][None, :]) * slots + jnp.arange(slots, dtype=jnp.int32)[None, :]
    chosen = jnp.argsort(scores, axis=1)[:, :requests]
    mixing = jax.random.randint(third, (devices, requests), 0, 4096, dtype=jnp.int32) * requests + jnp.arange(requests, dtype=jnp.int32)[None, :]
    chosen = jnp.take_along_axis(chosen, jnp.argsort(mixing, axis=1), axis=1)
    shard = slot_shard[chosen]
    repeat = slot_repeat[chosen]
    offsets = jax.random.randint(fourth, (devices, N_SEQ), 0, NB_DEV, dtype=jnp.int32)
    local = (jnp.take_along_axis(offsets, shard, axis=1) + repeat) % NB_DEV
    return (shard * NB_DEV + local).reshape(devices * C_DEV, NEIGH).astype(jnp.int32)


def steps_of(rng, shape, pieces, least, top_value):
    def one(axis_at, parts):
        steps = jax.random.uniform(jax.random.fold_in(jax.random.fold_in(rng, 6), axis_at), (parts,), jnp.float32, least / len(pieces), top_value / len(pieces))
        return jnp.repeat(jnp.exp(steps), shape[axis_at] // parts).reshape((-1,) + (1,) * (len(shape) - axis_at - 1))

    loudness = one(*pieces[0])
    for cut in pieces[1:]:
        loudness = loudness * one(*cut)
    return loudness


def bell_draw(key, extent, width, limit, shards=(), held_as=jnp.bfloat16):
    result = width * jax.random.normal(key, extent, jnp.float32)
    if shards:
        result = result * steps_of(key, extent, shards, -0.22, 0.18)
    return jnp.clip(result, -limit, limit).astype(held_as)


def setup_inputs(seed: int = 0) -> dict:
    key_of = jax.random.split(jax.random.key(seed), 7)
    hidden = bell_draw(key_of[0], (TOKENS, D), 1.0, 6.0, ((0, 128),))
    w_query = bell_draw(key_of[1], (D, HD), D ** -0.5, 0.09375, ((0, 16),))
    nbr_keys = draw_nbr_keys(jax.random.fold_in(key_of[6], 71), 0)
    nbr_values = bell_draw(key_of[3], (POOL, NLEN, HD), 1.0, 6.0, ((0, 128),))
    nbr_ids = draw_nbr_ids(jax.random.fold_in(key_of[6], 71), 0)
    d_attended = bell_draw(key_of[5], (TOKENS, HD), 1.0, 6.0, ((0, 128),))
    return dict(hidden=hidden, w_query=w_query, nbr_keys=nbr_keys, nbr_values=nbr_values, nbr_ids=nbr_ids, d_attended=d_attended)


def lowered(values):
    return lax.optimization_barrier(values.astype(jnp.bfloat16)).astype(jnp.float32)


def reference(hidden, w_query, nbr_keys, nbr_values, nbr_ids, d_attended):
    query = jnp.dot(hidden, w_query, preferred_element_type=jnp.float32).astype(jnp.bfloat16)
    block_count = nbr_ids.shape[0]
    group_of = jnp.arange(block_count, dtype=jnp.int32) // (C_DEV * N_SEQ)
    global_ids = nbr_ids.astype(jnp.int32) + (group_of * (NB_DEV * N_SEQ))[:, None]
    flat_ids = global_ids.reshape(-1)
    keys = jnp.take(nbr_keys, flat_ids, axis=0).astype(jnp.float32).reshape(block_count, NEIGH * NLEN, HEADS, HEAD_DIM)
    values = jnp.take(nbr_values, flat_ids, axis=0).astype(jnp.float32).reshape(block_count, NEIGH * NLEN, HEADS, HEAD_DIM)
    queries = query.astype(jnp.float32).reshape(block_count, BLOCK, HEADS, HEAD_DIM)
    scale = HEAD_DIM ** -0.5
    scores = jnp.einsum('cqhd,ckhd->chqk', queries, keys) * scale
    peak = jnp.max(scores, axis=-1, keepdims=True)
    expo = jnp.exp(scores - peak)
    probs = expo / jnp.sum(expo, axis=-1, keepdims=True)
    probs_low = lowered(probs)
    attended = jnp.einsum('chqk,ckhd->cqhd', probs_low, values).astype(jnp.bfloat16).reshape(TOKENS, HD)
    grads = d_attended.astype(jnp.float32).reshape(block_count, BLOCK, HEADS, HEAD_DIM)
    d_probs = jnp.einsum('cqhd,ckhd->chqk', grads, values)
    delta = jnp.sum(probs * d_probs, axis=-1, keepdims=True)
    d_scores = lowered(probs * (d_probs - delta) * scale)
    d_query = jnp.einsum('chqk,ckhd->cqhd', d_scores, keys).astype(jnp.bfloat16).reshape(TOKENS, HD)
    key_parts = lowered(jnp.einsum('chqk,cqhd->ckhd', d_scores, queries)).reshape(block_count * NEIGH, NLEN, HD)
    value_parts = lowered(jnp.einsum('chqk,cqhd->ckhd', probs_low, grads)).reshape(block_count * NEIGH, NLEN, HD)
    d_keys = jax.ops.segment_sum(key_parts, flat_ids, num_segments=POOL)
    d_values = jax.ops.segment_sum(value_parts, flat_ids, num_segments=POOL)
    d_hidden = lax.dot_general(d_query, w_query, (((1,), (1,)), ((), ())), preferred_element_type=jnp.float32).astype(jnp.bfloat16)
    d_wq = lax.dot_general(hidden, d_query, (((0,), (0,)), ((), ())), preferred_element_type=jnp.float32)
    return attended, d_hidden, d_wq, d_keys, d_values
```

```python
import functools

import jax
import jax.numpy as jnp
from jax import lax
from jax.experimental import pallas as pl
from jax.experimental.pallas import tpu as pltpu
from jax.sharding import PartitionSpec as P

BF16 = jnp.bfloat16
F32 = jnp.float32
MESH = pl.DeviceIdType.MESH
HEAD = 128
SCALE = HEAD ** (-0.5)
BLOCK = 64
NLEN = 128


class Pool:
    def __init__(self):
        self.used = 0

    def take(self, count):
        first = self.used
        self.used += count
        return first


POOL = Pool()
S_W = POOL.take(40)
S_KV = POOL.take(32)
S_DO = POOL.take(8)
S_ID = POOL.take(8)
S_HID = POOL.take(1)
S_Q = POOL.take(4)
S_HS = POOL.take(4)
S_HF = POOL.take(4)
S_ATT = POOL.take(16)
S_DQ = POOL.take(8)
S_DKV = POOL.take(32)
S_DH = POOL.take(1)
S_RS = POOL.take(16)
S_LOCAL = POOL.take(16)
N_SEMS = POOL.used


def dot(a, b, dims=((1,), (0,))):
    return lax.dot_general(a, b, (dims, ((), ())), preferred_element_type=F32)


def kernel(
    hidden, weight, keys, values, ids, grads,
    att_out, dh_out, dwq_out, dk_out, dv_out,
    hid, wb, kh0, kh1, vh0, vh1, doh, qh, qacc, qs, hs, ht, ck, cv, dks, dvs, atth, dqg, dqc, pw, rsb,
    dhs, dhr, dho, idg, ids_s, ssem, rsem,
):
    dp = lax.axis_index("dp")
    seq = lax.axis_index("seq")
    x, z = dp // 4, dp % 4
    y, c = seq // 2, seq % 2
    half = c * 1024
    kh, vh = (kh0, kh1), (vh0, vh1)

    def remote(src, dst, sem, to):
        return pltpu.make_async_remote_copy(
            src_ref=src, dst_ref=dst, send_sem=ssem.at[sem], recv_sem=rsem.at[sem],
            device_id=to, device_id_type=MESH,
        )

    def local(src, dst, sem):
        return pltpu.make_async_copy(src, dst, ssem.at[S_LOCAL + sem])

    def peer(dy, dc):
        return ((y + dy + 4) % 4) * 2 + (c + dc) % 2

    def cols(seq_of, h):
        return pl.multiple_of(((seq_of % 2) * 8 + (seq_of // 2) * 2 + h) * HEAD, HEAD)

    sibling = peer(0, 1)
    others = [(dy, dc) for dy in (1, 3, 2, 0) for dc in (0, 1) if (dy, dc) != (0, 0)]

    own_w = local(weight.at[:, pl.ds(pl.multiple_of(half, 1024), 1024)], wb.at[dp], 0)
    own_hid = local(hidden, hid.at[pl.ds(pl.multiple_of(c * 128, 128), 128)], 1)
    own_w.start()
    own_hid.start()
    rows4 = pl.ds(seq * 4, 4)
    own_kv = []
    for h in range(2):
        for i, (src, dst) in enumerate(((keys, kh), (values, vh))):
            own_kv.append(local(src.at[:, :, pl.ds(cols(seq, h), HEAD)], dst[h].at[rows4], 2 + 2 * h + i))
            own_kv[-1].start()
    own_tokens = pl.ds(pl.multiple_of(seq * 128, 128), 128)
    own_do = local(grads.at[:, pl.ds(cols(seq, 0), 2 * HEAD)], doh.at[own_tokens], 6)
    own_do.start()

    barrier = pltpu.get_barrier_semaphore()

    def greet(to):
        pl.semaphore_signal(barrier, inc=1, device_id=to, device_id_type=MESH)

    around = [
        (((x + 1) % 4) * 4 + z, seq), (((x + 3) % 4) * 4 + z, seq),
        (x * 4 + (z + 1) % 4, seq), (x * 4 + (z + 3) % 4, seq),
    ]
    for to in around:
        greet(to)
    for dy, dc in others:
        greet((dp, peer(dy, dc)))
    sender_core = dp // 8

    @pl.loop(0, 16)
    def _(k):
        @pl.when(jnp.logical_or(k != dp, c != sender_core))
        def _():
            greet((k, y * 2 + sender_core))

    own_block = jnp.where(c == sender_core, 1, 0)
    pl.semaphore_wait(barrier, 4 + 7 + 16 - own_block)

    def moved(axis, step):
        if axis == 0:
            return (((x + step + 4) % 4) * 4 + z, seq)
        return (x * 4 + (z + step + 4) % 4, seq)

    def source(t, r1, r2):
        rx, rz = (r1, r2) if t == 0 else (r2, r1)
        return ((x + rx + 4) % 4) * 4 + (z + rz + 4) % 4

    LINE = (0, -1, 1, 2)

    def piece(t, r1, r2, part):
        lo, n = {"all": (0, 128), "lo": (0, 64), "hi": (64, 64)}[part]
        return wb.at[source(t, r1, r2), pl.ds(t * 128 + lo, n)]

    def w_copy(t, phase, q, slot):
        axis = t if phase == 1 else 1 - t
        sem = S_W + 20 * t + (slot if phase == 1 else 4 + 4 * q + slot)
        step = 1 if slot % 2 == 0 else -1
        near = 0 if slot < 2 else -step
        part = "all" if slot < 2 else ("lo" if slot == 2 else "hi")
        src = piece(t, near, 0, part) if phase == 1 else piece(t, LINE[q], near, part)
        return remote(src, src, sem, moved(axis, step))

    def w_recv(t, phase, q, slot):
        axis = t if phase == 1 else 1 - t
        sem = S_W + 20 * t + (slot if phase == 1 else 4 + 4 * q + slot)
        step = 1 if slot % 2 == 0 else -1
        far = -step if slot < 2 else -2 * step
        part = "all" if slot < 2 else ("lo" if slot == 2 else "hi")
        if far == -2:
            far = 2
        dst = piece(t, far, 0, part) if phase == 1 else piece(t, LINE[q], far, part)
        remote(dst, dst, sem, moved(axis, step)).wait_recv()

    sent = []

    def go(copy):
        copy.start()
        sent.append(copy)

    own_w.wait()
    for t in (0, 1):
        for slot in (0, 1):
            go(w_copy(t, 1, 0, slot))
    for t in (0, 1):
        for slot in (0, 1):
            go(w_copy(t, 2, 0, slot))

    for j, (dy, dc) in enumerate(others):
        go(remote(ids, idg.at[seq], S_ID + j, (dp, peer(dy, dc))))
    own_hid.wait()
    own_hid_rows = hid.at[pl.ds(pl.multiple_of(c * 128, 128), 128)]
    hid_copy = remote(own_hid_rows, own_hid_rows, S_HID, (dp, sibling))
    go(hid_copy)

    def kv_sem(h, i, j):
        return S_KV + (h * 2 + i) * 8 + j

    for h in range(2):
        for i, (src, dst) in enumerate(((keys, kh), (values, vh))):
            for j, (dy, dc) in enumerate(others):
                to = peer(dy, dc)
                go(remote(src.at[:, :, pl.ds(cols(to, h), HEAD)], dst[h].at[rows4], kv_sem(h, i, j), (dp, to)))
        if h == 0:
            for j, (dy, dc) in enumerate(others):
                to = peer(dy, dc)
                go(remote(grads.at[:, pl.ds(cols(to, 0), 2 * HEAD)], doh.at[own_tokens], S_DO + j, (dp, to)))

    for t in (0, 1):
        for slot, q in ((0, 1), (1, 2)):
            w_recv(t, 1, 0, slot)
            go(w_copy(t, 1, 0, slot + 2))
            for s in (0, 1):
                go(w_copy(t, 2, q, s))
    for t in (0, 1):
        for slot in (0, 1):
            w_recv(t, 2, 0, slot)
            go(w_copy(t, 2, 0, slot + 2))
    other_rows = hid.at[pl.ds(pl.multiple_of((1 - c) * 128, 128), 128)]
    remote(other_rows, other_rows, S_HID, (dp, sibling)).wait_recv()
    for t in (0, 1):
        for slot in (2, 3):
            w_recv(t, 1, 0, slot)
        for s in (0, 1):
            go(w_copy(t, 2, 3, s))
    for q in (1, 2):
        for t in (0, 1):
            for slot in (0, 1):
                w_recv(t, 2, q, slot)
                go(w_copy(t, 2, q, slot + 2))

    def project(rx, first):
        @pl.loop(0, 4)
        def _(i):
            d = ((x + rx + 4) % 4) * 4 + i
            rows = hid[:, pl.ds(pl.multiple_of(d * 256, 256), 256)]
            for n in range(4):
                span = slice(n * 256, n * 256 + 256)
                part = dot(rows, wb[d, :, span])
                if first:
                    qacc[:, span] = jnp.where(i == 0, part, qacc[:, span] + part)
                else:
                    qacc[:, span] += part

    qacc[...] = jnp.zeros_like(qacc)
    for t in (0, 1):
        for slot in (0, 1):
            w_recv(t, 2, 3, slot)
            go(w_copy(t, 2, 3, slot + 2))
    for slot in (2, 3):
        w_recv(0, 2, 0, slot)
    project(0, False)
    for slot in (2, 3):
        w_recv(0, 2, 1, slot)
    project(-1, False)
    for slot in (2, 3):
        w_recv(0, 2, 2, slot)
    project(1, False)
    for slot in (2, 3):
        w_recv(0, 2, 3, slot)
        for q in range(4):
            w_recv(1, 2, q, slot)
    project(2, False)
    qs[...] = qacc[...].astype(BF16)

    def span256(k):
        return pl.ds(pl.multiple_of(k * 256, 256), 256)

    for dy in (1, 3, 2):
        to = peer(dy, 0)
        go(remote(qs.at[:, span256(to // 2)], qh.at[span256(y)], S_Q + dy, (dp, to)))
    qh[span256(y), :] = qs[:, span256(y)]

    def feats(k):
        return pl.ds(pl.multiple_of(k * 1024, 1024), 1024)

    def tokens(s):
        return pl.ds(pl.multiple_of(s * 128, 128), 128)

    for dy in (1, 3, 2):
        to = peer(dy, 0)
        go(remote(own_hid_rows.at[:, feats(to // 2)], hs.at[own_tokens], S_HS + dy, (dp, to)))
    hs[span256(y), :] = hid[:, feats(y)]

    for j, (dy, dc) in enumerate(others):
        frm = peer(-dy, -dc + 2)
        remote(ids, idg.at[frm], S_ID + j, (dp, frm)).wait_recv()
    idg[seq] = ids[...]
    to_smem = local(idg, ids_s, 7)
    to_smem.start()
    to_smem.wait()
    for j, (dy, dc) in enumerate(others):
        frm = peer(-dy, -dc + 2)
        dst = doh.at[tokens(frm)]
        remote(dst, dst, S_DO + j, (dp, frm)).wait_recv()
    own_do.wait()
    for cp in own_kv:
        cp.wait()

    def wait_kv(h):
        for i, dst in enumerate((kh, vh)):
            for j, (dy, dc) in enumerate(others):
                frm = peer(-dy, -dc + 2)
                ref = dst[h].at[pl.ds(frm * 4, 4)]
                remote(ref, ref, kv_sem(h, i, j), (dp, frm)).wait_recv()

    wait_kv(0)
    for dy in (1, 3, 2):
        frm = peer(-dy, 0)
        ref = qh.at[span256(frm // 2)]
        remote(ref, ref, S_Q + dy, (dp, frm)).wait_recv()

    ck[32] = jnp.zeros((NLEN, HEAD), BF16)
    cv[32] = jnp.zeros((NLEN, HEAD), BF16)

    def attend(h):
        lanes = slice(h * HEAD, h * HEAD + HEAD)

        @pl.loop(0, 8)
        def _(s):
            for u in range(2):
                rows = pl.ds(pl.multiple_of(s * 128 + u * BLOCK, BLOCK), BLOCK)
                first, second = ids_s[s, 0, 2 * u], ids_s[s, 0, 2 * u + 1]
                k = jnp.concatenate([kh[h][first], kh[h][second]], axis=0)
                v = jnp.concatenate([vh[h][first], vh[h][second]], axis=0)
                q = qh[rows, lanes]
                g = doh[rows, lanes]
                scores = dot(q, k, ((1,), (1,))) * SCALE
                peak = jnp.max(scores, axis=-1, keepdims=True)
                expo = jnp.exp(scores - peak)
                probs = expo / jnp.sum(expo, axis=-1, keepdims=True)
                low = probs.astype(BF16)
                atth[h, rows] = dot(low, v).astype(BF16)
                d_probs = dot(g, v, ((1,), (1,)))
                delta = jnp.sum(probs * d_probs, axis=-1, keepdims=True)
                d_scores = (probs * (d_probs - delta) * SCALE).astype(BF16)
                dqg[h, y, rows] = dot(d_scores, k).astype(BF16)
                dk = dot(d_scores, q, ((0,), (0,))).astype(BF16)
                dv = dot(low, g, ((0,), (0,))).astype(BF16)
                for i in range(2):
                    ck[s * 4 + 2 * u + i] = dk[i * NLEN:(i + 1) * NLEN]
                    cv[s * 4 + 2 * u + i] = dv[i * NLEN:(i + 1) * NLEN]

    def dq_copy(h, slot):
        step = 1 if slot % 2 == 0 else -1
        near = y if slot < 2 else (y - step + 4) % 4
        rows = {0: pl.ds(0, 1024), 1: pl.ds(0, 1024), 2: pl.ds(0, 512), 3: pl.ds(512, 512)}[slot]
        ref = dqg.at[h, near, rows]
        return remote(ref, ref, S_DQ + 4 * h + slot, (dp, peer(step, 0)))

    def dq_recv(h, slot):
        step = 1 if slot % 2 == 0 else -1
        far = (y - step + 4) % 4 if slot < 2 else (y + 2) % 4
        rows = {0: pl.ds(0, 1024), 1: pl.ds(0, 1024), 2: pl.ds(0, 512), 3: pl.ds(512, 512)}[slot]
        ref = dqg.at[h, far, rows]
        remote(ref, ref, S_DQ + 4 * h + slot, (dp, peer(step, 0))).wait_recv()

    def dkv_copy(h, i, j):
        dy, dc = j // 2, j % 2
        to = peer(dy, dc)
        src, dst = ((dks, dk_out), (dvs, dv_out))[i]
        return remote(
            src.at[h, pl.ds(to * 4, 4)], dst.at[:, :, pl.ds(cols(seq, h), HEAD)],
            S_DKV + (h * 2 + i) * 8 + j, (dp, to),
        )

    def return_kv(h):
        def accumulate(to):
            @pl.loop(0, 4)
            def _(r):
                row = to * 4 + r
                total_k = jnp.zeros((NLEN, HEAD), F32)
                total_v = jnp.zeros((NLEN, HEAD), F32)
                for s in range(8):
                    at = jnp.int32(32)
                    for j in range(4):
                        at = jnp.where(ids_s[s, 0, j] == row, 4 * s + j, at)
                    total_k += ck[at].astype(F32)
                    total_v += cv[at].astype(F32)
                dks[h, row] = total_k.astype(BF16)
                dvs[h, row] = total_v.astype(BF16)

        @pl.loop(0, 8)
        def _(jj):
            j = (jj + 1) % 8
            accumulate(peer(j // 2, j % 2))

            @pl.when(j != 0)
            def _():
                for i in range(2):
                    dkv_copy(h, i, j).start()

        for i, (src, dst) in enumerate(((dks, dk_out), (dvs, dv_out))):
            local(src.at[h, rows4], dst.at[:, :, pl.ds(cols(seq, h), HEAD)], 8 + 2 * h + i).start()

    def att_copy(h, j):
        dy, dc = others[j]
        to = peer(dy, dc)
        return remote(
            atth.at[h, tokens(to)], att_out.at[:, pl.ds(cols(seq, h), HEAD)],
            S_ATT + 8 * h + j, (dp, to),
        )

    def forward_hidden():
        for dy in (1, 3, 2):
            frm = peer(-dy, 0)
            ref = hs.at[tokens(frm)]
            remote(ref, ref, S_HS + dy, (dp, frm)).wait_recv()
            go(remote(ref, ref, S_HF + dy, (dp, sibling)))

    attend(0)
    for slot in (0, 1):
        go(dq_copy(0, slot))
    forward_hidden()
    return_kv(0)
    wait_kv(1)
    attend(1)
    for slot in (0, 1):
        go(dq_copy(1, slot))
    for slot in (0, 1):
        dq_recv(0, slot)
        go(dq_copy(0, slot + 2))
    return_kv(1)
    for slot in (0, 1):
        dq_recv(1, slot)
        go(dq_copy(1, slot + 2))
    for h in range(2):
        for j in range(7):
            go(att_copy(h, j))
        local(atth.at[h, own_tokens], att_out.at[:, pl.ds(cols(seq, h), HEAD)], 12 + h).start()

    for dy in (1, 3, 2):
        frm = peer(-dy, 1)
        ref = hs.at[tokens(frm)]
        remote(ref, ref, S_HF + dy, (dp, sibling)).wait_recv()

    @pl.loop(0, 4)
    def _(m):
        ht[span256(m), :] = jnp.transpose(hs[:, span256(m)])

    def rs_copy(i, other_core):
        to_core = (c + other_core) % 2
        return remote(
            pw.at[i, pl.ds(pl.multiple_of(to_core * 512, 512), 512)], rsb.at[dp],
            S_RS + 0, (8 * c + i, y * 2 + to_core),
        )

    def rs_send(i, other_core):
        to_core = (c + other_core) % 2
        return pltpu.make_async_remote_copy(
            src_ref=pw.at[i, pl.ds(pl.multiple_of(to_core * 512, 512), 512)], dst_ref=rsb.at[dp],
            send_sem=ssem.at[S_RS + 2 * i + other_core], recv_sem=rsem.at[S_RS + dp],
            device_id=(8 * c + i, y * 2 + to_core), device_id_type=MESH,
        )

    def own_rs():
        return local(
            pw.at[dp % 8, pl.ds(pl.multiple_of(c * 512, 512), 512)], rsb.at[dp], 14
        )

    def weight_grad(dy):
        yy = (y + dy) % 4
        both = jnp.concatenate([dqg[0, yy], dqg[1, yy]], axis=1)
        for m in range(4):
            out = dot(ht[m * 256:m * 256 + 256, :], both).astype(BF16)
            for h in range(2):
                pw[2 * yy + h, m * 256:m * 256 + 256] = out[:, h * HEAD:(h + 1) * HEAD]
        for h in range(2):
            i = 2 * yy + h
            for other_core in range(2):
                mine = jnp.logical_and(8 * c + i == dp, other_core == 0)

                @pl.when(jnp.logical_not(mine))
                def _():
                    rs_send(i, other_core).start()

    weight_grad(0)
    weight_grad(3)
    weight_grad(1)
    for h in range(2):
        for slot in (2, 3):
            dq_recv(h, slot)
    weight_grad(2)

    @pl.when(own_block == 1)
    def _():
        own_rs().start()

    for yy in range(4):
        for h in range(2):
            dqc[:, (2 * yy + h) * HEAD:(2 * yy + h + 1) * HEAD] = dqg[h, yy, span256(y)]

    @pl.loop(0, 16)
    def _(d):
        theirs = dot(dqc[pl.ds(pl.multiple_of((1 - c) * 128, 128), 128), :], wb[d], ((1,), (1,)))
        dhs[:, span256(d)] = theirs
        ours = dot(dqc[pl.ds(pl.multiple_of(c * 128, 128), 128), :], wb[d], ((1,), (1,)))
        dho[:, span256(d)] = ours

    dh_copy = remote(dhs, dhr, S_DH, (dp, sibling))
    dh_copy.start()
    sent.append(dh_copy)
    dh_copy.wait_recv()
    dh_out[...] = (dho[...] + dhr[...]).astype(BF16)

    @pl.when(own_block == 1)
    def _():
        own_rs().wait()

    @pl.loop(0, 16)
    def _(k):
        @pl.when(jnp.logical_or(k != dp, own_block == 0))
        def _():
            pltpu.make_async_remote_copy(
                src_ref=rsb.at[k], dst_ref=rsb.at[k], send_sem=ssem.at[S_RS], recv_sem=rsem.at[S_RS + k],
                device_id=(dp, sibling), device_id_type=MESH,
            ).wait_recv()

    total = rsb[0].astype(F32)
    for k in range(1, 16):
        total += rsb[k].astype(F32)
    dwq_out[...] = total

    for h in range(2):
        for j in range(7):
            att_copy(h, j).wait_recv()
        local(atth.at[h, own_tokens], att_out.at[:, pl.ds(cols(seq, h), HEAD)], 12 + h).wait()
        for i, (src, dst) in enumerate(((dks, dk_out), (dvs, dv_out))):
            local(src.at[h, rows4], dst.at[:, :, pl.ds(cols(seq, h), HEAD)], 8 + 2 * h + i).wait()

            @pl.loop(1, 8)
            def _(j):
                frm = peer(4 - j // 2, 2 - j % 2)
                ref = dst.at[:, :, pl.ds(cols(frm, h), HEAD)]
                remote(src.at[h, pl.ds(frm * 4, 4)], ref, S_DKV + (h * 2 + i) * 8 + j, (dp, frm)).wait_recv()
                dkv_copy(h, i, j).wait_send()

    @pl.loop(0, 8)
    def _(i):
        for other_core in range(2):
            mine = jnp.logical_and(8 * c + i == dp, other_core == 0)

            @pl.when(jnp.logical_not(mine))
            def _():
                rs_send(i, other_core).wait_send()

    for copy in sent:
        copy.wait_send()


def on_device(hidden, w_query, nbr_keys, nbr_values, nbr_ids, d_attended):
    ids = jnp.pad(nbr_ids.reshape(1, 4), ((0, 7), (0, 124)))
    vmem = pltpu.VMEM
    anywhere = pl.BlockSpec(memory_space=pl.ANY)
    in_vmem = pl.BlockSpec(memory_space=pltpu.VMEM)
    attended, d_hidden, d_wq, d_keys, d_values = pl.pallas_call(
        kernel,
        out_shape=(
            jax.ShapeDtypeStruct((128, 2048), BF16),
            jax.ShapeDtypeStruct((128, 4096), BF16),
            jax.ShapeDtypeStruct((512, 128), F32),
            jax.ShapeDtypeStruct((4, 128, 2048), BF16),
            jax.ShapeDtypeStruct((4, 128, 2048), BF16),
        ),
        in_specs=[anywhere, anywhere, anywhere, anywhere, in_vmem, anywhere],
        out_specs=(anywhere, in_vmem, in_vmem, anywhere, anywhere),
        scratch_shapes=[
            vmem((256, 4096), BF16),
            vmem((16, 256, 1024), BF16),
            *[vmem((32, 128, 128), BF16)] * 4,
            vmem((1024, 256), BF16),
            vmem((1024, 256), BF16),
            vmem((256, 1024), F32),
            vmem((256, 1024), BF16),
            vmem((1024, 1024), BF16),
            vmem((1024, 1024), BF16),
            vmem((33, 128, 128), BF16),
            vmem((33, 128, 128), BF16),
            vmem((2, 32, 128, 128), BF16),
            vmem((2, 32, 128, 128), BF16),
            vmem((2, 1024, 128), BF16),
            vmem((2, 4, 1024, 128), BF16),
            vmem((256, 1024), BF16),
            vmem((8, 1024, 128), BF16),
            vmem((16, 512, 128), BF16),
            vmem((128, 4096), F32),
            vmem((128, 4096), F32),
            vmem((128, 4096), F32),
            vmem((8, 8, 128), jnp.int32),
            pltpu.SMEM((8, 8, 128), jnp.int32),
            pltpu.SemaphoreType.DMA((N_SEMS,)),
            pltpu.SemaphoreType.DMA((N_SEMS,)),
        ],
        compiler_params=pltpu.CompilerParams(
            collective_id=0, has_side_effects=True, vmem_limit_bytes=60 * 2**20
        ),
        name="group_attention",
    )(hidden, w_query, nbr_keys, nbr_values, ids, d_attended)
    return attended, d_hidden, d_wq, d_keys.astype(F32), d_values.astype(F32)


def solution(mesh):
    placed = (
        P(("dp", "seq"), None),
        P("dp", None),
        P(("dp", "seq"), None, None),
        P(("dp", "seq"), None, None),
        P(("dp", "seq"), None),
        P(("dp", "seq"), None),
    )
    return jax.shard_map(
        on_device,
        mesh=mesh,
        in_specs=placed,
        out_specs=(
            P(("dp", "seq"), None),
            P(("dp", "seq"), None),
            P("seq", "dp"),
            P(("dp", "seq"), None, None),
            P(("dp", "seq"), None, None),
        ),
        check_vma=False,
    )
```

```python
import functools

import jax
import jax.numpy as jnp
from jax import lax
from jax.experimental import pallas as pl
from jax.experimental.pallas import tpu as pltpu
from jax.sharding import PartitionSpec as P

BF16 = jnp.bfloat16
F32 = jnp.float32
MESH = pl.DeviceIdType.MESH
HEAD = 128
SCALE = HEAD ** (-0.5)
BLOCK = 64
NLEN = 128


class Pool:
    def __init__(self):
        self.used = 0

    def take(self, count):
        first = self.used
        self.used += count
        return first


POOL = Pool()
S_W = POOL.take(40)
S_KV = POOL.take(32)
S_DO = POOL.take(8)
S_ID = POOL.take(8)
S_HID = POOL.take(1)
S_Q = POOL.take(4)
S_HS = POOL.take(4)
S_HF = POOL.take(4)
S_ATT = POOL.take(16)
S_DQ = POOL.take(8)
S_DKV = POOL.take(32)
S_DH = POOL.take(1)
S_R1 = POOL.take(8)
S_R2 = POOL.take(4)
S_LOCAL = POOL.take(16)
N_SEMS = POOL.used


def dot(a, b, dims=((1,), (0,))):
    return lax.dot_general(a, b, (dims, ((), ())), preferred_element_type=F32)


def kernel(
    hidden, weight, keys, values, ids, grads,
    att_out, dh_out, dwq_out, dk_out, dv_out,
    hid, wb, kh0, kh1, vh0, vh1, doh, qh, qacc, qs, hs, ht, ck, cv, dks, dvs, atth, dqg, dqc, pw, r1, r1s, r2,
    dhs, dhr, dho, idg, ids_s, ssem, rsem,
):
    dp = lax.axis_index("dp")
    seq = lax.axis_index("seq")
    x, z = dp // 4, dp % 4
    y, c = seq // 2, seq % 2
    half = c * 1024
    kh, vh = (kh0, kh1), (vh0, vh1)

    def remote(src, dst, sem, to):
        return pltpu.make_async_remote_copy(
            src_ref=src, dst_ref=dst, send_sem=ssem.at[sem], recv_sem=rsem.at[sem],
            device_id=to, device_id_type=MESH,
        )

    def local(src, dst, sem):
        return pltpu.make_async_copy(src, dst, ssem.at[S_LOCAL + sem])

    def peer(dy, dc):
        return ((y + dy + 4) % 4) * 2 + (c + dc) % 2

    def cols(seq_of, h):
        return pl.multiple_of(((seq_of % 2) * 8 + (seq_of // 2) * 2 + h) * HEAD, HEAD)

    sibling = peer(0, 1)
    others = [(dy, dc) for dy in (1, 3, 2, 0) for dc in (0, 1) if (dy, dc) != (0, 0)]

    own_w = local(weight.at[:, pl.ds(pl.multiple_of(half, 1024), 1024)], wb.at[dp], 0)
    own_hid = local(hidden, hid.at[pl.ds(pl.multiple_of(c * 128, 128), 128)], 1)
    own_w.start()
    own_hid.start()
    rows4 = pl.ds(seq * 4, 4)
    own_kv = []
    for h in range(2):
        for i, (src, dst) in enumerate(((keys, kh), (values, vh))):
            own_kv.append(local(src.at[:, :, pl.ds(cols(seq, h), HEAD)], dst[h].at[rows4], 2 + 2 * h + i))
            own_kv[-1].start()
    own_tokens = pl.ds(pl.multiple_of(seq * 128, 128), 128)
    own_do = local(grads.at[:, pl.ds(cols(seq, 0), 2 * HEAD)], doh.at[own_tokens], 6)
    own_do.start()

    barrier = pltpu.get_barrier_semaphore()

    def greet(to):
        pl.semaphore_signal(barrier, inc=1, device_id=to, device_id_type=MESH)

    for dy, dc in others:
        greet((dp, peer(dy, dc)))
    for step in (1, 2, 3):
        for core in (0, 1):
            greet((((x + step) % 4) * 4 + z, y * 2 + core))
            greet((x * 4 + (z + step) % 4, y * 2 + core))
    pl.semaphore_wait(barrier, 7 + 12)

    def moved(axis, step):
        if axis == 0:
            return (((x + step + 4) % 4) * 4 + z, seq)
        return (x * 4 + (z + step + 4) % 4, seq)

    def source(t, r1, r2):
        rx, rz = (r1, r2) if t == 0 else (r2, r1)
        return ((x + rx + 4) % 4) * 4 + (z + rz + 4) % 4

    LINE = (0, -1, 1, 2)

    def piece(t, r1, r2, part):
        lo, n = {"all": (0, 128), "lo": (0, 64), "hi": (64, 64)}[part]
        return wb.at[source(t, r1, r2), pl.ds(t * 128 + lo, n)]

    def w_copy(t, phase, q, slot):
        axis = t if phase == 1 else 1 - t
        sem = S_W + 20 * t + (slot if phase == 1 else 4 + 4 * q + slot)
        step = 1 if slot % 2 == 0 else -1
        near = 0 if slot < 2 else -step
        part = "all" if slot < 2 else ("lo" if slot == 2 else "hi")
        src = piece(t, near, 0, part) if phase == 1 else piece(t, LINE[q], near, part)
        return remote(src, src, sem, moved(axis, step))

    def w_recv(t, phase, q, slot):
        axis = t if phase == 1 else 1 - t
        sem = S_W + 20 * t + (slot if phase == 1 else 4 + 4 * q + slot)
        step = 1 if slot % 2 == 0 else -1
        far = -step if slot < 2 else -2 * step
        part = "all" if slot < 2 else ("lo" if slot == 2 else "hi")
        if far == -2:
            far = 2
        dst = piece(t, far, 0, part) if phase == 1 else piece(t, LINE[q], far, part)
        remote(dst, dst, sem, moved(axis, step)).wait_recv()

    sent = []

    def go(copy):
        copy.start()
        sent.append(copy)

    own_w.wait()
    for t in (0, 1):
        for slot in (0, 1):
            go(w_copy(t, 1, 0, slot))
    for t in (0, 1):
        for slot in (0, 1):
            go(w_copy(t, 2, 0, slot))

    for j, (dy, dc) in enumerate(others):
        go(remote(ids, idg.at[seq], S_ID + j, (dp, peer(dy, dc))))
    own_hid.wait()
    own_hid_rows = hid.at[pl.ds(pl.multiple_of(c * 128, 128), 128)]
    hid_copy = remote(own_hid_rows, own_hid_rows, S_HID, (dp, sibling))
    go(hid_copy)

    def kv_sem(h, i, j):
        return S_KV + (h * 2 + i) * 8 + j

    def send_kv(h, i):
        src, dst = ((keys, kh), (values, vh))[i]
        for j, (dy, dc) in enumerate(others):
            to = peer(dy, dc)
            go(remote(src.at[:, :, pl.ds(cols(to, h), HEAD)], dst[h].at[rows4], kv_sem(h, i, j), (dp, to)))

    send_kv(0, 0)

    for t in (0, 1):
        for slot, q in ((0, 1), (1, 2)):
            w_recv(t, 1, 0, slot)
            go(w_copy(t, 1, 0, slot + 2))
            for s in (0, 1):
                go(w_copy(t, 2, q, s))
    send_kv(0, 1)
    for t in (0, 1):
        for slot in (0, 1):
            w_recv(t, 2, 0, slot)
            go(w_copy(t, 2, 0, slot + 2))
    for j, (dy, dc) in enumerate(others):
        to = peer(dy, dc)
        go(remote(grads.at[:, pl.ds(cols(to, 0), 2 * HEAD)], doh.at[own_tokens], S_DO + j, (dp, to)))
    other_rows = hid.at[pl.ds(pl.multiple_of((1 - c) * 128, 128), 128)]
    remote(other_rows, other_rows, S_HID, (dp, sibling)).wait_recv()
    for t in (0, 1):
        for slot in (2, 3):
            w_recv(t, 1, 0, slot)
        for s in (0, 1):
            go(w_copy(t, 2, 3, s))
    send_kv(1, 0)
    for q in (1, 2):
        for t in (0, 1):
            for slot in (0, 1):
                w_recv(t, 2, q, slot)
                go(w_copy(t, 2, q, slot + 2))

    def project(rx, first):
        @pl.loop(0, 4)
        def _(i):
            d = ((x + rx + 4) % 4) * 4 + i
            rows = hid[:, pl.ds(pl.multiple_of(d * 256, 256), 256)]
            for n in range(4):
                span = slice(n * 256, n * 256 + 256)
                part = dot(rows, wb[d, :, span])
                if first:
                    qacc[:, span] = jnp.where(i == 0, part, qacc[:, span] + part)
                else:
                    qacc[:, span] += part

    qacc[...] = jnp.zeros_like(qacc)
    for t in (0, 1):
        for slot in (0, 1):
            w_recv(t, 2, 3, slot)
            go(w_copy(t, 2, 3, slot + 2))
    send_kv(1, 1)
    for slot in (2, 3):
        w_recv(0, 2, 0, slot)
    project(0, False)
    for slot in (2, 3):
        w_recv(0, 2, 1, slot)
    project(-1, False)
    for slot in (2, 3):
        w_recv(0, 2, 2, slot)
    project(1, False)
    for slot in (2, 3):
        w_recv(0, 2, 3, slot)
        for q in range(4):
            w_recv(1, 2, q, slot)
    project(2, False)
    qs[...] = qacc[...].astype(BF16)

    def span256(k):
        return pl.ds(pl.multiple_of(k * 256, 256), 256)

    for dy in (1, 3, 2):
        to = peer(dy, 0)
        go(remote(qs.at[:, span256(to // 2)], qh.at[span256(y)], S_Q + dy, (dp, to)))
    qh[span256(y), :] = qs[:, span256(y)]

    def feats(k):
        return pl.ds(pl.multiple_of(k * 1024, 1024), 1024)

    def tokens(s):
        return pl.ds(pl.multiple_of(s * 128, 128), 128)

    for dy in (1, 3, 2):
        to = peer(dy, 0)
        go(remote(own_hid_rows.at[:, feats(to // 2)], hs.at[own_tokens], S_HS + dy, (dp, to)))
    hs[span256(y), :] = hid[:, feats(y)]

    for j, (dy, dc) in enumerate(others):
        frm = peer(-dy, -dc + 2)
        remote(ids, idg.at[frm], S_ID + j, (dp, frm)).wait_recv()
    idg[seq] = ids[...]
    to_smem = local(idg, ids_s, 7)
    to_smem.start()
    to_smem.wait()
    for j, (dy, dc) in enumerate(others):
        frm = peer(-dy, -dc + 2)
        dst = doh.at[tokens(frm)]
        remote(dst, dst, S_DO + j, (dp, frm)).wait_recv()
    own_do.wait()
    for cp in own_kv:
        cp.wait()

    def wait_kv(h):
        for i, dst in enumerate((kh, vh)):
            for j, (dy, dc) in enumerate(others):
                frm = peer(-dy, -dc + 2)
                ref = dst[h].at[pl.ds(frm * 4, 4)]
                remote(ref, ref, kv_sem(h, i, j), (dp, frm)).wait_recv()

    wait_kv(0)
    for dy in (1, 3, 2):
        frm = peer(-dy, 0)
        ref = qh.at[span256(frm // 2)]
        remote(ref, ref, S_Q + dy, (dp, frm)).wait_recv()

    ck[32] = jnp.zeros((NLEN, HEAD), BF16)
    cv[32] = jnp.zeros((NLEN, HEAD), BF16)

    def attend(h):
        lanes = slice(h * HEAD, h * HEAD + HEAD)

        @pl.loop(0, 8)
        def _(s):
            for u in range(2):
                rows = pl.ds(pl.multiple_of(s * 128 + u * BLOCK, BLOCK), BLOCK)
                first, second = ids_s[s, 0, 2 * u], ids_s[s, 0, 2 * u + 1]
                k = jnp.concatenate([kh[h][first], kh[h][second]], axis=0)
                v = jnp.concatenate([vh[h][first], vh[h][second]], axis=0)
                q = qh[rows, lanes]
                g = doh[rows, lanes]
                scores = dot(q, k, ((1,), (1,))) * SCALE
                peak = jnp.max(scores, axis=-1, keepdims=True)
                expo = jnp.exp(scores - peak)
                probs = expo / jnp.sum(expo, axis=-1, keepdims=True)
                low = probs.astype(BF16)
                atth[h, rows] = dot(low, v).astype(BF16)
                d_probs = dot(g, v, ((1,), (1,)))
                delta = jnp.sum(probs * d_probs, axis=-1, keepdims=True)
                d_scores = (probs * (d_probs - delta) * SCALE).astype(BF16)
                dqg[h, y, rows] = dot(d_scores, k).astype(BF16)
                dk = dot(d_scores, q, ((0,), (0,))).astype(BF16)
                dv = dot(low, g, ((0,), (0,))).astype(BF16)
                for i in range(2):
                    ck[s * 4 + 2 * u + i] = dk[i * NLEN:(i + 1) * NLEN]
                    cv[s * 4 + 2 * u + i] = dv[i * NLEN:(i + 1) * NLEN]

    def dq_copy(h, slot):
        step = 1 if slot % 2 == 0 else -1
        near = y if slot < 2 else (y - step + 4) % 4
        rows = {0: pl.ds(0, 1024), 1: pl.ds(0, 1024), 2: pl.ds(0, 512), 3: pl.ds(512, 512)}[slot]
        ref = dqg.at[h, near, rows]
        return remote(ref, ref, S_DQ + 4 * h + slot, (dp, peer(step, 0)))

    def dq_recv(h, slot):
        step = 1 if slot % 2 == 0 else -1
        far = (y - step + 4) % 4 if slot < 2 else (y + 2) % 4
        rows = {0: pl.ds(0, 1024), 1: pl.ds(0, 1024), 2: pl.ds(0, 512), 3: pl.ds(512, 512)}[slot]
        ref = dqg.at[h, far, rows]
        remote(ref, ref, S_DQ + 4 * h + slot, (dp, peer(step, 0))).wait_recv()

    def dkv_copy(h, i, j):
        dy, dc = j // 2, j % 2
        to = peer(dy, dc)
        src, dst = ((dks, dk_out), (dvs, dv_out))[i]
        return remote(
            src.at[h, pl.ds(to * 4, 4)], dst.at[:, :, pl.ds(cols(seq, h), HEAD)],
            S_DKV + (h * 2 + i) * 8 + j, (dp, to),
        )

    def sum_kv(h):
        def accumulate(to):
            @pl.loop(0, 4)
            def _(r):
                row = to * 4 + r
                total_k = jnp.zeros((NLEN, HEAD), F32)
                total_v = jnp.zeros((NLEN, HEAD), F32)
                for s in range(8):
                    at = jnp.int32(32)
                    for j in range(4):
                        at = jnp.where(ids_s[s, 0, j] == row, 4 * s + j, at)
                    total_k += ck[at].astype(F32)
                    total_v += cv[at].astype(F32)
                dks[h, row] = total_k.astype(BF16)
                dvs[h, row] = total_v.astype(BF16)

        @pl.loop(0, 8)
        def _(to):
            accumulate(to)

    def send_dkv(h, i):
        @pl.loop(1, 8)
        def _(j):
            dkv_copy(h, i, j).start()

        src, dst = ((dks, dk_out), (dvs, dv_out))[i]
        local(src.at[h, rows4], dst.at[:, :, pl.ds(cols(seq, h), HEAD)], 8 + 2 * h + i).start()

    def att_copy(h, j):
        dy, dc = others[j]
        to = peer(dy, dc)
        return remote(
            atth.at[h, tokens(to)], att_out.at[:, pl.ds(cols(seq, h), HEAD)],
            S_ATT + 8 * h + j, (dp, to),
        )

    def forward_hidden():
        for dy in (1, 3, 2):
            frm = peer(-dy, 0)
            ref = hs.at[tokens(frm)]
            remote(ref, ref, S_HS + dy, (dp, frm)).wait_recv()
            go(remote(ref, ref, S_HF + dy, (dp, sibling)))

    attend(0)
    for slot in (0, 1):
        go(dq_copy(0, slot))
    sum_kv(0)
    send_dkv(0, 0)
    forward_hidden()
    wait_kv(1)
    attend(1)
    for slot in (0, 1):
        go(dq_copy(1, slot))
    for slot in (0, 1):
        dq_recv(0, slot)
        go(dq_copy(0, slot + 2))
    send_dkv(0, 1)
    sum_kv(1)
    for slot in (0, 1):
        dq_recv(1, slot)
        go(dq_copy(1, slot + 2))
    send_dkv(1, 0)

    for dy in (1, 3, 2):
        frm = peer(-dy, 1)
        ref = hs.at[tokens(frm)]
        remote(ref, ref, S_HF + dy, (dp, sibling)).wait_recv()

    @pl.loop(0, 4)
    def _(m):
        ht[span256(m), :] = jnp.transpose(hs[:, span256(m)])

    def wq_grad(k):
        both = jnp.concatenate([dqg[0, k], dqg[1, k]], axis=1)
        for m in range(4):
            out = dot(ht[m * 256:m * 256 + 256, :], both).astype(BF16)
            for h in range(2):
                pw[k // 2, 2 * (k % 2) + h, m * 256:m * 256 + 256] = out[:, h * HEAD:(h + 1) * HEAD]

    def r1_copy(core, to, part):
        if core == 0:
            src, slot, dest = pw.at[to, pl.ds(2 * part, 2), pl.ds(0, 512)], x, (2 * c + to) * 4 + z
        else:
            src, slot, dest = pw.at[:, to, pl.ds(512, 512)], z, x * 4 + to
            part = c
        dst = r1.at[slot, pl.ds(2 * part, 2)]
        sem = ssem.at[S_R1 + (2 * to + part if core == 0 else 4 + to)]
        own = jnp.logical_and(dest == dp, c == core)
        return src, dst, sem, rsem.at[S_R1 + slot * 2 + part], (dest, y * 2 + core), own

    def r1_start(core, to, part):
        src, dst, s_sem, r_sem, dest, own = r1_copy(core, to, part)

        @pl.when(own)
        def _():
            pltpu.make_async_copy(src, dst, s_sem).start()

        @pl.when(jnp.logical_not(own))
        def _():
            pltpu.make_async_remote_copy(
                src_ref=src, dst_ref=dst, send_sem=s_sem, recv_sem=r_sem, device_id=dest, device_id_type=MESH
            ).start()

    def r1_wait(core, to, part):
        src, dst, s_sem, r_sem, dest, own = r1_copy(core, to, part)

        @pl.when(own)
        def _():
            pltpu.make_async_copy(src, dst, s_sem).wait()

        @pl.when(jnp.logical_not(own))
        def _():
            pltpu.make_async_remote_copy(
                src_ref=src, dst_ref=dst, send_sem=s_sem, recv_sem=r_sem, device_id=dest, device_id_type=MESH
            ).wait_send()

    R1_ALL = [(0, to, part) for to in range(2) for part in range(2)] + [(1, to, 0) for to in range(4)]

    for h in range(2):
        for slot in (2, 3):
            dq_recv(h, slot)
    for k in range(4):
        wq_grad(k)
        r1_start(0, k // 2, k % 2)
        if k >= 2:
            r1_start(1, 2 * (k - 2), 0)
            r1_start(1, 2 * (k - 2) + 1, 0)
    send_dkv(1, 1)
    for h in range(2):
        for j in range(7):
            go(att_copy(h, j))
        local(atth.at[h, own_tokens], att_out.at[:, pl.ds(cols(seq, h), HEAD)], 12 + h).start()

    for yy in range(4):
        for h in range(2):
            dqc[:, (2 * yy + h) * HEAD:(2 * yy + h + 1) * HEAD] = dqg[h, yy, span256(y)]

    @pl.loop(0, 16)
    def _(d):
        theirs = dot(dqc[pl.ds(pl.multiple_of((1 - c) * 128, 128), 128), :], wb[d], ((1,), (1,)))
        dhs[:, span256(d)] = theirs
        ours = dot(dqc[pl.ds(pl.multiple_of(c * 128, 128), 128), :], wb[d], ((1,), (1,)))
        dho[:, span256(d)] = ours

    dh_copy = remote(dhs, dhr, S_DH, (dp, sibling))
    dh_copy.start()
    sent.append(dh_copy)
    for core, to, part in R1_ALL:
        r1_wait(core, to, part)
    line1, line2 = jnp.where(c == 0, x, z), jnp.where(c == 0, z, x)

    @pl.loop(0, 8)
    def _(k):
        from_core = jnp.where(c == 0, x // 2, k % 2)

        @pl.when(jnp.logical_not(jnp.logical_and(k // 2 == line1, from_core == c)))
        def _():
            ref = r1.at[k // 2, pl.ds(2 * (k % 2), 2)]
            pltpu.make_async_remote_copy(
                src_ref=ref, dst_ref=ref, send_sem=ssem.at[S_R1], recv_sem=rsem.at[S_R1 + k],
                device_id=(dp, sibling), device_id_type=MESH,
            ).wait_recv()

    def r2_copy(step):
        to = (line2 + step) % 4
        dest = jnp.where(c == 0, line1 * 4 + to, to * 4 + line1)
        return remote(r1s.at[to], r2.at[step], S_R2 + step, (dest, seq))

    for step in (1, 3, 2, 0):
        to = (line2 + step) % 4
        total = r1[0, to].astype(F32)
        for k in range(1, 4):
            total += r1[k, to].astype(F32)
        if step:
            r1s[to] = total.astype(BF16)
            go(r2_copy(step))
        else:
            dwq_out[...] = total
    dh_copy.wait_recv()
    dh_out[...] = (dho[...] + dhr[...]).astype(BF16)
    for step in (1, 3, 2):
        r2_copy(step).wait_recv()
        dwq_out[...] += r2[step].astype(F32)

    for h in range(2):
        for j in range(7):
            att_copy(h, j).wait_recv()
        local(atth.at[h, own_tokens], att_out.at[:, pl.ds(cols(seq, h), HEAD)], 12 + h).wait()
        for i, (src, dst) in enumerate(((dks, dk_out), (dvs, dv_out))):
            local(src.at[h, rows4], dst.at[:, :, pl.ds(cols(seq, h), HEAD)], 8 + 2 * h + i).wait()

            @pl.loop(1, 8)
            def _(j):
                frm = peer(4 - j // 2, 2 - j % 2)
                ref = dst.at[:, :, pl.ds(cols(frm, h), HEAD)]
                remote(src.at[h, pl.ds(frm * 4, 4)], ref, S_DKV + (h * 2 + i) * 8 + j, (dp, frm)).wait_recv()
                dkv_copy(h, i, j).wait_send()

    for copy in sent:
        copy.wait_send()


def finish(att_in, dh_in, dwq_in, dk_in, dv_in, att_out, dh_out, dwq_out, dk_out, dv_out):
    att_out[...] = att_in[...]
    dh_out[...] = dh_in[...]
    dwq_out[...] = dwq_in[...]
    dk_out[...] = dk_in[...].astype(F32)
    dv_out[...] = dv_in[...].astype(F32)


def on_device(hidden, w_query, nbr_keys, nbr_values, nbr_ids, d_attended):
    ids = jnp.pad(nbr_ids.reshape(1, 4), ((0, 7), (0, 124)))
    vmem = pltpu.VMEM
    anywhere = pl.BlockSpec(memory_space=pl.ANY)
    in_vmem = pl.BlockSpec(memory_space=pltpu.VMEM)
    attended, d_hidden, d_wq, d_keys, d_values = pl.pallas_call(
        kernel,
        out_shape=(
            jax.ShapeDtypeStruct((128, 2048), BF16),
            jax.ShapeDtypeStruct((128, 4096), BF16),
            jax.ShapeDtypeStruct((512, 128), F32),
            jax.ShapeDtypeStruct((4, 128, 2048), BF16),
            jax.ShapeDtypeStruct((4, 128, 2048), BF16),
        ),
        in_specs=[anywhere, anywhere, anywhere, anywhere, in_vmem, anywhere],
        out_specs=(anywhere, in_vmem, in_vmem, anywhere, anywhere),
        scratch_shapes=[
            vmem((256, 4096), BF16),
            vmem((16, 256, 1024), BF16),
            *[vmem((32, 128, 128), BF16)] * 4,
            vmem((1024, 256), BF16),
            vmem((1024, 256), BF16),
            vmem((256, 1024), F32),
            vmem((256, 1024), BF16),
            vmem((1024, 1024), BF16),
            vmem((1024, 1024), BF16),
            vmem((33, 128, 128), BF16),
            vmem((33, 128, 128), BF16),
            vmem((2, 32, 128, 128), BF16),
            vmem((2, 32, 128, 128), BF16),
            vmem((2, 1024, 128), BF16),
            vmem((2, 4, 1024, 128), BF16),
            vmem((256, 1024), BF16),
            vmem((2, 4, 1024, 128), BF16),
            vmem((4, 4, 512, 128), BF16),
            vmem((4, 512, 128), BF16),
            vmem((4, 512, 128), BF16),
            vmem((128, 4096), F32),
            vmem((128, 4096), F32),
            vmem((128, 4096), F32),
            vmem((8, 8, 128), jnp.int32),
            pltpu.SMEM((8, 8, 128), jnp.int32),
            pltpu.SemaphoreType.DMA((N_SEMS,)),
            pltpu.SemaphoreType.DMA((N_SEMS,)),
        ],
        compiler_params=pltpu.CompilerParams(
            collective_id=0, has_side_effects=True, vmem_limit_bytes=60 * 2**20
        ),
        name="group_attention",
    )(hidden, w_query, nbr_keys, nbr_values, ids, d_attended)
    parts = (attended, d_hidden, d_wq, d_keys.reshape(512, 2048), d_values.reshape(512, 2048))
    steps = 8
    specs = [pl.BlockSpec((p.shape[0] // steps, p.shape[1]), lambda i: (i, 0)) for p in parts]
    kinds = (BF16, BF16, F32, F32, F32)
    attended, d_hidden, d_wq, d_keys, d_values = pl.pallas_call(
        finish,
        grid=(steps,),
        out_shape=[jax.ShapeDtypeStruct(p.shape, kind) for p, kind in zip(parts, kinds)],
        in_specs=specs,
        out_specs=specs,
        compiler_params=pltpu.CompilerParams(vmem_limit_bytes=60 * 2**20),
        name="finish",
    )(*parts)
    return attended, d_hidden, d_wq, d_keys.reshape(4, 128, 2048), d_values.reshape(4, 128, 2048)


def solution(mesh):
    placed = (
        P(("dp", "seq"), None),
        P("dp", None),
        P(("dp", "seq"), None, None),
        P(("dp", "seq"), None, None),
        P(("dp", "seq"), None),
        P(("dp", "seq"), None),
    )
    return jax.shard_map(
        on_device,
        mesh=mesh,
        in_specs=placed,
        out_specs=(
            P(("dp", "seq"), None),
            P(("dp", "seq"), None),
            P("seq", "dp"),
            P(("dp", "seq"), None, None),
            P(("dp", "seq"), None, None),
        ),
        check_vma=False,
    )
```

```python
import functools

import jax
import jax.numpy as jnp
from jax import lax
from jax.experimental import pallas as pl
from jax.experimental.pallas import tpu as pltpu
from jax.sharding import PartitionSpec as P

BF16 = jnp.bfloat16
F32 = jnp.float32
MESH = pl.DeviceIdType.MESH
HEAD = 128
SCALE = HEAD ** (-0.5)
BLOCK = 64
NLEN = 128


class Pool:
    def __init__(self):
        self.used = 0

    def take(self, count):
        first = self.used
        self.used += count
        return first


POOL = Pool()
S_W = POOL.take(40)
S_KV = POOL.take(32)
S_DO = POOL.take(8)
S_ID = POOL.take(8)
S_HID = POOL.take(1)
S_Q = POOL.take(4)
S_HS = POOL.take(4)
S_HF = POOL.take(4)
S_ATT = POOL.take(16)
S_DQ = POOL.take(8)
S_DKV = POOL.take(32)
S_DH = POOL.take(1)
S_R1 = POOL.take(8)
S_R2 = POOL.take(4)
S_LOCAL = POOL.take(16)
N_SEMS = POOL.used


def dot(a, b, dims=((1,), (0,))):
    return lax.dot_general(a, b, (dims, ((), ())), preferred_element_type=F32)


def kernel(
    hidden, weight, keys, values, ids, grads,
    att_out, dh_out, dwq_out, dk_out, dv_out,
    hid, wb, kh0, kh1, vh0, vh1, doh, qh, qacc, qs, hs, ht, ck, cv, dks, dvs, atth, dqg, dqc, pw, r1, r1s, r2,
    dhs, dhr, dho, idv, idg, ids_s, ssem, rsem,
):
    dp = lax.axis_index("dp")
    seq = lax.axis_index("seq")
    x, z = dp // 4, dp % 4
    y, c = seq // 2, seq % 2
    half = c * 1024
    kh, vh = (kh0, kh1), (vh0, vh1)

    def remote(src, dst, sem, to):
        return pltpu.make_async_remote_copy(
            src_ref=src, dst_ref=dst, send_sem=ssem.at[sem], recv_sem=rsem.at[sem],
            device_id=to, device_id_type=MESH,
        )

    def local(src, dst, sem):
        return pltpu.make_async_copy(src, dst, ssem.at[S_LOCAL + sem])

    def peer(dy, dc):
        return ((y + dy + 4) % 4) * 2 + (c + dc) % 2

    def cols(seq_of, h):
        return pl.multiple_of(((seq_of % 2) * 8 + (seq_of // 2) * 2 + h) * HEAD, HEAD)

    sibling = peer(0, 1)
    others = [(dy, dc) for dy in (1, 3, 2, 0) for dc in (0, 1) if (dy, dc) != (0, 0)]

    idv[...] = jnp.zeros_like(idv)
    idv[0:2, 0:2] = ids[...]

    own_w = local(weight.at[:, pl.ds(pl.multiple_of(half, 1024), 1024)], wb.at[dp], 0)
    own_hid = local(hidden, hid.at[pl.ds(pl.multiple_of(c * 128, 128), 128)], 1)
    own_w.start()
    own_hid.start()
    rows4 = pl.ds(seq * 4, 4)
    own_kv = []
    for h in range(2):
        for i, (src, dst) in enumerate(((keys, kh), (values, vh))):
            own_kv.append(local(src.at[:, :, pl.ds(cols(seq, h), HEAD)], dst[h].at[rows4], 2 + 2 * h + i))
            own_kv[-1].start()
    own_tokens = pl.ds(pl.multiple_of(seq * 128, 128), 128)
    own_do = local(grads.at[:, pl.ds(cols(seq, 0), 2 * HEAD)], doh.at[own_tokens], 6)
    own_do.start()

    barrier = pltpu.get_barrier_semaphore()

    def greet(to):
        pl.semaphore_signal(barrier, inc=1, device_id=to, device_id_type=MESH)

    for dy, dc in others:
        greet((dp, peer(dy, dc)))
    for step in (1, 2, 3):
        for core in (0, 1):
            greet((((x + step) % 4) * 4 + z, y * 2 + core))
            greet((x * 4 + (z + step) % 4, y * 2 + core))
    pl.semaphore_wait(barrier, 7 + 12)

    def moved(axis, step):
        if axis == 0:
            return (((x + step + 4) % 4) * 4 + z, seq)
        return (x * 4 + (z + step + 4) % 4, seq)

    def source(t, r1, r2):
        rx, rz = (r1, r2) if t == 0 else (r2, r1)
        return ((x + rx + 4) % 4) * 4 + (z + rz + 4) % 4

    LINE = (0, -1, 1, 2)

    def piece(t, r1, r2, part):
        lo, n = {"all": (0, 128), "lo": (0, 64), "hi": (64, 64)}[part]
        return wb.at[source(t, r1, r2), pl.ds(t * 128 + lo, n)]

    def w_copy(t, phase, q, slot):
        axis = t if phase == 1 else 1 - t
        sem = S_W + 20 * t + (slot if phase == 1 else 4 + 4 * q + slot)
        step = 1 if slot % 2 == 0 else -1
        near = 0 if slot < 2 else -step
        part = "all" if slot < 2 else ("lo" if slot == 2 else "hi")
        src = piece(t, near, 0, part) if phase == 1 else piece(t, LINE[q], near, part)
        return remote(src, src, sem, moved(axis, step))

    def w_recv(t, phase, q, slot):
        axis = t if phase == 1 else 1 - t
        sem = S_W + 20 * t + (slot if phase == 1 else 4 + 4 * q + slot)
        step = 1 if slot % 2 == 0 else -1
        far = -step if slot < 2 else -2 * step
        part = "all" if slot < 2 else ("lo" if slot == 2 else "hi")
        if far == -2:
            far = 2
        dst = piece(t, far, 0, part) if phase == 1 else piece(t, LINE[q], far, part)
        remote(dst, dst, sem, moved(axis, step)).wait_recv()

    sent = []

    def go(copy):
        copy.start()
        sent.append(copy)

    own_w.wait()
    for t in (0, 1):
        for slot in (0, 1):
            go(w_copy(t, 1, 0, slot))
    for t in (0, 1):
        for slot in (0, 1):
            go(w_copy(t, 2, 0, slot))

    for j, (dy, dc) in enumerate(others):
        go(remote(idv, idg.at[seq], S_ID + j, (dp, peer(dy, dc))))
    own_hid.wait()
    own_hid_rows = hid.at[pl.ds(pl.multiple_of(c * 128, 128), 128)]
    hid_copy = remote(own_hid_rows, own_hid_rows, S_HID, (dp, sibling))
    go(hid_copy)

    def kv_sem(h, i, j):
        return S_KV + (h * 2 + i) * 8 + j

    def send_kv(h, i):
        src, dst = ((keys, kh), (values, vh))[i]
        for j, (dy, dc) in enumerate(others):
            to = peer(dy, dc)
            go(remote(src.at[:, :, pl.ds(cols(to, h), HEAD)], dst[h].at[rows4], kv_sem(h, i, j), (dp, to)))

    send_kv(0, 0)

    for t in (0, 1):
        for slot, q in ((0, 1), (1, 2)):
            w_recv(t, 1, 0, slot)
            go(w_copy(t, 1, 0, slot + 2))
            for s in (0, 1):
                go(w_copy(t, 2, q, s))
    send_kv(0, 1)
    for t in (0, 1):
        for slot in (0, 1):
            w_recv(t, 2, 0, slot)
            go(w_copy(t, 2, 0, slot + 2))
    for j, (dy, dc) in enumerate(others):
        to = peer(dy, dc)
        go(remote(grads.at[:, pl.ds(cols(to, 0), 2 * HEAD)], doh.at[own_tokens], S_DO + j, (dp, to)))
    other_rows = hid.at[pl.ds(pl.multiple_of((1 - c) * 128, 128), 128)]
    remote(other_rows, other_rows, S_HID, (dp, sibling)).wait_recv()
    for t in (0, 1):
        for slot in (2, 3):
            w_recv(t, 1, 0, slot)
        for s in (0, 1):
            go(w_copy(t, 2, 3, s))
    send_kv(1, 0)
    for q in (1, 2):
        for t in (0, 1):
            for slot in (0, 1):
                w_recv(t, 2, q, slot)
                go(w_copy(t, 2, q, slot + 2))

    def project(rx, first):
        @pl.loop(0, 4)
        def _(i):
            d = ((x + rx + 4) % 4) * 4 + i
            rows = hid[:, pl.ds(pl.multiple_of(d * 256, 256), 256)]
            for n in range(4):
                span = slice(n * 256, n * 256 + 256)
                part = dot(rows, wb[d, :, span])
                if first:
                    qacc[:, span] = jnp.where(i == 0, part, qacc[:, span] + part)
                else:
                    qacc[:, span] += part

    qacc[...] = jnp.zeros_like(qacc)
    for t in (0, 1):
        for slot in (0, 1):
            w_recv(t, 2, 3, slot)
            go(w_copy(t, 2, 3, slot + 2))
    send_kv(1, 1)
    for slot in (2, 3):
        w_recv(0, 2, 0, slot)
    project(0, False)
    for slot in (2, 3):
        w_recv(0, 2, 1, slot)
    project(-1, False)
    for slot in (2, 3):
        w_recv(0, 2, 2, slot)
    project(1, False)
    for slot in (2, 3):
        w_recv(0, 2, 3, slot)
        for q in range(4):
            w_recv(1, 2, q, slot)
    project(2, False)
    qs[...] = qacc[...].astype(BF16)

    def span256(k):
        return pl.ds(pl.multiple_of(k * 256, 256), 256)

    for dy in (1, 3, 2):
        to = peer(dy, 0)
        go(remote(qs.at[:, span256(to // 2)], qh.at[span256(y)], S_Q + dy, (dp, to)))
    qh[span256(y), :] = qs[:, span256(y)]

    def feats(k):
        return pl.ds(pl.multiple_of(k * 1024, 1024), 1024)

    def tokens(s):
        return pl.ds(pl.multiple_of(s * 128, 128), 128)

    for dy in (1, 3, 2):
        to = peer(dy, 0)
        go(remote(own_hid_rows.at[:, feats(to // 2)], hs.at[own_tokens], S_HS + dy, (dp, to)))
    hs[span256(y), :] = hid[:, feats(y)]

    for j, (dy, dc) in enumerate(others):
        frm = peer(-dy, -dc + 2)
        remote(idv, idg.at[frm], S_ID + j, (dp, frm)).wait_recv()
    idg[seq] = idv[...]
    to_smem = local(idg, ids_s, 7)
    to_smem.start()
    to_smem.wait()
    for j, (dy, dc) in enumerate(others):
        frm = peer(-dy, -dc + 2)
        dst = doh.at[tokens(frm)]
        remote(dst, dst, S_DO + j, (dp, frm)).wait_recv()
    own_do.wait()
    for cp in own_kv:
        cp.wait()

    def wait_kv(h):
        for i, dst in enumerate((kh, vh)):
            for j, (dy, dc) in enumerate(others):
                frm = peer(-dy, -dc + 2)
                ref = dst[h].at[pl.ds(frm * 4, 4)]
                remote(ref, ref, kv_sem(h, i, j), (dp, frm)).wait_recv()

    wait_kv(0)
    for dy in (1, 3, 2):
        frm = peer(-dy, 0)
        ref = qh.at[span256(frm // 2)]
        remote(ref, ref, S_Q + dy, (dp, frm)).wait_recv()

    ck[32] = jnp.zeros((NLEN, HEAD), BF16)
    cv[32] = jnp.zeros((NLEN, HEAD), BF16)

    def attend(h):
        lanes = slice(h * HEAD, h * HEAD + HEAD)

        @pl.loop(0, 8)
        def _(s):
            for u in range(2):
                rows = pl.ds(pl.multiple_of(s * 128 + u * BLOCK, BLOCK), BLOCK)
                first, second = ids_s[s, u, 0], ids_s[s, u, 1]
                k = jnp.concatenate([kh[h][first], kh[h][second]], axis=0)
                v = jnp.concatenate([vh[h][first], vh[h][second]], axis=0)
                q = qh[rows, lanes]
                g = doh[rows, lanes]
                scores = dot(q, k, ((1,), (1,))) * SCALE
                peak = jnp.max(scores, axis=-1, keepdims=True)
                expo = jnp.exp(scores - peak)
                probs = expo / jnp.sum(expo, axis=-1, keepdims=True)
                low = probs.astype(BF16)
                atth[h, rows] = dot(low, v).astype(BF16)
                d_probs = dot(g, v, ((1,), (1,)))
                delta = jnp.sum(probs * d_probs, axis=-1, keepdims=True)
                d_scores = (probs * (d_probs - delta) * SCALE).astype(BF16)
                dqg[h, y, rows] = dot(d_scores, k).astype(BF16)
                dk = dot(d_scores, q, ((0,), (0,))).astype(BF16)
                dv = dot(low, g, ((0,), (0,))).astype(BF16)
                for i in range(2):
                    ck[s * 4 + 2 * u + i] = dk[i * NLEN:(i + 1) * NLEN]
                    cv[s * 4 + 2 * u + i] = dv[i * NLEN:(i + 1) * NLEN]

    def dq_copy(h, slot):
        step = 1 if slot % 2 == 0 else -1
        near = y if slot < 2 else (y - step + 4) % 4
        rows = {0: pl.ds(0, 1024), 1: pl.ds(0, 1024), 2: pl.ds(0, 512), 3: pl.ds(512, 512)}[slot]
        ref = dqg.at[h, near, rows]
        return remote(ref, ref, S_DQ + 4 * h + slot, (dp, peer(step, 0)))

    def dq_recv(h, slot):
        step = 1 if slot % 2 == 0 else -1
        far = (y - step + 4) % 4 if slot < 2 else (y + 2) % 4
        rows = {0: pl.ds(0, 1024), 1: pl.ds(0, 1024), 2: pl.ds(0, 512), 3: pl.ds(512, 512)}[slot]
        ref = dqg.at[h, far, rows]
        remote(ref, ref, S_DQ + 4 * h + slot, (dp, peer(step, 0))).wait_recv()

    def dkv_copy(h, i, j):
        dy, dc = j // 2, j % 2
        to = peer(dy, dc)
        src, dst = ((dks, dk_out), (dvs, dv_out))[i]
        return remote(
            src.at[h, pl.ds(to * 4, 4)], dst.at[:, :, pl.ds(cols(seq, h), HEAD)],
            S_DKV + (h * 2 + i) * 8 + j, (dp, to),
        )

    def sum_kv(h):
        def accumulate(to):
            @pl.loop(0, 4)
            def _(r):
                row = to * 4 + r
                total_k = jnp.zeros((NLEN, HEAD), F32)
                total_v = jnp.zeros((NLEN, HEAD), F32)
                for s in range(8):
                    at = jnp.int32(32)
                    for j in range(4):
                        at = jnp.where(ids_s[s, j // 2, j % 2] == row, 4 * s + j, at)
                    total_k += ck[at].astype(F32)
                    total_v += cv[at].astype(F32)
                dks[h, row] = total_k.astype(BF16)
                dvs[h, row] = total_v.astype(BF16)

        @pl.loop(0, 8)
        def _(to):
            accumulate(to)

    def send_dkv(h, i):
        @pl.loop(1, 8)
        def _(j):
            dkv_copy(h, i, j).start()

        src, dst = ((dks, dk_out), (dvs, dv_out))[i]
        local(src.at[h, rows4], dst.at[:, :, pl.ds(cols(seq, h), HEAD)], 8 + 2 * h + i).start()

    def att_copy(h, j):
        dy, dc = others[j]
        to = peer(dy, dc)
        return remote(
            atth.at[h, tokens(to)], att_out.at[:, pl.ds(cols(seq, h), HEAD)],
            S_ATT + 8 * h + j, (dp, to),
        )

    def forward_hidden():
        for dy in (1, 3, 2):
            frm = peer(-dy, 0)
            ref = hs.at[tokens(frm)]
            remote(ref, ref, S_HS + dy, (dp, frm)).wait_recv()
            go(remote(ref, ref, S_HF + dy, (dp, sibling)))

    attend(0)
    for slot in (0, 1):
        go(dq_copy(0, slot))
    sum_kv(0)
    send_dkv(0, 0)
    forward_hidden()
    wait_kv(1)
    attend(1)
    for slot in (0, 1):
        go(dq_copy(1, slot))
    for slot in (0, 1):
        dq_recv(0, slot)
        go(dq_copy(0, slot + 2))
    send_dkv(0, 1)
    sum_kv(1)
    for slot in (0, 1):
        dq_recv(1, slot)
        go(dq_copy(1, slot + 2))
    send_dkv(1, 0)

    for dy in (1, 3, 2):
        frm = peer(-dy, 1)
        ref = hs.at[tokens(frm)]
        remote(ref, ref, S_HF + dy, (dp, sibling)).wait_recv()

    @pl.loop(0, 4)
    def _(m):
        ht[span256(m), :] = jnp.transpose(hs[:, span256(m)])

    def wq_grad(k):
        both = jnp.concatenate([dqg[0, k], dqg[1, k]], axis=1)
        for m in range(4):
            out = dot(ht[m * 256:m * 256 + 256, :], both).astype(BF16)
            for h in range(2):
                pw[k // 2, 2 * (k % 2) + h, m * 256:m * 256 + 256] = out[:, h * HEAD:(h + 1) * HEAD]

    def r1_copy(core, to, part):
        if core == 0:
            src, slot, dest = pw.at[to, pl.ds(2 * part, 2), pl.ds(0, 512)], x, (2 * c + to) * 4 + z
        else:
            src, slot, dest = pw.at[:, to, pl.ds(512, 512)], z, x * 4 + to
            part = c
        dst = r1.at[slot, pl.ds(2 * part, 2)]
        sem = ssem.at[S_R1 + (2 * to + part if core == 0 else 4 + to)]
        own = jnp.logical_and(dest == dp, c == core)
        return src, dst, sem, rsem.at[S_R1 + slot * 2 + part], (dest, y * 2 + core), own

    def r1_start(core, to, part):
        src, dst, s_sem, r_sem, dest, own = r1_copy(core, to, part)

        @pl.when(own)
        def _():
            pltpu.make_async_copy(src, dst, s_sem).start()

        @pl.when(jnp.logical_not(own))
        def _():
            pltpu.make_async_remote_copy(
                src_ref=src, dst_ref=dst, send_sem=s_sem, recv_sem=r_sem, device_id=dest, device_id_type=MESH
            ).start()

    def r1_wait(core, to, part):
        src, dst, s_sem, r_sem, dest, own = r1_copy(core, to, part)

        @pl.when(own)
        def _():
            pltpu.make_async_copy(src, dst, s_sem).wait()

        @pl.when(jnp.logical_not(own))
        def _():
            pltpu.make_async_remote_copy(
                src_ref=src, dst_ref=dst, send_sem=s_sem, recv_sem=r_sem, device_id=dest, device_id_type=MESH
            ).wait_send()

    R1_ALL = [(0, to, part) for to in range(2) for part in range(2)] + [(1, to, 0) for to in range(4)]

    for h in range(2):
        for slot in (2, 3):
            dq_recv(h, slot)
    for k in range(4):
        wq_grad(k)
        r1_start(0, k // 2, k % 2)
        if k >= 2:
            r1_start(1, 2 * (k - 2), 0)
            r1_start(1, 2 * (k - 2) + 1, 0)
    send_dkv(1, 1)
    for h in range(2):
        for j in range(7):
            go(att_copy(h, j))
        local(atth.at[h, own_tokens], att_out.at[:, pl.ds(cols(seq, h), HEAD)], 12 + h).start()

    for yy in range(4):
        for h in range(2):
            dqc[:, (2 * yy + h) * HEAD:(2 * yy + h + 1) * HEAD] = dqg[h, yy, span256(y)]

    @pl.loop(0, 16)
    def _(d):
        theirs = dot(dqc[pl.ds(pl.multiple_of((1 - c) * 128, 128), 128), :], wb[d], ((1,), (1,)))
        dhs[:, span256(d)] = theirs
        ours = dot(dqc[pl.ds(pl.multiple_of(c * 128, 128), 128), :], wb[d], ((1,), (1,)))
        dho[:, span256(d)] = ours

    dh_copy = remote(dhs, dhr, S_DH, (dp, sibling))
    dh_copy.start()
    sent.append(dh_copy)
    for core, to, part in R1_ALL:
        r1_wait(core, to, part)
    line1, line2 = jnp.where(c == 0, x, z), jnp.where(c == 0, z, x)

    @pl.loop(0, 8)
    def _(k):
        from_core = jnp.where(c == 0, x // 2, k % 2)

        @pl.when(jnp.logical_not(jnp.logical_and(k // 2 == line1, from_core == c)))
        def _():
            ref = r1.at[k // 2, pl.ds(2 * (k % 2), 2)]
            pltpu.make_async_remote_copy(
                src_ref=ref, dst_ref=ref, send_sem=ssem.at[S_R1], recv_sem=rsem.at[S_R1 + k],
                device_id=(dp, sibling), device_id_type=MESH,
            ).wait_recv()

    def r2_copy(step):
        to = (line2 + step) % 4
        dest = jnp.where(c == 0, line1 * 4 + to, to * 4 + line1)
        return remote(r1s.at[to], r2.at[step], S_R2 + step, (dest, seq))

    for step in (1, 3, 2, 0):
        to = (line2 + step) % 4
        total = r1[0, to].astype(F32)
        for k in range(1, 4):
            total += r1[k, to].astype(F32)
        if step:
            r1s[to] = total.astype(BF16)
            go(r2_copy(step))
        else:
            dwq_out[...] = total
    dh_copy.wait_recv()
    dh_out[...] = (dho[...] + dhr[...]).astype(BF16)
    for step in (1, 3, 2):
        r2_copy(step).wait_recv()
        dwq_out[...] += r2[step].astype(F32)

    for h in range(2):
        for j in range(7):
            att_copy(h, j).wait_recv()
        local(atth.at[h, own_tokens], att_out.at[:, pl.ds(cols(seq, h), HEAD)], 12 + h).wait()
        for i, (src, dst) in enumerate(((dks, dk_out), (dvs, dv_out))):
            local(src.at[h, rows4], dst.at[:, :, pl.ds(cols(seq, h), HEAD)], 8 + 2 * h + i).wait()

            @pl.loop(1, 8)
            def _(j):
                frm = peer(4 - j // 2, 2 - j % 2)
                ref = dst.at[:, :, pl.ds(cols(frm, h), HEAD)]
                remote(src.at[h, pl.ds(frm * 4, 4)], ref, S_DKV + (h * 2 + i) * 8 + j, (dp, frm)).wait_recv()
                dkv_copy(h, i, j).wait_send()

    for copy in sent:
        copy.wait_send()


FINISH_PARTS = 4


def finish(
    att_in, dh_in, dwq_in, dk_in, dv_in, att_out, dh_out, dwq_out, dk_out, dv_out,
    att, dh, dwq, dk, dv, dk_wide, dv_wide, in_sem, out_sem,
):
    rows = 512 // FINISH_PARTS
    loads, stores = [], []
    for k in range(FINISH_PARTS):
        span = pl.ds(k * rows, rows)
        for t, (src, dst) in enumerate(((dk_in, dk), (dv_in, dv))):
            loads.append(pltpu.make_async_copy(src.at[span], dst.at[span], in_sem.at[2 * k + t]))
    small = ((att_in, att, att_out), (dh_in, dh, dh_out), (dwq_in, dwq, dwq_out))
    for t, (src, mid, _) in enumerate(small):
        loads.append(pltpu.make_async_copy(src, mid, in_sem.at[2 * FINISH_PARTS + t]))
    for load in loads:
        load.start()
    for k in range(FINISH_PARTS):
        span = pl.ds(k * rows, rows)
        for t, (narrow, wide, dst) in enumerate(((dk, dk_wide, dk_out), (dv, dv_wide, dv_out))):
            loads[2 * k + t].wait()
            wide[span, :] = narrow[span, :].astype(F32)
            stores.append(pltpu.make_async_copy(wide.at[span], dst.at[span], out_sem.at[2 * k + t]))
            stores[-1].start()
    for t, (_, mid, dst) in enumerate(small):
        loads[2 * FINISH_PARTS + t].wait()
        stores.append(pltpu.make_async_copy(mid, dst, out_sem.at[2 * FINISH_PARTS + t]))
        stores[-1].start()
    for store in stores:
        store.wait()


def on_device(hidden, w_query, nbr_keys, nbr_values, nbr_ids, d_attended):
    vmem = pltpu.VMEM
    anywhere = pl.BlockSpec(memory_space=pl.ANY)
    in_vmem = pl.BlockSpec(memory_space=pltpu.VMEM)
    attended, d_hidden, d_wq, d_keys, d_values = pl.pallas_call(
        kernel,
        out_shape=(
            jax.ShapeDtypeStruct((128, 2048), BF16),
            jax.ShapeDtypeStruct((128, 4096), BF16),
            jax.ShapeDtypeStruct((512, 128), F32),
            jax.ShapeDtypeStruct((4, 128, 2048), BF16),
            jax.ShapeDtypeStruct((4, 128, 2048), BF16),
        ),
        in_specs=[anywhere, anywhere, anywhere, anywhere, in_vmem, anywhere],
        out_specs=(anywhere, in_vmem, in_vmem, anywhere, anywhere),
        scratch_shapes=[
            vmem((256, 4096), BF16),
            vmem((16, 256, 1024), BF16),
            *[vmem((32, 128, 128), BF16)] * 4,
            vmem((1024, 256), BF16),
            vmem((1024, 256), BF16),
            vmem((256, 1024), F32),
            vmem((256, 1024), BF16),
            vmem((1024, 1024), BF16),
            vmem((1024, 1024), BF16),
            vmem((33, 128, 128), BF16),
            vmem((33, 128, 128), BF16),
            vmem((2, 32, 128, 128), BF16),
            vmem((2, 32, 128, 128), BF16),
            vmem((2, 1024, 128), BF16),
            vmem((2, 4, 1024, 128), BF16),
            vmem((256, 1024), BF16),
            vmem((2, 4, 1024, 128), BF16),
            vmem((4, 4, 512, 128), BF16),
            vmem((4, 512, 128), BF16),
            vmem((4, 512, 128), BF16),
            vmem((128, 4096), F32),
            vmem((128, 4096), F32),
            vmem((128, 4096), F32),
            vmem((8, 128), jnp.int32),
            vmem((8, 8, 128), jnp.int32),
            pltpu.SMEM((8, 8, 128), jnp.int32),
            pltpu.SemaphoreType.DMA((N_SEMS,)),
            pltpu.SemaphoreType.DMA((N_SEMS,)),
        ],
        compiler_params=pltpu.CompilerParams(
            collective_id=0, has_side_effects=True, vmem_limit_bytes=60 * 2**20
        ),
        name="group_attention",
    )(hidden, w_query, nbr_keys, nbr_values, nbr_ids, d_attended)
    parts = (attended, d_hidden, d_wq, d_keys.reshape(512, 2048), d_values.reshape(512, 2048))
    kinds = (BF16, BF16, F32, F32, F32)
    attended, d_hidden, d_wq, d_keys, d_values = pl.pallas_call(
        finish,
        out_shape=[jax.ShapeDtypeStruct(p.shape, kind) for p, kind in zip(parts, kinds)],
        in_specs=[anywhere] * 5,
        out_specs=[anywhere] * 5,
        scratch_shapes=[
            *[vmem(p.shape, p.dtype) for p in parts],
            *[vmem((512, 2048), F32)] * 2,
            *[pltpu.SemaphoreType.DMA((2 * FINISH_PARTS + 3,))] * 2,
        ],
        compiler_params=pltpu.CompilerParams(vmem_limit_bytes=60 * 2**20),
        name="finish",
    )(*parts)
    return attended, d_hidden, d_wq, d_keys.reshape(4, 128, 2048), d_values.reshape(4, 128, 2048)


def solution(mesh):
    placed = (
        P(("dp", "seq"), None),
        P("dp", None),
        P(("dp", "seq"), None, None),
        P(("dp", "seq"), None, None),
        P(("dp", "seq"), None),
        P(("dp", "seq"), None),
    )
    return jax.shard_map(
        on_device,
        mesh=mesh,
        in_specs=placed,
        out_specs=(
            P(("dp", "seq"), None),
            P(("dp", "seq"), None),
            P("seq", "dp"),
            P(("dp", "seq"), None, None),
            P(("dp", "seq"), None, None),
        ),
        check_vma=False,
    )
```

```python
import functools

import jax
import jax.numpy as jnp
from jax import lax
from jax.experimental import pallas as pl
from jax.experimental.pallas import tpu as pltpu
from jax.sharding import PartitionSpec as P

BF16 = jnp.bfloat16
F32 = jnp.float32
MESH = pl.DeviceIdType.MESH
HEAD = 128
SCALE = HEAD ** (-0.5)
BLOCK = 64
NLEN = 128


class Pool:
    def __init__(self):
        self.used = 0

    def take(self, count):
        first = self.used
        self.used += count
        return first


POOL = Pool()
S_W = POOL.take(80)
S_KV = POOL.take(4)
S_DO = POOL.take(1)
S_GG = POOL.take(4)
S_ID = POOL.take(8)
S_HID = POOL.take(1)
S_Q = POOL.take(8)
S_HS = POOL.take(4)
S_HF = POOL.take(4)
S_ST = POOL.take(8)
S_RET = POOL.take(16)
S_DQ = POOL.take(8)
S_DKV = POOL.take(2)
S_ATT = POOL.take(1)
S_DH = POOL.take(1)
S_R1 = POOL.take(16)
S_R2 = POOL.take(4)
S_LOCAL = POOL.take(16)
N_SEMS = POOL.used
SLOTS = 16


def dot(a, b, dims=((1,), (0,))):
    return lax.dot_general(a, b, (dims, ((), ())), preferred_element_type=F32)


def kernel(
    hidden, weight, keys, values, ids, grads,
    att_out, dh_out, dwq_out, dk_out, dv_out,
    hid, wb0, wb1, kc0, kc1, vc0, vc1, gg, qg0, qg1, qacc, hs, ht, st_buf, dp_buf, low_buf, ds_buf, stat0, stat1,
    sa0, sa1, sd0, sd1, ra0, ra1, rd0, rd1, ck, cv, dks, dvs, att_s, dqg0, dqg1,
    r1, r1s, r2, dhs, dho, dhr, idv, idg, ids_s, ssem, rsem,
):
    dp = lax.axis_index("dp")
    seq = lax.axis_index("seq")
    x, z = dp // 4, dp % 4
    y, c = seq // 2, seq % 2
    wb, kc, vc, qg, stat = (wb0, wb1), (kc0, kc1), (vc0, vc1), (qg0, qg1), (stat0, stat1)
    sa, sd, ra, rd, dqg = (sa0, sa1), (sd0, sd1), (ra0, ra1), (rd0, rd1), (dqg0, dqg1)

    def remote(src, dst, sem, to):
        return pltpu.make_async_remote_copy(
            src_ref=src, dst_ref=dst, send_sem=ssem.at[sem], recv_sem=rsem.at[sem],
            device_id=to, device_id_type=MESH,
        )

    def local(src, dst, sem):
        return pltpu.make_async_copy(src, dst, ssem.at[S_LOCAL + sem])

    def peer(dy, dc):
        return ((y + dy + 4) % 4) * 2 + (c + dc) % 2

    def wide(core):
        return pl.ds(pl.multiple_of(core * 1024, 1024), 1024)

    def chunk(core, ch):
        return pl.ds(pl.multiple_of(core * 1024 + ch * 512, 512), 512)

    sibling = peer(0, 1)
    others = [(dy, dc) for dy in (1, 3, 2, 0) for dc in (0, 1) if (dy, dc) != (0, 0)]

    idv[...] = jnp.zeros_like(idv)
    idv[0:2, 0:2] = ids[...]

    own_w = [local(weight.at[:, chunk(c, ch)], wb[ch].at[dp], ch) for ch in range(2)]
    own_hid = local(hidden, hid.at[pl.ds(pl.multiple_of(c * 128, 128), 128)], 2)
    own_blocks = pl.ds(4 * y + 2 * c, 2)
    own_do = local(grads.at[:, :, wide(c)], gg.at[own_blocks], 3)
    own_rows = pl.ds(4 * c, 4)
    own_kv = [
        local(src.at[:, :, chunk(c, ch)], dst[ch].at[own_rows], 4 + 2 * i + ch)
        for i, (src, dst) in enumerate(((keys, kc), (values, vc))) for ch in range(2)
    ]
    for copy in own_w + [own_hid, own_do] + own_kv:
        copy.start()

    barrier = pltpu.get_barrier_semaphore()

    def greet(to):
        pl.semaphore_signal(barrier, inc=1, device_id=to, device_id_type=MESH)

    for dy, dc in others:
        greet((dp, peer(dy, dc)))
    for step in (1, 2, 3):
        for core in (0, 1):
            greet((((x + step) % 4) * 4 + z, y * 2 + core))
            greet((x * 4 + (z + step) % 4, y * 2 + core))
    pl.semaphore_wait(barrier, 7 + 12)

    def moved(axis, step):
        if axis == 0:
            return (((x + step + 4) % 4) * 4 + z, seq)
        return (x * 4 + (z + step + 4) % 4, seq)

    def source(t, r1_, r2_):
        rx, rz = (r1_, r2_) if t == 0 else (r2_, r1_)
        return ((x + rx + 4) % 4) * 4 + (z + rz + 4) % 4

    LINE = (0, -1, 1, 2)
    PART = {"all": (0, 128), "lo": (0, 64), "hi": (64, 64)}

    def piece(ch, t, r1_, r2_, part):
        lo, n = PART[part]
        return wb[ch].at[source(t, r1_, r2_), pl.ds(t * 128 + lo, n)]

    def w_parts(ch, t, phase, q, slot):
        axis = t if phase == 1 else 1 - t
        sem = S_W + 40 * ch + 20 * t + (slot if phase == 1 else 4 + 4 * q + slot)
        step = 1 if slot % 2 == 0 else -1
        return axis, sem, step, "all" if slot < 2 else ("lo" if slot == 2 else "hi")

    def w_copy(ch, t, phase, q, slot):
        axis, sem, step, part = w_parts(ch, t, phase, q, slot)
        near = 0 if slot < 2 else -step
        src = piece(ch, t, near, 0, part) if phase == 1 else piece(ch, t, LINE[q], near, part)
        return remote(src, src, sem, moved(axis, step))

    def w_recv(ch, t, phase, q, slot):
        axis, sem, step, part = w_parts(ch, t, phase, q, slot)
        far = -step if slot < 2 else 2
        dst = piece(ch, t, far, 0, part) if phase == 1 else piece(ch, t, LINE[q], far, part)
        remote(dst, dst, sem, moved(axis, step)).wait_recv()

    sent = []

    def go(copy):
        copy.start()
        sent.append(copy)

    def w_wave(ch, wave):
        if wave == 0:
            own_w[ch].wait()
            for phase in (1, 2):
                for t in (0, 1):
                    for slot in (0, 1):
                        go(w_copy(ch, t, phase, 0, slot))
        elif wave == 1:
            for t in (0, 1):
                for slot, q in ((0, 1), (1, 2)):
                    w_recv(ch, t, 1, 0, slot)
                    go(w_copy(ch, t, 1, 0, slot + 2))
                    for s in (0, 1):
                        go(w_copy(ch, t, 2, q, s))
        elif wave == 3:
            for t in (0, 1):
                for slot in (2, 3):
                    w_recv(ch, t, 1, 0, slot)
                for s in (0, 1):
                    go(w_copy(ch, t, 2, 3, s))
        else:
            for q in {2: (0,), 4: (1, 2), 5: (3,)}[wave]:
                for t in (0, 1):
                    for slot in (0, 1):
                        w_recv(ch, t, 2, q, slot)
                        go(w_copy(ch, t, 2, q, slot + 2))

    def ring_copy(ref, sem, slot):
        step = 1 if slot % 2 == 0 else -1
        near = y if slot < 2 else (y - step + 4) % 4
        lo, n = ((0, 4), (0, 4), (0, 2), (2, 2))[slot]
        part = ref.at[pl.ds(4 * near + lo, n)]
        return remote(part, part, sem + slot, (dp, peer(step, 0)))

    def ring_recv(ref, sem, slot):
        step = 1 if slot % 2 == 0 else -1
        far = (y - step + 4) % 4 if slot < 2 else (y + 2) % 4
        lo, n = ((0, 4), (0, 4), (0, 2), (2, 2))[slot]
        part = ref.at[pl.ds(4 * far + lo, n)]
        remote(part, part, sem + slot, (dp, peer(step, 0))).wait_recv()

    def ring_send(ref, sem):
        for slot in (0, 1):
            go(ring_copy(ref, sem, slot))

    def ring_forward(ref, sem):
        for slot in (0, 1):
            ring_recv(ref, sem, slot)
            go(ring_copy(ref, sem, slot + 2))

    def ring_finish(ref, sem):
        for slot in (2, 3):
            ring_recv(ref, sem, slot)

    def project(ch, rx):
        @pl.loop(0, 4)
        def _(i):
            d = ((x + rx + 4) % 4) * 4 + i
            rows = hid[:, pl.ds(pl.multiple_of(d * 256, 256), 256)]
            for n in range(2):
                span = slice(n * 256, n * 256 + 256)
                qacc[:, span] += dot(rows, wb[ch][d, :, span])

    def query(ch):
        qacc[...] = jnp.zeros_like(qacc)
        for q, rx in ((0, 0), (1, -1), (2, 1)):
            for slot in (2, 3):
                w_recv(ch, 0, 2, q, slot)
            project(ch, rx)
        for slot in (2, 3):
            w_recv(ch, 0, 2, 3, slot)
            for q in range(4):
                w_recv(ch, 1, 2, q, slot)
        project(ch, 2)
        qg[ch][pl.ds(4 * y, 4)] = qacc[...].astype(BF16).reshape(4, BLOCK, 512)
        ring_send(qg[ch], S_Q + 4 * ch)

    def span256(k):
        return pl.ds(pl.multiple_of(k * 256, 256), 256)

    def feats(k):
        return pl.ds(pl.multiple_of(k * 1024, 1024), 1024)

    def tokens(s):
        return pl.ds(pl.multiple_of(s * 128, 128), 128)

    own_hid_rows = hid.at[tokens(c)]
    hidden_out = []

    def send_hidden():
        for dy in (1, 3, 2):
            to = peer(dy, 0)
            go(remote(own_hid_rows.at[:, feats(to // 2)], hs.at[tokens(seq)], S_HS + dy, (dp, to)))
        hs[span256(y), :] = hid[:, feats(y)]

    def forward_hidden():
        for dy in (1, 3, 2):
            frm = peer(-dy, 0)
            ref = hs.at[tokens(frm)]
            remote(ref, ref, S_HS + dy, (dp, frm)).wait_recv()
            hidden_out.append(remote(ref, ref, S_HF + dy, (dp, sibling)))
            hidden_out[-1].start()

    def slot_of(s, core):
        shard = 2 * y + core
        block, row, other = jnp.int32(0), jnp.int32(0), jnp.int32(0)
        for j in range(4):
            here = ids_s[s, j // 2, j % 2]
            hit = here // 4 == shard
            block = jnp.where(hit, j // 2, block)
            row = jnp.where(hit, here % 4, row)
            other = jnp.where(hit, ids_s[s, j // 2, 1 - j % 2], other)
        return 2 * s + block, 4 * core + row, other

    def diagonal(a, b):
        none = jnp.zeros((BLOCK, HEAD), BF16)
        return jnp.concatenate(
            [jnp.concatenate([a, none], axis=1), jnp.concatenate([none, b], axis=1)], axis=0
        )

    def operands(ch, e, b0, k0, b1, k1):
        lanes = slice(e * HEAD, e * HEAD + HEAD)
        far = slice(ch * 512 + e * HEAD, ch * 512 + e * HEAD + HEAD)
        kk = jnp.concatenate([kc[ch][k0, :, lanes], kc[ch][k1, :, lanes]], axis=1)
        vv = jnp.concatenate([vc[ch][k0, :, lanes], vc[ch][k1, :, lanes]], axis=1)
        qq = diagonal(qg[ch][b0, :, lanes], qg[ch][b1, :, lanes])
        dd = diagonal(gg[b0, :, far], gg[b1, :, far])
        return lanes, kk, vv, qq, dd

    def first_pass(ch):
        @pl.loop(0, 8)
        def _(s):
            b0, k0, _o0 = slot_of(s, 0)
            b1, k1, _o1 = slot_of(s, 1)
            for e in range(4):
                _, kk, vv, qq, dd = operands(ch, e, b0, k0, b1, k1)
                scores = dot(kk, qq, ((1,), (1,))) * SCALE
                d_probs = dot(vv, dd, ((1,), (1,)))
                peak = jnp.max(scores, axis=0, keepdims=True)
                expo = jnp.exp(scores - peak)
                total = jnp.sum(expo, axis=0, keepdims=True)
                st_buf[4 * s + e] = scores
                dp_buf[4 * s + e] = d_probs
                stat[ch][y, s, e:e + 1] = peak + jnp.log(total)
                stat[ch][y, s, 4 + e:5 + e] = jnp.sum(expo * d_probs, axis=0, keepdims=True) / total
        for dy in (1, 3, 2):
            go(remote(stat[ch].at[y], stat[ch].at[y], S_ST + 4 * ch + dy, (dp, peer(dy, 0))))

    def wait_stats(ch):
        for dy in (1, 3, 2):
            frm = peer(-dy, 0)
            ref = stat[ch].at[frm // 2]
            remote(ref, ref, S_ST + 4 * ch + dy, (dp, frm)).wait_recv()

    def second_pass(ch):
        left = lax.broadcasted_iota(jnp.int32, (8, 128), 1) < BLOCK

        @pl.loop(0, 8)
        def _(s):
            b0, k0, o0 = slot_of(s, 0)
            b1, k1, o1 = slot_of(s, 1)
            theirs0 = stat[ch][o0 // 8, s]
            theirs1 = stat[ch][o1 // 8, s]
            turned0 = jnp.concatenate([theirs0[:, BLOCK:], theirs0[:, :BLOCK]], axis=1)
            turned1 = jnp.concatenate([theirs1[:, BLOCK:], theirs1[:, :BLOCK]], axis=1)
            theirs0 = jnp.where((o0 // 4) % 2 == 0, theirs0, turned0)
            theirs1 = jnp.where((o1 // 4) % 2 == 1, theirs1, turned1)
            theirs = jnp.where(left, theirs0, theirs1)
            ours = stat[ch][y, s]
            top = jnp.maximum(ours[:4], theirs[:4])
            whole = top + jnp.log(jnp.exp(ours[:4] - top) + jnp.exp(theirs[:4] - top))
            delta = jnp.exp(ours[:4] - whole) * ours[4:] + jnp.exp(theirs[:4] - whole) * theirs[4:]
            for e in range(4):
                lanes, kk, _, _, _ = operands(ch, e, b0, k0, b1, k1)
                probs = jnp.exp(st_buf[4 * s + e] - whole[e:e + 1])
                low = probs.astype(BF16)
                d_scores = (probs * (dp_buf[4 * s + e] - delta[e:e + 1]) * SCALE).astype(BF16)
                dq = dot(d_scores, kk, ((0,), (0,))).astype(BF16)
                sd[ch][2 * s, :, lanes] = dq[:BLOCK, :HEAD]
                sd[ch][2 * s + 1, :, lanes] = dq[BLOCK:, HEAD:]
                low_buf[4 * s + e] = low
                ds_buf[4 * s + e] = d_scores

    def third_pass(ch):
        @pl.loop(0, 8)
        def _(s):
            b0, k0, _o0 = slot_of(s, 0)
            b1, k1, _o1 = slot_of(s, 1)
            for e in range(4):
                lanes, _, vv, qq, dd = operands(ch, e, b0, k0, b1, k1)
                low, d_scores = low_buf[4 * s + e], ds_buf[4 * s + e]
                att = dot(low, vv, ((0,), (0,))).astype(BF16)
                sa[ch][2 * s, :, lanes] = att[:BLOCK, :HEAD]
                sa[ch][2 * s + 1, :, lanes] = att[BLOCK:, HEAD:]
                dk = dot(d_scores, qq).astype(BF16)
                dv = dot(low, dd).astype(BF16)
                for i in range(2):
                    ck[2 * s + i, :, lanes] = dk[:, i * HEAD:(i + 1) * HEAD]
                    cv[2 * s + i, :, lanes] = dv[:, i * HEAD:(i + 1) * HEAD]

    def give_back(ch, kind):
        src, dst = ((sd, rd), (sa, ra))[kind]
        for dy in (1, 3, 2):
            to = peer(dy, 0)
            go(remote(
                src[ch].at[pl.ds(4 * (to // 2), 4)], dst[ch].at[pl.ds(4 * y, 4)],
                S_RET + 8 * kind + 4 * ch + dy, (dp, to),
            ))
        dst[ch][pl.ds(4 * y, 4)] = src[ch][pl.ds(4 * y, 4)]

    def take_back(ch, kind):
        src, dst = ((sd, rd), (sa, ra))[kind]
        for dy in (1, 3, 2):
            frm = peer(-dy, 0)
            ref = dst[ch].at[pl.ds(4 * (frm // 2), 4)]
            remote(ref, ref, S_RET + 8 * kind + 4 * ch + dy, (dp, frm)).wait_recv()
        for block in range(4):
            core, u = block // 2, block % 2
            total = jnp.zeros((BLOCK, 512), F32)
            for j in range(2):
                name = ids_s[2 * y + core, u, j]
                total += dst[ch][(name // 8) * 4 + core * 2 + (name // 4) % 2].astype(F32)
            if kind == 0:
                dqg[ch][4 * y + block] = total.astype(BF16)
            else:
                att_s[block * BLOCK:(block + 1) * BLOCK, ch * 512:(ch + 1) * 512] = total.astype(BF16)

    def sum_kv(ch):
        @pl.loop(0, 8)
        def _(row):
            at = []
            for s in range(8):
                one = jnp.int32(SLOTS)
                for j in range(4):
                    one = jnp.where(ids_s[s, j // 2, j % 2] == 8 * y + row, 2 * s + row // 4, one)
                at.append(one)
            for src, dst in ((ck, dks), (cv, dvs)):
                for e in range(4):
                    lanes = slice(e * HEAD, e * HEAD + HEAD)
                    total = src[at[0], :, lanes].astype(F32)
                    for s in range(1, 8):
                        total += src[at[s], :, lanes].astype(F32)
                    dst[row, :, ch * 512 + e * HEAD:ch * 512 + (e + 1) * HEAD] = total.astype(BF16)

    def wq_grad(k):
        ch, pair = k // 2, k % 2
        both = dqg[ch][:, :, pair * 256:pair * 256 + 256].reshape(1024, 256)
        for m in range(4):
            hs[m * 256:m * 256 + 256, k * 256:k * 256 + 256] = dot(
                ht[m * 256:m * 256 + 256, :], both
            ).astype(BF16)

    def r1_copy(core, ch, b):
        src = hs.at[pl.ds(core * 512, 512), pl.ds((4 * ch + b) * HEAD, HEAD)]
        if core == 0:
            slot, part, dest = x, b, (2 * c + ch) * 4 + z
        else:
            slot, part, dest = z, 2 * c + ch, x * 4 + b
        dst = r1.at[slot, part]
        sem = ssem.at[S_R1 + core * 8 + ch * 4 + b]
        own = jnp.logical_and(dest == dp, c == core)
        return src, dst, sem, rsem.at[S_R1 + slot * 4 + part], (dest, y * 2 + core), own

    def r1_start(core, ch, b):
        src, dst, s_sem, r_sem, dest, own = r1_copy(core, ch, b)

        @pl.when(own)
        def _():
            pltpu.make_async_copy(src, dst, s_sem).start()

        @pl.when(jnp.logical_not(own))
        def _():
            pltpu.make_async_remote_copy(
                src_ref=src, dst_ref=dst, send_sem=s_sem, recv_sem=r_sem, device_id=dest, device_id_type=MESH
            ).start()

    def r1_wait(core, ch, b):
        src, dst, s_sem, r_sem, dest, own = r1_copy(core, ch, b)

        @pl.when(own)
        def _():
            pltpu.make_async_copy(src, dst, s_sem).wait()

        @pl.when(jnp.logical_not(own))
        def _():
            pltpu.make_async_remote_copy(
                src_ref=src, dst_ref=dst, send_sem=s_sem, recv_sem=r_sem, device_id=dest, device_id_type=MESH
            ).wait_send()

    def wq_send(k):
        wq_grad(k)
        for b in (2 * (k % 2), 2 * (k % 2) + 1):
            for core in range(2):
                r1_start(core, k // 2, b)

    w_wave(0, 0)
    own_hid.wait()
    go(remote(own_hid_rows, own_hid_rows, S_HID, (dp, sibling)))
    go(remote(grads.at[:, :, wide(1 - c)], gg.at[own_blocks], S_DO, (dp, sibling)))
    for j, (dy, dc) in enumerate(others):
        go(remote(idv, idg.at[seq], S_ID + j, (dp, peer(dy, dc))))
    for i, (src, dst) in enumerate(((keys, kc), (values, vc))):
        for ch in range(2):
            go(remote(src.at[:, :, chunk(1 - c, ch)], dst[ch].at[own_rows], S_KV + 2 * i + ch, (dp, sibling)))
    w_wave(0, 1)
    their_blocks = gg.at[pl.ds(4 * y + 2 * (1 - c), 2)]
    remote(their_blocks, their_blocks, S_DO, (dp, sibling)).wait_recv()
    own_do.wait()
    ring_send(gg, S_GG)
    w_wave(0, 2)
    w_wave(0, 3)
    w_wave(1, 0)
    other_rows = hid.at[tokens(1 - c)]
    remote(other_rows, other_rows, S_HID, (dp, sibling)).wait_recv()
    w_wave(0, 4)
    ring_forward(gg, S_GG)
    w_wave(0, 5)
    for j, (dy, dc) in enumerate(others):
        frm = peer(-dy, -dc + 2)
        remote(idv, idg.at[frm], S_ID + j, (dp, frm)).wait_recv()
    idg[seq] = idv[...]
    to_smem = local(idg, ids_s, 8)
    to_smem.start()
    to_smem.wait()
    query(0)
    w_wave(1, 1)
    w_wave(1, 2)
    ck[SLOTS] = jnp.zeros((NLEN, 512), BF16)
    cv[SLOTS] = jnp.zeros((NLEN, 512), BF16)
    for copy in own_kv:
        copy.wait()
    their_rows = pl.ds(4 * (1 - c), 4)
    for i, dst in enumerate((kc, vc)):
        for ch in range(2):
            ref = dst[ch].at[their_rows]
            remote(ref, ref, S_KV + 2 * i + ch, (dp, sibling)).wait_recv()
    ring_forward(qg[0], S_Q)
    send_hidden()
    w_wave(1, 3)
    w_wave(1, 4)
    ring_finish(gg, S_GG)
    ring_finish(qg[0], S_Q)
    first_pass(0)
    w_wave(1, 5)
    def dh_add(ch, first):
        @pl.loop(0, 16)
        def _(d):
            for core, buf in ((1 - c, dhs), (c, dho)):
                rows = dqg[ch][pl.ds(4 * y + 2 * core, 2)].reshape(128, 512)
                part = dot(rows, wb[ch][d], ((1,), (1,)))
                if first:
                    buf[:, span256(d)] = part
                else:
                    buf[:, span256(d)] += part

    query(1)
    wait_stats(0)
    second_pass(0)
    ring_forward(qg[1], S_Q + 4)
    give_back(0, 0)
    third_pass(0)
    sum_kv(0)
    ring_finish(qg[1], S_Q + 4)
    first_pass(1)
    take_back(0, 0)
    ring_send(dqg[0], S_DQ)
    wait_stats(1)
    second_pass(1)
    give_back(1, 0)
    forward_hidden()
    ring_forward(dqg[0], S_DQ)
    third_pass(1)
    for dy in (1, 3, 2):
        frm = peer(-dy, 1)
        ref = hs.at[tokens(frm)]
        remote(ref, ref, S_HF + dy, (dp, sibling)).wait_recv()

    @pl.loop(0, 4)
    def _(m):
        ht[span256(m), :] = jnp.transpose(hs[:, span256(m)])

    for copy in hidden_out:
        copy.wait_send()
    dh_add(0, True)
    take_back(1, 0)
    ring_send(dqg[1], S_DQ + 4)
    ring_finish(dqg[0], S_DQ)
    wq_send(0)
    ring_forward(dqg[1], S_DQ + 4)
    give_back(0, 1)
    give_back(1, 1)
    wq_send(1)
    sum_kv(1)
    their_kv = []
    for i, (src, dst) in enumerate(((dks, dk_out), (dvs, dv_out))):
        go(remote(src.at[their_rows], dst.at[:, :, wide(c)], S_DKV + i, (dp, sibling)))
        their_kv.append(remote(src.at[their_rows], dst.at[:, :, wide(1 - c)], S_DKV + i, (dp, sibling)))
    own_kv_out = [
        local(src.at[own_rows], dst.at[:, :, wide(c)], 9 + i)
        for i, (src, dst) in enumerate(((dks, dk_out), (dvs, dv_out)))
    ]
    for copy in own_kv_out:
        copy.start()
    ring_finish(dqg[1], S_DQ + 4)
    wq_send(2)
    wq_send(3)
    dh_add(1, False)
    dh_copy = remote(dhs, dhr, S_DH, (dp, sibling))
    go(dh_copy)

    for core in range(2):
        for ch in range(2):
            for b in range(4):
                r1_wait(core, ch, b)
    line1, line2 = jnp.where(c == 0, x, z), jnp.where(c == 0, z, x)

    @pl.loop(0, 16)
    def _(k):
        from_core = jnp.where(c == 0, x // 2, (k % 4) // 2)

        @pl.when(jnp.logical_not(jnp.logical_and(k // 4 == line1, from_core == c)))
        def _():
            ref = r1.at[k // 4, k % 4]
            pltpu.make_async_remote_copy(
                src_ref=ref, dst_ref=ref, send_sem=ssem.at[S_R1], recv_sem=rsem.at[S_R1 + k],
                device_id=(dp, sibling), device_id_type=MESH,
            ).wait_recv()

    def r2_copy(step):
        to = (line2 + step) % 4
        dest = jnp.where(c == 0, line1 * 4 + to, to * 4 + line1)
        return remote(r1s.at[to], r2.at[step], S_R2 + step, (dest, seq))

    for step in (1, 3, 2, 0):
        to = (line2 + step) % 4
        total = r1[0, to].astype(F32)
        for k in range(1, 4):
            total += r1[k, to].astype(F32)
        if step:
            r1s[to] = total.astype(BF16)
            go(r2_copy(step))
        else:
            dwq_out[...] = total
    dh_copy.wait_recv()
    dh_out[...] = (dho[...] + dhr[...]).astype(BF16)
    for step in (1, 3, 2):
        r2_copy(step).wait_recv()
        dwq_out[...] += r2[step].astype(F32)
    for ch in range(2):
        take_back(ch, 1)
    own_att = local(att_s.at[tokens(c)], att_out.at[:, wide(c)], 11)
    own_att.start()
    go(remote(att_s.at[tokens(1 - c)], att_out.at[:, wide(c)], S_ATT, (dp, sibling)))

    own_att.wait()
    remote(att_s.at[tokens(1 - c)], att_out.at[:, wide(1 - c)], S_ATT, (dp, sibling)).wait_recv()
    for copy in own_kv_out:
        copy.wait()
    for copy in their_kv:
        copy.wait_recv()
    for copy in sent:
        copy.wait_send()


FINISH_PARTS = 4


def finish(
    att_in, dh_in, dwq_in, dk_in, dv_in, att_out, dh_out, dwq_out, dk_out, dv_out,
    att, dh, dwq, dk, dv, dk_wide, dv_wide, in_sem, out_sem,
):
    rows = 512 // FINISH_PARTS
    loads, stores = [], []
    for k in range(FINISH_PARTS):
        span = pl.ds(k * rows, rows)
        for t, (src, dst) in enumerate(((dk_in, dk), (dv_in, dv))):
            loads.append(pltpu.make_async_copy(src.at[span], dst.at[span], in_sem.at[2 * k + t]))
    small = ((att_in, att, att_out), (dh_in, dh, dh_out), (dwq_in, dwq, dwq_out))
    for t, (src, mid, _) in enumerate(small):
        loads.append(pltpu.make_async_copy(src, mid, in_sem.at[2 * FINISH_PARTS + t]))
    for load in loads:
        load.start()
    for k in range(FINISH_PARTS):
        span = pl.ds(k * rows, rows)
        for t, (narrow, wide, dst) in enumerate(((dk, dk_wide, dk_out), (dv, dv_wide, dv_out))):
            loads[2 * k + t].wait()
            wide[span, :] = narrow[span, :].astype(F32)
            stores.append(pltpu.make_async_copy(wide.at[span], dst.at[span], out_sem.at[2 * k + t]))
            stores[-1].start()
    for t, (_, mid, dst) in enumerate(small):
        loads[2 * FINISH_PARTS + t].wait()
        stores.append(pltpu.make_async_copy(mid, dst, out_sem.at[2 * FINISH_PARTS + t]))
        stores[-1].start()
    for store in stores:
        store.wait()


def on_device(hidden, w_query, nbr_keys, nbr_values, nbr_ids, d_attended):
    vmem = pltpu.VMEM
    anywhere = pl.BlockSpec(memory_space=pl.ANY)
    in_vmem = pl.BlockSpec(memory_space=pltpu.VMEM)
    attended, d_hidden, d_wq, d_keys, d_values = pl.pallas_call(
        kernel,
        out_shape=(
            jax.ShapeDtypeStruct((128, 2048), BF16),
            jax.ShapeDtypeStruct((128, 4096), BF16),
            jax.ShapeDtypeStruct((512, 128), F32),
            jax.ShapeDtypeStruct((4, 128, 2048), BF16),
            jax.ShapeDtypeStruct((4, 128, 2048), BF16),
        ),
        in_specs=[anywhere, anywhere, anywhere, anywhere, in_vmem, anywhere],
        out_specs=(anywhere, in_vmem, in_vmem, anywhere, anywhere),
        scratch_shapes=[
            vmem((256, 4096), BF16),
            *[vmem((16, 256, 512), BF16)] * 2,
            *[vmem((8, 128, 512), BF16)] * 4,
            vmem((16, 64, 1024), BF16),
            *[vmem((16, 64, 512), BF16)] * 2,
            vmem((256, 512), F32),
            vmem((1024, 1024), BF16),
            vmem((1024, 1024), BF16),
            vmem((32, 128, 128), F32),
            vmem((32, 128, 128), F32),
            vmem((32, 128, 128), BF16),
            vmem((32, 128, 128), BF16),
            *[vmem((4, 8, 8, 128), F32)] * 2,
            *[vmem((SLOTS, 64, 512), BF16)] * 8,
            *[vmem((SLOTS + 1, 128, 512), BF16)] * 2,
            *[vmem((8, 128, 1024), BF16)] * 2,
            vmem((256, 1024), BF16),
            *[vmem((16, 64, 512), BF16)] * 2,
            vmem((4, 4, 512, 128), BF16),
            vmem((4, 512, 128), BF16),
            vmem((4, 512, 128), BF16),
            vmem((128, 4096), F32),
            vmem((128, 4096), F32),
            vmem((128, 4096), F32),
            vmem((8, 128), jnp.int32),
            vmem((8, 8, 128), jnp.int32),
            pltpu.SMEM((8, 8, 128), jnp.int32),
            pltpu.SemaphoreType.DMA((N_SEMS,)),
            pltpu.SemaphoreType.DMA((N_SEMS,)),
        ],
        compiler_params=pltpu.CompilerParams(
            collective_id=0, has_side_effects=True, vmem_limit_bytes=62 * 2**20
        ),
        name="group_attention",
    )(hidden, w_query, nbr_keys, nbr_values, nbr_ids, d_attended.reshape(2, 64, 2048))
    parts = (attended, d_hidden, d_wq, d_keys.reshape(512, 2048), d_values.reshape(512, 2048))
    kinds = (BF16, BF16, F32, F32, F32)
    attended, d_hidden, d_wq, d_keys, d_values = pl.pallas_call(
        finish,
        out_shape=[jax.ShapeDtypeStruct(p.shape, kind) for p, kind in zip(parts, kinds)],
        in_specs=[anywhere] * 5,
        out_specs=[anywhere] * 5,
        scratch_shapes=[
            *[vmem(p.shape, p.dtype) for p in parts],
            *[vmem((512, 2048), F32)] * 2,
            *[pltpu.SemaphoreType.DMA((2 * FINISH_PARTS + 3,))] * 2,
        ],
        compiler_params=pltpu.CompilerParams(vmem_limit_bytes=60 * 2**20),
        name="finish",
    )(*parts)
    return attended, d_hidden, d_wq, d_keys.reshape(4, 128, 2048), d_values.reshape(4, 128, 2048)


def solution(mesh):
    placed = (
        P(("dp", "seq"), None),
        P("dp", None),
        P(("dp", "seq"), None, None),
        P(("dp", "seq"), None, None),
        P(("dp", "seq"), None),
        P(("dp", "seq"), None),
    )
    return jax.shard_map(
        on_device,
        mesh=mesh,
        in_specs=placed,
        out_specs=(
            P(("dp", "seq"), None),
            P(("dp", "seq"), None),
            P("seq", "dp"),
            P(("dp", "seq"), None, None),
            P(("dp", "seq"), None, None),
        ),
        check_vma=False,
    )
```

```python
import functools

import jax
import jax.numpy as jnp
from jax import lax
from jax.experimental import pallas as pl
from jax.experimental.pallas import tpu as pltpu
from jax.sharding import PartitionSpec as P

BF16 = jnp.bfloat16
F32 = jnp.float32
MESH = pl.DeviceIdType.MESH
HEAD = 128
SCALE = HEAD ** (-0.5)
BLOCK = 64
NLEN = 128


class Pool:
    def __init__(self):
        self.used = 0

    def take(self, count):
        first = self.used
        self.used += count
        return first


POOL = Pool()
S_W = POOL.take(80)
S_KV = POOL.take(4)
S_DO = POOL.take(1)
S_GG = POOL.take(4)
S_ID = POOL.take(8)
S_HID = POOL.take(1)
S_Q = POOL.take(8)
S_HS = POOL.take(4)
S_HF = POOL.take(4)
S_ST = POOL.take(8)
S_RET = POOL.take(16)
S_DQ = POOL.take(8)
S_DKV = POOL.take(2)
S_ATT = POOL.take(1)
S_DH = POOL.take(1)
S_R1 = POOL.take(16)
S_R2 = POOL.take(4)
S_LOCAL = POOL.take(16)
N_SEMS = POOL.used
SLOTS = 16


def dot(a, b, dims=((1,), (0,))):
    return lax.dot_general(a, b, (dims, ((), ())), preferred_element_type=F32)


def kernel(
    hidden, weight, keys, values, ids, grads,
    att_out, dh_out, dwq_out, dk_out, dv_out,
    hid, wb0, wb1, kc0, kc1, vc0, vc1, gg, qg0, qg1, qacc, hs, ht, st_buf, dp_buf, low_buf, ds_buf, stat0, stat1,
    sa0, sa1, sd0, sd1, ra0, ra1, rd0, rd1, ck, cv, dks, dvs, att_s, dqg0, dqg1,
    r1, r1s, r2, dhs, dho, dhr, idv, idg, ids_s, ssem, rsem,
):
    dp = lax.axis_index("dp")
    seq = lax.axis_index("seq")
    x, z = dp // 4, dp % 4
    y, c = seq // 2, seq % 2
    wb, kc, vc, qg, stat = (wb0, wb1), (kc0, kc1), (vc0, vc1), (qg0, qg1), (stat0, stat1)
    sa, sd, ra, rd, dqg = (sa0, sa1), (sd0, sd1), (ra0, ra1), (rd0, rd1), (dqg0, dqg1)

    def remote(src, dst, sem, to):
        return pltpu.make_async_remote_copy(
            src_ref=src, dst_ref=dst, send_sem=ssem.at[sem], recv_sem=rsem.at[sem],
            device_id=to, device_id_type=MESH,
        )

    def local(src, dst, sem):
        return pltpu.make_async_copy(src, dst, ssem.at[S_LOCAL + sem])

    def peer(dy, dc):
        return ((y + dy + 4) % 4) * 2 + (c + dc) % 2

    def wide(core):
        return pl.ds(pl.multiple_of(core * 1024, 1024), 1024)

    def chunk(core, ch):
        return pl.ds(pl.multiple_of(core * 1024 + ch * 512, 512), 512)

    sibling = peer(0, 1)
    others = [(dy, dc) for dy in (1, 3, 2, 0) for dc in (0, 1) if (dy, dc) != (0, 0)]

    idv[...] = jnp.zeros_like(idv)
    idv[0:2, 0:2] = ids[...]

    own_w = [local(weight.at[:, chunk(c, ch)], wb[ch].at[dp], ch) for ch in range(2)]
    own_hid = local(hidden, hid.at[pl.ds(pl.multiple_of(c * 128, 128), 128)], 2)
    own_blocks = pl.ds(4 * y + 2 * c, 2)
    own_do = local(grads.at[:, :, wide(c)], gg.at[own_blocks], 3)
    own_rows = pl.ds(4 * c, 4)
    own_kv = [
        local(src.at[:, :, chunk(c, ch)], dst[ch].at[own_rows], 4 + 2 * i + ch)
        for i, (src, dst) in enumerate(((keys, kc), (values, vc))) for ch in range(2)
    ]
    for copy in own_w + [own_hid, own_do] + own_kv:
        copy.start()

    barrier = pltpu.get_barrier_semaphore()

    def greet(to):
        pl.semaphore_signal(barrier, inc=1, device_id=to, device_id_type=MESH)

    for dy, dc in others:
        greet((dp, peer(dy, dc)))
    for step in (1, 2, 3):
        for core in (0, 1):
            greet((((x + step) % 4) * 4 + z, y * 2 + core))
            greet((x * 4 + (z + step) % 4, y * 2 + core))
    pl.semaphore_wait(barrier, 7 + 12)

    def moved(axis, step):
        if axis == 0:
            return (((x + step + 4) % 4) * 4 + z, seq)
        return (x * 4 + (z + step + 4) % 4, seq)

    def source(t, r1_, r2_):
        rx, rz = (r1_, r2_) if t == 0 else (r2_, r1_)
        return ((x + rx + 4) % 4) * 4 + (z + rz + 4) % 4

    LINE = (0, -1, 1, 2)
    PART = {"all": (0, 128), "lo": (0, 64), "hi": (64, 64)}

    def piece(ch, t, r1_, r2_, part):
        lo, n = PART[part]
        return wb[ch].at[source(t, r1_, r2_), pl.ds(t * 128 + lo, n)]

    def w_parts(ch, t, phase, q, slot):
        axis = t if phase == 1 else 1 - t
        sem = S_W + 40 * ch + 20 * t + (slot if phase == 1 else 4 + 4 * q + slot)
        step = 1 if slot % 2 == 0 else -1
        return axis, sem, step, "all" if slot < 2 else ("lo" if slot == 2 else "hi")

    def w_copy(ch, t, phase, q, slot):
        axis, sem, step, part = w_parts(ch, t, phase, q, slot)
        near = 0 if slot < 2 else -step
        src = piece(ch, t, near, 0, part) if phase == 1 else piece(ch, t, LINE[q], near, part)
        return remote(src, src, sem, moved(axis, step))

    def w_recv(ch, t, phase, q, slot):
        axis, sem, step, part = w_parts(ch, t, phase, q, slot)
        far = -step if slot < 2 else 2
        dst = piece(ch, t, far, 0, part) if phase == 1 else piece(ch, t, LINE[q], far, part)
        remote(dst, dst, sem, moved(axis, step)).wait_recv()

    sent = []

    def go(copy):
        copy.start()
        sent.append(copy)

    def w_wave(ch, wave):
        if wave == 0:
            own_w[ch].wait()
            for phase in (1, 2):
                for t in (0, 1):
                    for slot in (0, 1):
                        go(w_copy(ch, t, phase, 0, slot))
        elif wave == 1:
            for t in (0, 1):
                for slot, q in ((0, 1), (1, 2)):
                    w_recv(ch, t, 1, 0, slot)
                    go(w_copy(ch, t, 1, 0, slot + 2))
                    for s in (0, 1):
                        go(w_copy(ch, t, 2, q, s))
        elif wave == 3:
            for t in (0, 1):
                for slot in (2, 3):
                    w_recv(ch, t, 1, 0, slot)
                for s in (0, 1):
                    go(w_copy(ch, t, 2, 3, s))
        else:
            for q in {2: (0,), 4: (1, 2), 5: (3,)}[wave]:
                for t in (0, 1):
                    for slot in (0, 1):
                        w_recv(ch, t, 2, q, slot)
                        go(w_copy(ch, t, 2, q, slot + 2))

    def ring_copy(ref, sem, slot):
        step = 1 if slot % 2 == 0 else -1
        near = y if slot < 2 else (y - step + 4) % 4
        lo, n = ((0, 4), (0, 4), (0, 2), (2, 2))[slot]
        part = ref.at[pl.ds(4 * near + lo, n)]
        return remote(part, part, sem + slot, (dp, peer(step, 0)))

    def ring_recv(ref, sem, slot):
        step = 1 if slot % 2 == 0 else -1
        far = (y - step + 4) % 4 if slot < 2 else (y + 2) % 4
        lo, n = ((0, 4), (0, 4), (0, 2), (2, 2))[slot]
        part = ref.at[pl.ds(4 * far + lo, n)]
        remote(part, part, sem + slot, (dp, peer(step, 0))).wait_recv()

    def ring_send(ref, sem):
        for slot in (0, 1):
            go(ring_copy(ref, sem, slot))

    def ring_forward(ref, sem):
        for slot in (0, 1):
            ring_recv(ref, sem, slot)
            go(ring_copy(ref, sem, slot + 2))

    def ring_finish(ref, sem):
        for slot in (2, 3):
            ring_recv(ref, sem, slot)

    def project(ch, rx):
        @pl.loop(0, 4)
        def _(i):
            d = ((x + rx + 4) % 4) * 4 + i
            rows = hid[:, pl.ds(pl.multiple_of(d * 256, 256), 256)]
            for n in range(2):
                span = slice(n * 256, n * 256 + 256)
                qacc[:, span] += dot(rows, wb[ch][d, :, span])

    def query(ch):
        qacc[...] = jnp.zeros_like(qacc)
        for q, rx in ((0, 0), (1, -1), (2, 1)):
            for slot in (2, 3):
                w_recv(ch, 0, 2, q, slot)
            project(ch, rx)
        for slot in (2, 3):
            w_recv(ch, 0, 2, 3, slot)
            for q in range(4):
                w_recv(ch, 1, 2, q, slot)
        project(ch, 2)
        qg[ch][pl.ds(4 * y, 4)] = qacc[...].astype(BF16).reshape(4, BLOCK, 512)
        ring_send(qg[ch], S_Q + 4 * ch)

    def span256(k):
        return pl.ds(pl.multiple_of(k * 256, 256), 256)

    def feats(k):
        return pl.ds(pl.multiple_of(k * 1024, 1024), 1024)

    def tokens(s):
        return pl.ds(pl.multiple_of(s * 128, 128), 128)

    own_hid_rows = hid.at[tokens(c)]
    hidden_out = []

    def send_hidden():
        for dy in (1, 3, 2):
            to = peer(dy, 0)
            go(remote(own_hid_rows.at[:, feats(to // 2)], hs.at[tokens(seq)], S_HS + dy, (dp, to)))
        hs[span256(y), :] = hid[:, feats(y)]

    def forward_hidden():
        for dy in (1, 3, 2):
            frm = peer(-dy, 0)
            ref = hs.at[tokens(frm)]
            remote(ref, ref, S_HS + dy, (dp, frm)).wait_recv()
            hidden_out.append(remote(ref, ref, S_HF + dy, (dp, sibling)))
            hidden_out[-1].start()

    def slot_of(s, core):
        shard = 2 * y + core
        block, row, other = jnp.int32(0), jnp.int32(0), jnp.int32(0)
        for j in range(4):
            here = ids_s[s, j // 2, j % 2]
            hit = here // 4 == shard
            block = jnp.where(hit, j // 2, block)
            row = jnp.where(hit, here % 4, row)
            other = jnp.where(hit, ids_s[s, j // 2, 1 - j % 2], other)
        return 2 * s + block, 4 * core + row, other

    def diagonal(a, b):
        none = jnp.zeros((BLOCK, HEAD), BF16)
        return jnp.concatenate(
            [jnp.concatenate([a, none], axis=1), jnp.concatenate([none, b], axis=1)], axis=0
        )

    def operands(ch, e, b0, k0, b1, k1):
        lanes = slice(e * HEAD, e * HEAD + HEAD)
        far = slice(ch * 512 + e * HEAD, ch * 512 + e * HEAD + HEAD)
        kk = jnp.concatenate([kc[ch][k0, :, lanes], kc[ch][k1, :, lanes]], axis=1)
        vv = jnp.concatenate([vc[ch][k0, :, lanes], vc[ch][k1, :, lanes]], axis=1)
        qq = diagonal(qg[ch][b0, :, lanes], qg[ch][b1, :, lanes])
        dd = diagonal(gg[b0, :, far], gg[b1, :, far])
        return lanes, kk, vv, qq, dd

    def first_pass(ch):
        @pl.loop(0, 8)
        def _(s):
            b0, k0, _o0 = slot_of(s, 0)
            b1, k1, _o1 = slot_of(s, 1)
            for e in range(4):
                _, kk, vv, qq, dd = operands(ch, e, b0, k0, b1, k1)
                scores = dot(kk, qq, ((1,), (1,))) * SCALE
                d_probs = dot(vv, dd, ((1,), (1,)))
                peak = jnp.max(scores, axis=0, keepdims=True)
                expo = jnp.exp(scores - peak)
                total = jnp.sum(expo, axis=0, keepdims=True)
                st_buf[4 * s + e] = scores
                dp_buf[4 * s + e] = d_probs
                stat[ch][y, s, e:e + 1] = peak + jnp.log(total)
                stat[ch][y, s, 4 + e:5 + e] = jnp.sum(expo * d_probs, axis=0, keepdims=True) / total
        for dy in (1, 3, 2):
            go(remote(stat[ch].at[y], stat[ch].at[y], S_ST + 4 * ch + dy, (dp, peer(dy, 0))))

    def wait_stats(ch):
        for dy in (1, 3, 2):
            frm = peer(-dy, 0)
            ref = stat[ch].at[frm // 2]
            remote(ref, ref, S_ST + 4 * ch + dy, (dp, frm)).wait_recv()

    def second_pass(ch):
        left = lax.broadcasted_iota(jnp.int32, (8, 128), 1) < BLOCK

        @pl.loop(0, 8)
        def _(s):
            b0, k0, o0 = slot_of(s, 0)
            b1, k1, o1 = slot_of(s, 1)
            theirs0 = stat[ch][o0 // 8, s]
            theirs1 = stat[ch][o1 // 8, s]
            turned0 = jnp.concatenate([theirs0[:, BLOCK:], theirs0[:, :BLOCK]], axis=1)
            turned1 = jnp.concatenate([theirs1[:, BLOCK:], theirs1[:, :BLOCK]], axis=1)
            theirs0 = jnp.where((o0 // 4) % 2 == 0, theirs0, turned0)
            theirs1 = jnp.where((o1 // 4) % 2 == 1, theirs1, turned1)
            theirs = jnp.where(left, theirs0, theirs1)
            ours = stat[ch][y, s]
            top = jnp.maximum(ours[:4], theirs[:4])
            whole = top + jnp.log(jnp.exp(ours[:4] - top) + jnp.exp(theirs[:4] - top))
            delta = jnp.exp(ours[:4] - whole) * ours[4:] + jnp.exp(theirs[:4] - whole) * theirs[4:]
            for e in range(4):
                lanes, kk, _, _, _ = operands(ch, e, b0, k0, b1, k1)
                probs = jnp.exp(st_buf[4 * s + e] - whole[e:e + 1])
                low = probs.astype(BF16)
                d_scores = (probs * (dp_buf[4 * s + e] - delta[e:e + 1]) * SCALE).astype(BF16)
                dq = dot(d_scores, kk, ((0,), (0,))).astype(BF16)
                sd[ch][2 * s, :, lanes] = dq[:BLOCK, :HEAD]
                sd[ch][2 * s + 1, :, lanes] = dq[BLOCK:, HEAD:]
                low_buf[4 * s + e] = low
                ds_buf[4 * s + e] = d_scores

    def third_pass(ch):
        @pl.loop(0, 8)
        def _(s):
            b0, k0, _o0 = slot_of(s, 0)
            b1, k1, _o1 = slot_of(s, 1)
            for e in range(4):
                lanes, _, vv, qq, dd = operands(ch, e, b0, k0, b1, k1)
                low, d_scores = low_buf[4 * s + e], ds_buf[4 * s + e]
                att = dot(low, vv, ((0,), (0,))).astype(BF16)
                sa[ch][2 * s, :, lanes] = att[:BLOCK, :HEAD]
                sa[ch][2 * s + 1, :, lanes] = att[BLOCK:, HEAD:]
                dk = dot(d_scores, qq).astype(BF16)
                dv = dot(low, dd).astype(BF16)
                for i in range(2):
                    ck[2 * s + i, :, lanes] = dk[:, i * HEAD:(i + 1) * HEAD]
                    cv[2 * s + i, :, lanes] = dv[:, i * HEAD:(i + 1) * HEAD]

    def give_back(ch, kind):
        src, dst = ((sd, rd), (sa, ra))[kind]
        for dy in (1, 3, 2):
            to = peer(dy, 0)
            go(remote(
                src[ch].at[pl.ds(4 * (to // 2), 4)], dst[ch].at[pl.ds(4 * y, 4)],
                S_RET + 8 * kind + 4 * ch + dy, (dp, to),
            ))
        dst[ch][pl.ds(4 * y, 4)] = src[ch][pl.ds(4 * y, 4)]

    def take_back(ch, kind):
        src, dst = ((sd, rd), (sa, ra))[kind]
        for dy in (1, 3, 2):
            frm = peer(-dy, 0)
            ref = dst[ch].at[pl.ds(4 * (frm // 2), 4)]
            remote(ref, ref, S_RET + 8 * kind + 4 * ch + dy, (dp, frm)).wait_recv()
        for block in range(4):
            core, u = block // 2, block % 2
            total = jnp.zeros((BLOCK, 512), F32)
            for j in range(2):
                name = ids_s[2 * y + core, u, j]
                total += dst[ch][(name // 8) * 4 + core * 2 + (name // 4) % 2].astype(F32)
            if kind == 0:
                dqg[ch][4 * y + block] = total.astype(BF16)
            else:
                att_s[block * BLOCK:(block + 1) * BLOCK, ch * 512:(ch + 1) * 512] = total.astype(BF16)

    def sum_kv(ch):
        @pl.loop(0, 8)
        def _(row):
            at = []
            for s in range(8):
                one = jnp.int32(SLOTS)
                for j in range(4):
                    one = jnp.where(ids_s[s, j // 2, j % 2] == 8 * y + row, 2 * s + row // 4, one)
                at.append(one)
            for src, dst in ((ck, dks), (cv, dvs)):
                for e in range(4):
                    lanes = slice(e * HEAD, e * HEAD + HEAD)
                    total = src[at[0], :, lanes].astype(F32)
                    for s in range(1, 8):
                        total += src[at[s], :, lanes].astype(F32)
                    dst[row, :, ch * 512 + e * HEAD:ch * 512 + (e + 1) * HEAD] = total.astype(BF16)

    def wq_grad(k):
        ch, pair = k // 2, k % 2
        both = dqg[ch][:, :, pair * 256:pair * 256 + 256].reshape(1024, 256)
        for m in range(4):
            hs[m * 256:m * 256 + 256, k * 256:k * 256 + 256] = dot(
                ht[m * 256:m * 256 + 256, :], both
            ).astype(BF16)

    def r1_copy(core, ch, b):
        src = hs.at[pl.ds(core * 512, 512), pl.ds((4 * ch + b) * HEAD, HEAD)]
        slot, part, dest = z, 2 * c + ch, x * 4 + b
        dst = r1.at[slot, part]
        sem = ssem.at[S_R1 + core * 8 + ch * 4 + b]
        own = jnp.logical_and(dest == dp, c == core)
        return src, dst, sem, rsem.at[S_R1 + slot * 4 + part], (dest, y * 2 + core), own

    def r1_start(core, ch, b):
        src, dst, s_sem, r_sem, dest, own = r1_copy(core, ch, b)

        @pl.when(own)
        def _():
            pltpu.make_async_copy(src, dst, s_sem).start()

        @pl.when(jnp.logical_not(own))
        def _():
            pltpu.make_async_remote_copy(
                src_ref=src, dst_ref=dst, send_sem=s_sem, recv_sem=r_sem, device_id=dest, device_id_type=MESH
            ).start()

    def r1_wait(core, ch, b):
        src, dst, s_sem, r_sem, dest, own = r1_copy(core, ch, b)

        @pl.when(own)
        def _():
            pltpu.make_async_copy(src, dst, s_sem).wait()

        @pl.when(jnp.logical_not(own))
        def _():
            pltpu.make_async_remote_copy(
                src_ref=src, dst_ref=dst, send_sem=s_sem, recv_sem=r_sem, device_id=dest, device_id_type=MESH
            ).wait_send()

    def wq_send(k):
        wq_grad(k)
        for b in (2 * (k % 2), 2 * (k % 2) + 1):
            for core in range(2):
                r1_start(core, k // 2, b)

    w_wave(0, 0)
    own_hid.wait()
    go(remote(own_hid_rows, own_hid_rows, S_HID, (dp, sibling)))
    go(remote(grads.at[:, :, wide(1 - c)], gg.at[own_blocks], S_DO, (dp, sibling)))
    for j, (dy, dc) in enumerate(others):
        go(remote(idv, idg.at[seq], S_ID + j, (dp, peer(dy, dc))))
    for i, (src, dst) in enumerate(((keys, kc), (values, vc))):
        for ch in range(2):
            go(remote(src.at[:, :, chunk(1 - c, ch)], dst[ch].at[own_rows], S_KV + 2 * i + ch, (dp, sibling)))
    w_wave(0, 1)
    their_blocks = gg.at[pl.ds(4 * y + 2 * (1 - c), 2)]
    remote(their_blocks, their_blocks, S_DO, (dp, sibling)).wait_recv()
    own_do.wait()
    ring_send(gg, S_GG)
    w_wave(0, 2)
    w_wave(0, 3)
    w_wave(1, 0)
    other_rows = hid.at[tokens(1 - c)]
    remote(other_rows, other_rows, S_HID, (dp, sibling)).wait_recv()
    w_wave(0, 4)
    ring_forward(gg, S_GG)
    w_wave(0, 5)
    for j, (dy, dc) in enumerate(others):
        frm = peer(-dy, -dc + 2)
        remote(idv, idg.at[frm], S_ID + j, (dp, frm)).wait_recv()
    idg[seq] = idv[...]
    to_smem = local(idg, ids_s, 8)
    to_smem.start()
    to_smem.wait()
    query(0)
    w_wave(1, 1)
    w_wave(1, 2)
    ck[SLOTS] = jnp.zeros((NLEN, 512), BF16)
    cv[SLOTS] = jnp.zeros((NLEN, 512), BF16)
    for copy in own_kv:
        copy.wait()
    their_rows = pl.ds(4 * (1 - c), 4)
    for i, dst in enumerate((kc, vc)):
        for ch in range(2):
            ref = dst[ch].at[their_rows]
            remote(ref, ref, S_KV + 2 * i + ch, (dp, sibling)).wait_recv()
    ring_forward(qg[0], S_Q)
    send_hidden()
    w_wave(1, 3)
    w_wave(1, 4)
    ring_finish(gg, S_GG)
    ring_finish(qg[0], S_Q)
    first_pass(0)
    w_wave(1, 5)
    def dh_add(ch, first):
        @pl.loop(0, 16)
        def _(d):
            for core, buf in ((1 - c, dhs), (c, dho)):
                rows = dqg[ch][pl.ds(4 * y + 2 * core, 2)].reshape(128, 512)
                part = dot(rows, wb[ch][d], ((1,), (1,)))
                if first:
                    buf[:, span256(d)] = part
                else:
                    buf[:, span256(d)] += part

    query(1)
    wait_stats(0)
    second_pass(0)
    ring_forward(qg[1], S_Q + 4)
    give_back(0, 0)
    third_pass(0)
    sum_kv(0)
    ring_finish(qg[1], S_Q + 4)
    first_pass(1)
    take_back(0, 0)
    ring_send(dqg[0], S_DQ)
    wait_stats(1)
    second_pass(1)
    give_back(1, 0)
    forward_hidden()
    ring_forward(dqg[0], S_DQ)
    third_pass(1)
    for dy in (1, 3, 2):
        frm = peer(-dy, 1)
        ref = hs.at[tokens(frm)]
        remote(ref, ref, S_HF + dy, (dp, sibling)).wait_recv()

    @pl.loop(0, 4)
    def _(m):
        ht[span256(m), :] = jnp.transpose(hs[:, span256(m)])

    for copy in hidden_out:
        copy.wait_send()
    dh_add(0, True)
    take_back(1, 0)
    ring_send(dqg[1], S_DQ + 4)
    ring_finish(dqg[0], S_DQ)
    wq_send(0)
    ring_forward(dqg[1], S_DQ + 4)
    give_back(0, 1)
    give_back(1, 1)
    wq_send(1)
    sum_kv(1)
    their_kv = []
    for i, (src, dst) in enumerate(((dks, dk_out), (dvs, dv_out))):
        go(remote(src.at[their_rows], dst.at[:, :, wide(c)], S_DKV + i, (dp, sibling)))
        their_kv.append(remote(src.at[their_rows], dst.at[:, :, wide(1 - c)], S_DKV + i, (dp, sibling)))
    own_kv_out = [
        local(src.at[own_rows], dst.at[:, :, wide(c)], 9 + i)
        for i, (src, dst) in enumerate(((dks, dk_out), (dvs, dv_out)))
    ]
    for copy in own_kv_out:
        copy.start()
    ring_finish(dqg[1], S_DQ + 4)
    wq_send(2)
    wq_send(3)
    dh_add(1, False)
    dh_copy = remote(dhs, dhr, S_DH, (dp, sibling))
    go(dh_copy)

    for core in range(2):
        for ch in range(2):
            for b in range(4):
                r1_wait(core, ch, b)

    @pl.loop(0, 16)
    def _(k):
        @pl.when(jnp.logical_not(jnp.logical_and(k // 4 == z, (k % 4) // 2 == c)))
        def _():
            ref = r1.at[k // 4, k % 4]
            pltpu.make_async_remote_copy(
                src_ref=ref, dst_ref=ref, send_sem=ssem.at[S_R1], recv_sem=rsem.at[S_R1 + k],
                device_id=(dp, sibling), device_id_type=MESH,
            ).wait_recv()

    def r2_copy(step):
        to = (x + step) % 4
        return remote(r1s.at[to], r2.at[step], S_R2 + step, (to * 4 + z, seq))

    for step in (1, 3, 2, 0):
        to = (x + step) % 4
        total = r1[0, to].astype(F32)
        for k in range(1, 4):
            total += r1[k, to].astype(F32)
        if step:
            r1s[to] = total.astype(BF16)
            go(r2_copy(step))
        else:
            dwq_out[...] = total
    dh_copy.wait_recv()
    dh_out[...] = (dho[...] + dhr[...]).astype(BF16)
    for step in (1, 3, 2):
        r2_copy(step).wait_recv()
        dwq_out[...] += r2[step].astype(F32)
    for ch in range(2):
        take_back(ch, 1)
    own_att = local(att_s.at[tokens(c)], att_out.at[:, wide(c)], 11)
    own_att.start()
    go(remote(att_s.at[tokens(1 - c)], att_out.at[:, wide(c)], S_ATT, (dp, sibling)))

    own_att.wait()
    remote(att_s.at[tokens(1 - c)], att_out.at[:, wide(1 - c)], S_ATT, (dp, sibling)).wait_recv()
    for copy in own_kv_out:
        copy.wait()
    for copy in their_kv:
        copy.wait_recv()
    for copy in sent:
        copy.wait_send()


FINISH_PARTS = 4


def finish(
    att_in, dh_in, dwq_in, dk_in, dv_in, att_out, dh_out, dwq_out, dk_out, dv_out,
    att, dh, dwq, dk, dv, dk_wide, dv_wide, in_sem, out_sem,
):
    rows = 512 // FINISH_PARTS
    loads, stores = [], []
    for k in range(FINISH_PARTS):
        span = pl.ds(k * rows, rows)
        for t, (src, dst) in enumerate(((dk_in, dk), (dv_in, dv))):
            loads.append(pltpu.make_async_copy(src.at[span], dst.at[span], in_sem.at[2 * k + t]))
    small = ((att_in, att, att_out), (dh_in, dh, dh_out), (dwq_in, dwq, dwq_out))
    for t, (src, mid, _) in enumerate(small):
        loads.append(pltpu.make_async_copy(src, mid, in_sem.at[2 * FINISH_PARTS + t]))
    for load in loads:
        load.start()
    for k in range(FINISH_PARTS):
        span = pl.ds(k * rows, rows)
        for t, (narrow, wide, dst) in enumerate(((dk, dk_wide, dk_out), (dv, dv_wide, dv_out))):
            loads[2 * k + t].wait()
            wide[span, :] = narrow[span, :].astype(F32)
            stores.append(pltpu.make_async_copy(wide.at[span], dst.at[span], out_sem.at[2 * k + t]))
            stores[-1].start()
    for t, (_, mid, dst) in enumerate(small):
        loads[2 * FINISH_PARTS + t].wait()
        stores.append(pltpu.make_async_copy(mid, dst, out_sem.at[2 * FINISH_PARTS + t]))
        stores[-1].start()
    for store in stores:
        store.wait()


def on_device(hidden, w_query, nbr_keys, nbr_values, nbr_ids, d_attended):
    vmem = pltpu.VMEM
    anywhere = pl.BlockSpec(memory_space=pl.ANY)
    in_vmem = pl.BlockSpec(memory_space=pltpu.VMEM)
    attended, d_hidden, d_wq, d_keys, d_values = pl.pallas_call(
        kernel,
        out_shape=(
            jax.ShapeDtypeStruct((128, 2048), BF16),
            jax.ShapeDtypeStruct((128, 4096), BF16),
            jax.ShapeDtypeStruct((512, 128), F32),
            jax.ShapeDtypeStruct((4, 128, 2048), BF16),
            jax.ShapeDtypeStruct((4, 128, 2048), BF16),
        ),
        in_specs=[anywhere, anywhere, anywhere, anywhere, in_vmem, anywhere],
        out_specs=(anywhere, in_vmem, in_vmem, anywhere, anywhere),
        scratch_shapes=[
            vmem((256, 4096), BF16),
            *[vmem((16, 256, 512), BF16)] * 2,
            *[vmem((8, 128, 512), BF16)] * 4,
            vmem((16, 64, 1024), BF16),
            *[vmem((16, 64, 512), BF16)] * 2,
            vmem((256, 512), F32),
            vmem((1024, 1024), BF16),
            vmem((1024, 1024), BF16),
            vmem((32, 128, 128), F32),
            vmem((32, 128, 128), F32),
            vmem((32, 128, 128), BF16),
            vmem((32, 128, 128), BF16),
            *[vmem((4, 8, 8, 128), F32)] * 2,
            *[vmem((SLOTS, 64, 512), BF16)] * 8,
            *[vmem((SLOTS + 1, 128, 512), BF16)] * 2,
            *[vmem((8, 128, 1024), BF16)] * 2,
            vmem((256, 1024), BF16),
            *[vmem((16, 64, 512), BF16)] * 2,
            vmem((4, 4, 512, 128), BF16),
            vmem((4, 512, 128), BF16),
            vmem((4, 512, 128), BF16),
            vmem((128, 4096), F32),
            vmem((128, 4096), F32),
            vmem((128, 4096), F32),
            vmem((8, 128), jnp.int32),
            vmem((8, 8, 128), jnp.int32),
            pltpu.SMEM((8, 8, 128), jnp.int32),
            pltpu.SemaphoreType.DMA((N_SEMS,)),
            pltpu.SemaphoreType.DMA((N_SEMS,)),
        ],
        compiler_params=pltpu.CompilerParams(
            collective_id=0, has_side_effects=True, vmem_limit_bytes=62 * 2**20
        ),
        name="group_attention",
    )(hidden, w_query, nbr_keys, nbr_values, nbr_ids, d_attended.reshape(2, 64, 2048))
    parts = (attended, d_hidden, d_wq, d_keys.reshape(512, 2048), d_values.reshape(512, 2048))
    kinds = (BF16, BF16, F32, F32, F32)
    attended, d_hidden, d_wq, d_keys, d_values = pl.pallas_call(
        finish,
        out_shape=[jax.ShapeDtypeStruct(p.shape, kind) for p, kind in zip(parts, kinds)],
        in_specs=[anywhere] * 5,
        out_specs=[anywhere] * 5,
        scratch_shapes=[
            *[vmem(p.shape, p.dtype) for p in parts],
            *[vmem((512, 2048), F32)] * 2,
            *[pltpu.SemaphoreType.DMA((2 * FINISH_PARTS + 3,))] * 2,
        ],
        compiler_params=pltpu.CompilerParams(vmem_limit_bytes=60 * 2**20),
        name="finish",
    )(*parts)
    return attended, d_hidden, d_wq, d_keys.reshape(4, 128, 2048), d_values.reshape(4, 128, 2048)


def solution(mesh):
    placed = (
        P(("dp", "seq"), None),
        P("dp", None),
        P(("dp", "seq"), None, None),
        P(("dp", "seq"), None, None),
        P(("dp", "seq"), None),
        P(("dp", "seq"), None),
    )
    return jax.shard_map(
        on_device,
        mesh=mesh,
        in_specs=placed,
        out_specs=(
            P(("dp", "seq"), None),
            P(("dp", "seq"), None),
            P("seq", "dp"),
            P(("dp", "seq"), None, None),
            P(("dp", "seq"), None, None),
        ),
        check_vma=False,
    )
```

```python
import functools

import jax
import jax.numpy as jnp
from jax import lax
from jax.experimental import pallas as pl
from jax.experimental.pallas import tpu as pltpu
from jax.sharding import PartitionSpec as P

BF16 = jnp.bfloat16
F32 = jnp.float32
MESH = pl.DeviceIdType.MESH
HEAD = 128
SCALE = HEAD ** (-0.5)
BLOCK = 64
NLEN = 128


class Pool:
    def __init__(self):
        self.used = 0

    def take(self, count):
        first = self.used
        self.used += count
        return first


POOL = Pool()
S_W = POOL.take(80)
S_KV = POOL.take(4)
S_DO = POOL.take(1)
S_GG = POOL.take(4)
S_ID = POOL.take(8)
S_HID = POOL.take(1)
S_Q = POOL.take(8)
S_HS = POOL.take(4)
S_HF = POOL.take(4)
S_ST = POOL.take(8)
S_RET = POOL.take(16)
S_DQ = POOL.take(8)
S_DKV = POOL.take(2)
S_ATT = POOL.take(1)
S_DH = POOL.take(1)
S_R1 = POOL.take(16)
S_R2 = POOL.take(4)
S_LOCAL = POOL.take(16)
N_SEMS = POOL.used
SLOTS = 16


def dot(a, b, dims=((1,), (0,))):
    return lax.dot_general(a, b, (dims, ((), ())), preferred_element_type=F32)


def kernel(
    hidden, weight, keys, values, ids, grads,
    att_out, dh_out, dwq_out, dk_out, dv_out,
    hid, wb0, wb1, kc0, kc1, vc0, vc1, gg, qg0, qg1, qacc, hs, ht, st_buf, dp_buf, low_buf, ds_buf, stat0, stat1,
    sa0, sa1, sd0, sd1, ra0, ra1, rd0, rd1, ck, cv, dks, dvs, att_s, dqg0, dqg1,
    r1, r1s, r2, dhs, dho, dhr, dh_s, dwq_s, idv, idg, ids_s, ssem, rsem,
):
    dp = lax.axis_index("dp")
    seq = lax.axis_index("seq")
    x, z = dp // 4, dp % 4
    y, c = seq // 2, seq % 2
    wb, kc, vc, qg, stat = (wb0, wb1), (kc0, kc1), (vc0, vc1), (qg0, qg1), (stat0, stat1)
    sa, sd, ra, rd, dqg = (sa0, sa1), (sd0, sd1), (ra0, ra1), (rd0, rd1), (dqg0, dqg1)

    def remote(src, dst, sem, to):
        return pltpu.make_async_remote_copy(
            src_ref=src, dst_ref=dst, send_sem=ssem.at[sem], recv_sem=rsem.at[sem],
            device_id=to, device_id_type=MESH,
        )

    def local(src, dst, sem):
        return pltpu.make_async_copy(src, dst, ssem.at[S_LOCAL + sem])

    def peer(dy, dc):
        return ((y + dy + 4) % 4) * 2 + (c + dc) % 2

    def wide(core):
        return pl.ds(pl.multiple_of(core * 1024, 1024), 1024)

    def chunk(core, ch):
        return pl.ds(pl.multiple_of(core * 1024 + ch * 512, 512), 512)

    sibling = peer(0, 1)
    others = [(dy, dc) for dy in (1, 3, 2, 0) for dc in (0, 1) if (dy, dc) != (0, 0)]

    idv[...] = jnp.zeros_like(idv)
    idv[0:2, 0:2] = ids[...]

    own_w = [local(weight.at[:, chunk(c, ch)], wb[ch].at[dp], ch) for ch in range(2)]
    own_hid = local(hidden, hid.at[pl.ds(pl.multiple_of(c * 128, 128), 128)], 2)
    own_blocks = pl.ds(4 * y + 2 * c, 2)
    own_do = local(grads.at[:, :, wide(c)], gg.at[own_blocks], 3)
    own_rows = pl.ds(4 * c, 4)
    own_kv = [
        local(src.at[:, :, chunk(c, ch)], dst[ch].at[own_rows], 4 + 2 * i + ch)
        for i, (src, dst) in enumerate(((keys, kc), (values, vc))) for ch in range(2)
    ]
    for copy in own_w + [own_hid, own_do] + own_kv:
        copy.start()

    barrier = pltpu.get_barrier_semaphore()

    def greet(to):
        pl.semaphore_signal(barrier, inc=1, device_id=to, device_id_type=MESH)

    for dy, dc in others:
        greet((dp, peer(dy, dc)))
    for step in (1, 2, 3):
        for core in (0, 1):
            greet((((x + step) % 4) * 4 + z, y * 2 + core))
            greet((x * 4 + (z + step) % 4, y * 2 + core))
    pl.semaphore_wait(barrier, 7 + 12)

    def moved(axis, step):
        if axis == 0:
            return (((x + step + 4) % 4) * 4 + z, seq)
        return (x * 4 + (z + step + 4) % 4, seq)

    def source(t, r1_, r2_):
        rx, rz = (r1_, r2_) if t == 0 else (r2_, r1_)
        return ((x + rx + 4) % 4) * 4 + (z + rz + 4) % 4

    LINE = (0, -1, 1, 2)
    PART = {"all": (0, 128), "lo": (0, 64), "hi": (64, 64)}

    def piece(ch, t, r1_, r2_, part):
        lo, n = PART[part]
        return wb[ch].at[source(t, r1_, r2_), pl.ds(t * 128 + lo, n)]

    def w_parts(ch, t, phase, q, slot):
        axis = t if phase == 1 else 1 - t
        sem = S_W + 40 * ch + 20 * t + (slot if phase == 1 else 4 + 4 * q + slot)
        step = 1 if slot % 2 == 0 else -1
        return axis, sem, step, "all" if slot < 2 else ("lo" if slot == 2 else "hi")

    def w_copy(ch, t, phase, q, slot):
        axis, sem, step, part = w_parts(ch, t, phase, q, slot)
        near = 0 if slot < 2 else -step
        src = piece(ch, t, near, 0, part) if phase == 1 else piece(ch, t, LINE[q], near, part)
        return remote(src, src, sem, moved(axis, step))

    def w_recv(ch, t, phase, q, slot):
        axis, sem, step, part = w_parts(ch, t, phase, q, slot)
        far = -step if slot < 2 else 2
        dst = piece(ch, t, far, 0, part) if phase == 1 else piece(ch, t, LINE[q], far, part)
        remote(dst, dst, sem, moved(axis, step)).wait_recv()

    sent = []

    def go(copy):
        copy.start()
        sent.append(copy)

    def w_wave(ch, wave):
        if wave == 0:
            own_w[ch].wait()
            for phase in (1, 2):
                for t in (0, 1):
                    for slot in (0, 1):
                        go(w_copy(ch, t, phase, 0, slot))
        elif wave == 1:
            for t in (0, 1):
                for slot, q in ((0, 1), (1, 2)):
                    w_recv(ch, t, 1, 0, slot)
                    go(w_copy(ch, t, 1, 0, slot + 2))
                    for s in (0, 1):
                        go(w_copy(ch, t, 2, q, s))
        elif wave == 3:
            for t in (0, 1):
                for slot in (2, 3):
                    w_recv(ch, t, 1, 0, slot)
                for s in (0, 1):
                    go(w_copy(ch, t, 2, 3, s))
        else:
            for q in {2: (0,), 4: (1, 2), 5: (3,)}[wave]:
                for t in (0, 1):
                    for slot in (0, 1):
                        w_recv(ch, t, 2, q, slot)
                        go(w_copy(ch, t, 2, q, slot + 2))

    def ring_copy(ref, sem, slot):
        step = 1 if slot % 2 == 0 else -1
        near = y if slot < 2 else (y - step + 4) % 4
        lo, n = ((0, 4), (0, 4), (0, 2), (2, 2))[slot]
        part = ref.at[pl.ds(4 * near + lo, n)]
        return remote(part, part, sem + slot, (dp, peer(step, 0)))

    def ring_recv(ref, sem, slot):
        step = 1 if slot % 2 == 0 else -1
        far = (y - step + 4) % 4 if slot < 2 else (y + 2) % 4
        lo, n = ((0, 4), (0, 4), (0, 2), (2, 2))[slot]
        part = ref.at[pl.ds(4 * far + lo, n)]
        remote(part, part, sem + slot, (dp, peer(step, 0))).wait_recv()

    def ring_send(ref, sem):
        for slot in (0, 1):
            go(ring_copy(ref, sem, slot))

    def ring_forward(ref, sem):
        for slot in (0, 1):
            ring_recv(ref, sem, slot)
            go(ring_copy(ref, sem, slot + 2))

    def ring_finish(ref, sem):
        for slot in (2, 3):
            ring_recv(ref, sem, slot)

    def project(ch, rx):
        @pl.loop(0, 4)
        def _(i):
            d = ((x + rx + 4) % 4) * 4 + i
            rows = hid[:, pl.ds(pl.multiple_of(d * 256, 256), 256)]
            for n in range(2):
                span = slice(n * 256, n * 256 + 256)
                qacc[:, span] += dot(rows, wb[ch][d, :, span])

    def query(ch):
        qacc[...] = jnp.zeros_like(qacc)
        for q, rx in ((0, 0), (1, -1), (2, 1)):
            for slot in (2, 3):
                w_recv(ch, 0, 2, q, slot)
            project(ch, rx)
        for slot in (2, 3):
            w_recv(ch, 0, 2, 3, slot)
            for q in range(4):
                w_recv(ch, 1, 2, q, slot)
        project(ch, 2)
        qg[ch][pl.ds(4 * y, 4)] = qacc[...].astype(BF16).reshape(4, BLOCK, 512)
        ring_send(qg[ch], S_Q + 4 * ch)

    def span256(k):
        return pl.ds(pl.multiple_of(k * 256, 256), 256)

    def feats(k):
        return pl.ds(pl.multiple_of(k * 1024, 1024), 1024)

    def tokens(s):
        return pl.ds(pl.multiple_of(s * 128, 128), 128)

    own_hid_rows = hid.at[tokens(c)]
    hidden_out = []

    def send_hidden():
        for dy in (1, 3, 2):
            to = peer(dy, 0)
            go(remote(own_hid_rows.at[:, feats(to // 2)], hs.at[tokens(seq)], S_HS + dy, (dp, to)))
        hs[span256(y), :] = hid[:, feats(y)]

    def forward_hidden():
        for dy in (1, 3, 2):
            frm = peer(-dy, 0)
            ref = hs.at[tokens(frm)]
            remote(ref, ref, S_HS + dy, (dp, frm)).wait_recv()
            hidden_out.append(remote(ref, ref, S_HF + dy, (dp, sibling)))
            hidden_out[-1].start()

    def slot_of(s, core):
        shard = 2 * y + core
        block, row, other = jnp.int32(0), jnp.int32(0), jnp.int32(0)
        for j in range(4):
            here = ids_s[s, j // 2, j % 2]
            hit = here // 4 == shard
            block = jnp.where(hit, j // 2, block)
            row = jnp.where(hit, here % 4, row)
            other = jnp.where(hit, ids_s[s, j // 2, 1 - j % 2], other)
        return 2 * s + block, 4 * core + row, other

    def diagonal(a, b):
        none = jnp.zeros((BLOCK, HEAD), BF16)
        return jnp.concatenate(
            [jnp.concatenate([a, none], axis=1), jnp.concatenate([none, b], axis=1)], axis=0
        )

    def operands(ch, e, b0, k0, b1, k1):
        lanes = slice(e * HEAD, e * HEAD + HEAD)
        far = slice(ch * 512 + e * HEAD, ch * 512 + e * HEAD + HEAD)
        kk = jnp.concatenate([kc[ch][k0, :, lanes], kc[ch][k1, :, lanes]], axis=1)
        vv = jnp.concatenate([vc[ch][k0, :, lanes], vc[ch][k1, :, lanes]], axis=1)
        qq = diagonal(qg[ch][b0, :, lanes], qg[ch][b1, :, lanes])
        dd = diagonal(gg[b0, :, far], gg[b1, :, far])
        return lanes, kk, vv, qq, dd

    def first_pass(ch):
        @pl.loop(0, 8)
        def _(s):
            b0, k0, _o0 = slot_of(s, 0)
            b1, k1, _o1 = slot_of(s, 1)
            for e in range(4):
                _, kk, vv, qq, dd = operands(ch, e, b0, k0, b1, k1)
                scores = dot(kk, qq, ((1,), (1,))) * SCALE
                d_probs = dot(vv, dd, ((1,), (1,)))
                peak = jnp.max(scores, axis=0, keepdims=True)
                expo = jnp.exp(scores - peak)
                total = jnp.sum(expo, axis=0, keepdims=True)
                st_buf[4 * s + e] = scores
                dp_buf[4 * s + e] = d_probs
                stat[ch][y, s, e:e + 1] = peak + jnp.log(total)
                stat[ch][y, s, 4 + e:5 + e] = jnp.sum(expo * d_probs, axis=0, keepdims=True) / total
        for dy in (1, 3, 2):
            go(remote(stat[ch].at[y], stat[ch].at[y], S_ST + 4 * ch + dy, (dp, peer(dy, 0))))

    def wait_stats(ch):
        for dy in (1, 3, 2):
            frm = peer(-dy, 0)
            ref = stat[ch].at[frm // 2]
            remote(ref, ref, S_ST + 4 * ch + dy, (dp, frm)).wait_recv()

    def second_pass(ch):
        left = lax.broadcasted_iota(jnp.int32, (8, 128), 1) < BLOCK

        @pl.loop(0, 8)
        def _(s):
            b0, k0, o0 = slot_of(s, 0)
            b1, k1, o1 = slot_of(s, 1)
            theirs0 = stat[ch][o0 // 8, s]
            theirs1 = stat[ch][o1 // 8, s]
            turned0 = jnp.concatenate([theirs0[:, BLOCK:], theirs0[:, :BLOCK]], axis=1)
            turned1 = jnp.concatenate([theirs1[:, BLOCK:], theirs1[:, :BLOCK]], axis=1)
            theirs0 = jnp.where((o0 // 4) % 2 == 0, theirs0, turned0)
            theirs1 = jnp.where((o1 // 4) % 2 == 1, theirs1, turned1)
            theirs = jnp.where(left, theirs0, theirs1)
            ours = stat[ch][y, s]
            top = jnp.maximum(ours[:4], theirs[:4])
            whole = top + jnp.log(jnp.exp(ours[:4] - top) + jnp.exp(theirs[:4] - top))
            delta = jnp.exp(ours[:4] - whole) * ours[4:] + jnp.exp(theirs[:4] - whole) * theirs[4:]
            for e in range(4):
                lanes, kk, _, _, _ = operands(ch, e, b0, k0, b1, k1)
                probs = jnp.exp(st_buf[4 * s + e] - whole[e:e + 1])
                low = probs.astype(BF16)
                d_scores = (probs * (dp_buf[4 * s + e] - delta[e:e + 1]) * SCALE).astype(BF16)
                dq = dot(d_scores, kk, ((0,), (0,))).astype(BF16)
                sd[ch][2 * s, :, lanes] = dq[:BLOCK, :HEAD]
                sd[ch][2 * s + 1, :, lanes] = dq[BLOCK:, HEAD:]
                low_buf[4 * s + e] = low
                ds_buf[4 * s + e] = d_scores

    def third_pass(ch):
        @pl.loop(0, 8)
        def _(s):
            b0, k0, _o0 = slot_of(s, 0)
            b1, k1, _o1 = slot_of(s, 1)
            for e in range(4):
                lanes, _, vv, qq, dd = operands(ch, e, b0, k0, b1, k1)
                low, d_scores = low_buf[4 * s + e], ds_buf[4 * s + e]
                att = dot(low, vv, ((0,), (0,))).astype(BF16)
                sa[ch][2 * s, :, lanes] = att[:BLOCK, :HEAD]
                sa[ch][2 * s + 1, :, lanes] = att[BLOCK:, HEAD:]
                dk = dot(d_scores, qq).astype(BF16)
                dv = dot(low, dd).astype(BF16)
                for i in range(2):
                    ck[2 * s + i, :, lanes] = dk[:, i * HEAD:(i + 1) * HEAD]
                    cv[2 * s + i, :, lanes] = dv[:, i * HEAD:(i + 1) * HEAD]

    def give_back(ch, kind):
        src, dst = ((sd, rd), (sa, ra))[kind]
        for dy in (1, 3, 2) if kind == 0 else (2, 1, 3):
            to = peer(dy, 0)
            go(remote(
                src[ch].at[pl.ds(4 * (to // 2), 4)], dst[ch].at[pl.ds(4 * y, 4)],
                S_RET + 8 * kind + 4 * ch + dy, (dp, to),
            ))
        dst[ch][pl.ds(4 * y, 4)] = src[ch][pl.ds(4 * y, 4)]

    def take_back(ch, kind):
        src, dst = ((sd, rd), (sa, ra))[kind]
        for dy in (1, 3, 2):
            frm = peer(-dy, 0)
            ref = dst[ch].at[pl.ds(4 * (frm // 2), 4)]
            remote(ref, ref, S_RET + 8 * kind + 4 * ch + dy, (dp, frm)).wait_recv()
        for block in range(4):
            core, u = block // 2, block % 2
            total = jnp.zeros((BLOCK, 512), F32)
            for j in range(2):
                name = ids_s[2 * y + core, u, j]
                total += dst[ch][(name // 8) * 4 + core * 2 + (name // 4) % 2].astype(F32)
            if kind == 0:
                dqg[ch][4 * y + block] = total.astype(BF16)
            else:
                att_s[block * BLOCK:(block + 1) * BLOCK, ch * 512:(ch + 1) * 512] = total.astype(BF16)

    def sum_kv(ch):
        @pl.loop(0, 8)
        def _(row):
            at = []
            for s in range(8):
                one = jnp.int32(SLOTS)
                for j in range(4):
                    one = jnp.where(ids_s[s, j // 2, j % 2] == 8 * y + row, 2 * s + row // 4, one)
                at.append(one)
            for src, dst in ((ck, dks), (cv, dvs)):
                for e in range(4):
                    lanes = slice(e * HEAD, e * HEAD + HEAD)
                    total = src[at[0], :, lanes].astype(F32)
                    for s in range(1, 8):
                        total += src[at[s], :, lanes].astype(F32)
                    dst[row, :, ch * 512 + e * HEAD:ch * 512 + (e + 1) * HEAD] = total.astype(BF16)

    def wq_grad(k):
        ch, pair = k // 2, k % 2
        both = dqg[ch][:, :, pair * 256:pair * 256 + 256].reshape(1024, 256)
        for m in range(4):
            hs[m * 256:m * 256 + 256, k * 256:k * 256 + 256] = dot(
                ht[m * 256:m * 256 + 256, :], both
            ).astype(BF16)

    def r1_copy(core, ch, b):
        src = hs.at[pl.ds(core * 512, 512), pl.ds((4 * ch + b) * HEAD, HEAD)]
        slot, part, dest = z, 2 * c + ch, x * 4 + b
        dst = r1.at[slot, part]
        sem = ssem.at[S_R1 + core * 8 + ch * 4 + b]
        own = jnp.logical_and(dest == dp, c == core)
        return src, dst, sem, rsem.at[S_R1 + slot * 4 + part], (dest, y * 2 + core), own

    def r1_start(core, ch, b):
        src, dst, s_sem, r_sem, dest, own = r1_copy(core, ch, b)

        @pl.when(own)
        def _():
            pltpu.make_async_copy(src, dst, s_sem).start()

        @pl.when(jnp.logical_not(own))
        def _():
            pltpu.make_async_remote_copy(
                src_ref=src, dst_ref=dst, send_sem=s_sem, recv_sem=r_sem, device_id=dest, device_id_type=MESH
            ).start()

    def r1_wait(core, ch, b):
        src, dst, s_sem, r_sem, dest, own = r1_copy(core, ch, b)

        @pl.when(own)
        def _():
            pltpu.make_async_copy(src, dst, s_sem).wait()

        @pl.when(jnp.logical_not(own))
        def _():
            pltpu.make_async_remote_copy(
                src_ref=src, dst_ref=dst, send_sem=s_sem, recv_sem=r_sem, device_id=dest, device_id_type=MESH
            ).wait_send()

    def wq_send(k):
        wq_grad(k)
        for b in (2 * (k % 2), 2 * (k % 2) + 1):
            for core in range(2):
                r1_start(core, k // 2, b)

    w_wave(0, 0)
    own_hid.wait()
    go(remote(own_hid_rows, own_hid_rows, S_HID, (dp, sibling)))
    go(remote(grads.at[:, :, wide(1 - c)], gg.at[own_blocks], S_DO, (dp, sibling)))
    for j, (dy, dc) in enumerate(others):
        go(remote(idv, idg.at[seq], S_ID + j, (dp, peer(dy, dc))))
    for i, (src, dst) in enumerate(((keys, kc), (values, vc))):
        for ch in range(2):
            go(remote(src.at[:, :, chunk(1 - c, ch)], dst[ch].at[own_rows], S_KV + 2 * i + ch, (dp, sibling)))
    w_wave(0, 1)
    their_blocks = gg.at[pl.ds(4 * y + 2 * (1 - c), 2)]
    remote(their_blocks, their_blocks, S_DO, (dp, sibling)).wait_recv()
    own_do.wait()
    ring_send(gg, S_GG)
    w_wave(0, 2)
    w_wave(0, 3)
    w_wave(1, 0)
    other_rows = hid.at[tokens(1 - c)]
    remote(other_rows, other_rows, S_HID, (dp, sibling)).wait_recv()
    w_wave(0, 4)
    ring_forward(gg, S_GG)
    w_wave(0, 5)
    for j, (dy, dc) in enumerate(others):
        frm = peer(-dy, -dc + 2)
        remote(idv, idg.at[frm], S_ID + j, (dp, frm)).wait_recv()
    idg[seq] = idv[...]
    to_smem = local(idg, ids_s, 8)
    to_smem.start()
    to_smem.wait()
    query(0)
    w_wave(1, 1)
    w_wave(1, 2)
    ck[SLOTS] = jnp.zeros((NLEN, 512), BF16)
    cv[SLOTS] = jnp.zeros((NLEN, 512), BF16)
    for copy in own_kv:
        copy.wait()
    their_rows = pl.ds(4 * (1 - c), 4)
    for i, dst in enumerate((kc, vc)):
        for ch in range(2):
            ref = dst[ch].at[their_rows]
            remote(ref, ref, S_KV + 2 * i + ch, (dp, sibling)).wait_recv()
    ring_forward(qg[0], S_Q)
    send_hidden()
    w_wave(1, 3)
    w_wave(1, 4)
    ring_finish(gg, S_GG)
    ring_finish(qg[0], S_Q)
    first_pass(0)
    w_wave(1, 5)
    def dh_add(ch, first):
        @pl.loop(0, 16)
        def _(d):
            for core, buf in ((1 - c, dhs), (c, dho)):
                rows = dqg[ch][pl.ds(4 * y + 2 * core, 2)].reshape(128, 512)
                part = dot(rows, wb[ch][d], ((1,), (1,)))
                if first:
                    buf[:, span256(d)] = part
                else:
                    buf[:, span256(d)] += part

    query(1)
    wait_stats(0)
    second_pass(0)
    ring_forward(qg[1], S_Q + 4)
    give_back(0, 0)
    third_pass(0)
    sum_kv(0)
    ring_finish(qg[1], S_Q + 4)
    first_pass(1)
    take_back(0, 0)
    ring_send(dqg[0], S_DQ)
    wait_stats(1)
    second_pass(1)
    give_back(1, 0)
    forward_hidden()
    ring_forward(dqg[0], S_DQ)
    third_pass(1)
    for dy in (1, 3, 2):
        frm = peer(-dy, 1)
        ref = hs.at[tokens(frm)]
        remote(ref, ref, S_HF + dy, (dp, sibling)).wait_recv()

    @pl.loop(0, 4)
    def _(m):
        ht[span256(m), :] = jnp.transpose(hs[:, span256(m)])

    for copy in hidden_out:
        copy.wait_send()
    dh_add(0, True)
    take_back(1, 0)
    ring_send(dqg[1], S_DQ + 4)
    ring_finish(dqg[0], S_DQ)
    wq_send(0)
    ring_forward(dqg[1], S_DQ + 4)
    give_back(0, 1)
    give_back(1, 1)
    wq_send(1)
    sum_kv(1)
    their_kv = []
    for i, (src, dst) in enumerate(((dks, dk_out), (dvs, dv_out))):
        go(remote(src.at[their_rows], dst.at[:, :, wide(c)], S_DKV + i, (dp, sibling)))
        their_kv.append(remote(src.at[their_rows], dst.at[:, :, wide(1 - c)], S_DKV + i, (dp, sibling)))
    own_kv_out = [
        local(src.at[own_rows], dst.at[:, :, wide(c)], 9 + i)
        for i, (src, dst) in enumerate(((dks, dk_out), (dvs, dv_out)))
    ]
    for copy in own_kv_out:
        copy.start()
    ring_finish(dqg[1], S_DQ + 4)
    wq_send(2)
    wq_send(3)
    dh_add(1, False)
    dh_copy = remote(dhs, dhr, S_DH, (dp, sibling))
    go(dh_copy)

    for core in range(2):
        for ch in range(2):
            for b in range(4):
                r1_wait(core, ch, b)

    @pl.loop(0, 16)
    def _(k):
        @pl.when(jnp.logical_not(jnp.logical_and(k // 4 == z, (k % 4) // 2 == c)))
        def _():
            ref = r1.at[k // 4, k % 4]
            pltpu.make_async_remote_copy(
                src_ref=ref, dst_ref=ref, send_sem=ssem.at[S_R1], recv_sem=rsem.at[S_R1 + k],
                device_id=(dp, sibling), device_id_type=MESH,
            ).wait_recv()

    def r2_copy(step):
        to = (x + step) % 4
        return remote(r1s.at[to], r2.at[step], S_R2 + step, (to * 4 + z, seq))

    for step in (1, 3, 2, 0):
        to = (x + step) % 4
        total = r1[0, to].astype(F32)
        for k in range(1, 4):
            total += r1[k, to].astype(F32)
        if step:
            r1s[to] = total.astype(BF16)
            go(r2_copy(step))
        else:
            dwq_s[...] = total
    take_back(0, 1)
    dh_copy.wait_recv()
    dh_s[...] = (dho[...] + dhr[...]).astype(BF16)
    late_out = [local(dh_s, dh_out, 12), local(dwq_s, dwq_out, 13)]
    late_out[0].start()
    for step in (1, 3, 2):
        r2_copy(step).wait_recv()
        dwq_s[...] += r2[step].astype(F32)
    late_out[1].start()
    take_back(1, 1)
    own_att = local(att_s.at[tokens(c)], att_out.at[:, wide(c)], 11)
    own_att.start()
    go(remote(att_s.at[tokens(1 - c)], att_out.at[:, wide(c)], S_ATT, (dp, sibling)))

    own_att.wait()
    for copy in late_out:
        copy.wait()
    remote(att_s.at[tokens(1 - c)], att_out.at[:, wide(1 - c)], S_ATT, (dp, sibling)).wait_recv()
    for copy in own_kv_out:
        copy.wait()
    for copy in their_kv:
        copy.wait_recv()
    for copy in sent:
        copy.wait_send()


FINISH_PARTS = 4


def finish(
    att_in, dh_in, dwq_in, dk_in, dv_in, att_out, dh_out, dwq_out, dk_out, dv_out,
    att, dh, dwq, dk, dv, dk_wide, dv_wide, in_sem, out_sem,
):
    rows = 512 // FINISH_PARTS
    loads, stores = [], []
    for k in range(FINISH_PARTS):
        span = pl.ds(k * rows, rows)
        for t, (src, dst) in enumerate(((dk_in, dk), (dv_in, dv))):
            loads.append(pltpu.make_async_copy(src.at[span], dst.at[span], in_sem.at[2 * k + t]))
    small = ((att_in, att, att_out), (dh_in, dh, dh_out), (dwq_in, dwq, dwq_out))
    for t, (src, mid, _) in enumerate(small):
        loads.append(pltpu.make_async_copy(src, mid, in_sem.at[2 * FINISH_PARTS + t]))
    for load in loads:
        load.start()
    for k in range(FINISH_PARTS):
        span = pl.ds(k * rows, rows)
        for t, (narrow, wide, dst) in enumerate(((dk, dk_wide, dk_out), (dv, dv_wide, dv_out))):
            loads[2 * k + t].wait()
            wide[span, :] = narrow[span, :].astype(F32)
            stores.append(pltpu.make_async_copy(wide.at[span], dst.at[span], out_sem.at[2 * k + t]))
            stores[-1].start()
    for t, (_, mid, dst) in enumerate(small):
        loads[2 * FINISH_PARTS + t].wait()
        stores.append(pltpu.make_async_copy(mid, dst, out_sem.at[2 * FINISH_PARTS + t]))
        stores[-1].start()
    for store in stores:
        store.wait()


def on_device(hidden, w_query, nbr_keys, nbr_values, nbr_ids, d_attended):
    vmem = pltpu.VMEM
    anywhere = pl.BlockSpec(memory_space=pl.ANY)
    in_vmem = pl.BlockSpec(memory_space=pltpu.VMEM)
    attended, d_hidden, d_wq, d_keys, d_values = pl.pallas_call(
        kernel,
        out_shape=(
            jax.ShapeDtypeStruct((128, 2048), BF16),
            jax.ShapeDtypeStruct((128, 4096), BF16),
            jax.ShapeDtypeStruct((512, 128), F32),
            jax.ShapeDtypeStruct((4, 128, 2048), BF16),
            jax.ShapeDtypeStruct((4, 128, 2048), BF16),
        ),
        in_specs=[anywhere, anywhere, anywhere, anywhere, in_vmem, anywhere],
        out_specs=[anywhere] * 5,
        scratch_shapes=[
            vmem((256, 4096), BF16),
            *[vmem((16, 256, 512), BF16)] * 2,
            *[vmem((8, 128, 512), BF16)] * 4,
            vmem((16, 64, 1024), BF16),
            *[vmem((16, 64, 512), BF16)] * 2,
            vmem((256, 512), F32),
            vmem((1024, 1024), BF16),
            vmem((1024, 1024), BF16),
            vmem((32, 128, 128), F32),
            vmem((32, 128, 128), F32),
            vmem((32, 128, 128), BF16),
            vmem((32, 128, 128), BF16),
            *[vmem((4, 8, 8, 128), F32)] * 2,
            *[vmem((SLOTS, 64, 512), BF16)] * 8,
            *[vmem((SLOTS + 1, 128, 512), BF16)] * 2,
            *[vmem((8, 128, 1024), BF16)] * 2,
            vmem((256, 1024), BF16),
            *[vmem((16, 64, 512), BF16)] * 2,
            vmem((4, 4, 512, 128), BF16),
            vmem((4, 512, 128), BF16),
            vmem((4, 512, 128), BF16),
            vmem((128, 4096), F32),
            vmem((128, 4096), F32),
            vmem((128, 4096), F32),
            vmem((128, 4096), BF16),
            vmem((512, 128), F32),
            vmem((8, 128), jnp.int32),
            vmem((8, 8, 128), jnp.int32),
            pltpu.SMEM((8, 8, 128), jnp.int32),
            pltpu.SemaphoreType.DMA((N_SEMS,)),
            pltpu.SemaphoreType.DMA((N_SEMS,)),
        ],
        compiler_params=pltpu.CompilerParams(
            collective_id=0, has_side_effects=True, vmem_limit_bytes=62 * 2**20
        ),
        name="group_attention",
    )(hidden, w_query, nbr_keys, nbr_values, nbr_ids, d_attended.reshape(2, 64, 2048))
    parts = (attended, d_hidden, d_wq, d_keys.reshape(512, 2048), d_values.reshape(512, 2048))
    kinds = (BF16, BF16, F32, F32, F32)
    attended, d_hidden, d_wq, d_keys, d_values = pl.pallas_call(
        finish,
        out_shape=[jax.ShapeDtypeStruct(p.shape, kind) for p, kind in zip(parts, kinds)],
        in_specs=[anywhere] * 5,
        out_specs=[anywhere] * 5,
        scratch_shapes=[
            *[vmem(p.shape, p.dtype) for p in parts],
            *[vmem((512, 2048), F32)] * 2,
            *[pltpu.SemaphoreType.DMA((2 * FINISH_PARTS + 3,))] * 2,
        ],
        compiler_params=pltpu.CompilerParams(vmem_limit_bytes=60 * 2**20),
        name="finish",
    )(*parts)
    return attended, d_hidden, d_wq, d_keys.reshape(4, 128, 2048), d_values.reshape(4, 128, 2048)


def solution(mesh):
    placed = (
        P(("dp", "seq"), None),
        P("dp", None),
        P(("dp", "seq"), None, None),
        P(("dp", "seq"), None, None),
        P(("dp", "seq"), None),
        P(("dp", "seq"), None),
    )
    return jax.shard_map(
        on_device,
        mesh=mesh,
        in_specs=placed,
        out_specs=(
            P(("dp", "seq"), None),
            P(("dp", "seq"), None),
            P("seq", "dp"),
            P(("dp", "seq"), None, None),
            P(("dp", "seq"), None, None),
        ),
        check_vma=False,
    )
```

```python
import functools

import jax
import jax.numpy as jnp
from jax import lax
from jax.experimental import pallas as pl
from jax.experimental.pallas import tpu as pltpu
from jax.sharding import PartitionSpec as P

BF16 = jnp.bfloat16
F32 = jnp.float32
MESH = pl.DeviceIdType.MESH
HEAD = 128
SCALE = HEAD ** (-0.5)
BLOCK = 64
NLEN = 128


class Pool:
    def __init__(self):
        self.used = 0

    def take(self, count):
        first = self.used
        self.used += count
        return first


POOL = Pool()
S_W = POOL.take(80)
S_KV = POOL.take(4)
S_DO = POOL.take(1)
S_GG = POOL.take(6)
S_ID = POOL.take(8)
S_HID = POOL.take(1)
S_Q = POOL.take(12)
S_HS = POOL.take(4)
S_HF = POOL.take(4)
S_ST = POOL.take(8)
S_RET = POOL.take(16)
S_DQ = POOL.take(12)
S_DKV = POOL.take(2)
S_ATT = POOL.take(1)
S_DH = POOL.take(1)
S_R1 = POOL.take(16)
S_R2 = POOL.take(4)
S_LOCAL = POOL.take(16)
N_SEMS = POOL.used
SLOTS = 16


def dot(a, b, dims=((1,), (0,))):
    return lax.dot_general(a, b, (dims, ((), ())), preferred_element_type=F32)


def kernel(
    hidden, weight, keys, values, ids, grads,
    att_out, dh_out, dwq_out, dk_out, dv_out,
    hid, wb0, wb1, kc0, kc1, vc0, vc1, gg, qg0, qg1, qacc, hs, ht, st_buf, dp_buf, low_buf, ds_buf, stat0, stat1,
    sa0, sa1, sd0, sd1, ra0, ra1, rd0, rd1, ck, cv, dks, dvs, att_s, dqg0, dqg1,
    r1, r1s, r2, dhs, dho, dhr, dh_s, dwq_s, idv, idg, ids_s, ssem, rsem,
):
    dp = lax.axis_index("dp")
    seq = lax.axis_index("seq")
    x, z = dp // 4, dp % 4
    y, c = seq // 2, seq % 2
    wb, kc, vc, qg, stat = (wb0, wb1), (kc0, kc1), (vc0, vc1), (qg0, qg1), (stat0, stat1)
    sa, sd, ra, rd, dqg = (sa0, sa1), (sd0, sd1), (ra0, ra1), (rd0, rd1), (dqg0, dqg1)

    def remote(src, dst, sem, to):
        return pltpu.make_async_remote_copy(
            src_ref=src, dst_ref=dst, send_sem=ssem.at[sem], recv_sem=rsem.at[sem],
            device_id=to, device_id_type=MESH,
        )

    def local(src, dst, sem):
        return pltpu.make_async_copy(src, dst, ssem.at[S_LOCAL + sem])

    def peer(dy, dc):
        return ((y + dy + 4) % 4) * 2 + (c + dc) % 2

    def wide(core):
        return pl.ds(pl.multiple_of(core * 1024, 1024), 1024)

    def chunk(core, ch):
        return pl.ds(pl.multiple_of(core * 1024 + ch * 512, 512), 512)

    sibling = peer(0, 1)
    others = [(dy, dc) for dy in (1, 3, 2, 0) for dc in (0, 1) if (dy, dc) != (0, 0)]

    idv[...] = jnp.zeros_like(idv)
    idv[0:2, 0:2] = ids[...]

    own_w = [local(weight.at[:, chunk(c, ch)], wb[ch].at[dp], ch) for ch in range(2)]
    own_hid = local(hidden, hid.at[pl.ds(pl.multiple_of(c * 128, 128), 128)], 2)
    own_blocks = pl.ds(4 * y + 2 * c, 2)
    own_do = local(grads.at[:, :, wide(c)], gg.at[own_blocks], 3)
    own_rows = pl.ds(4 * c, 4)
    own_kv = [
        local(src.at[:, :, chunk(c, ch)], dst[ch].at[own_rows], 4 + 2 * i + ch)
        for i, (src, dst) in enumerate(((keys, kc), (values, vc))) for ch in range(2)
    ]
    for copy in own_w + [own_hid, own_do] + own_kv:
        copy.start()

    barrier = pltpu.get_barrier_semaphore()

    def greet(to):
        pl.semaphore_signal(barrier, inc=1, device_id=to, device_id_type=MESH)

    for dy, dc in others:
        greet((dp, peer(dy, dc)))
    for step in (1, 2, 3):
        for core in (0, 1):
            greet((((x + step) % 4) * 4 + z, y * 2 + core))
            greet((x * 4 + (z + step) % 4, y * 2 + core))
    pl.semaphore_wait(barrier, 7 + 12)

    def moved(axis, step):
        if axis == 0:
            return (((x + step + 4) % 4) * 4 + z, seq)
        return (x * 4 + (z + step + 4) % 4, seq)

    def source(t, r1_, r2_):
        rx, rz = (r1_, r2_) if t == 0 else (r2_, r1_)
        return ((x + rx + 4) % 4) * 4 + (z + rz + 4) % 4

    LINE = (0, -1, 1, 2)
    PART = {"all": (0, 128), "lo": (0, 64), "hi": (64, 64)}

    def piece(ch, t, r1_, r2_, part):
        lo, n = PART[part]
        return wb[ch].at[source(t, r1_, r2_), pl.ds(t * 128 + lo, n)]

    def w_parts(ch, t, phase, q, slot):
        axis = t if phase == 1 else 1 - t
        sem = S_W + 40 * ch + 20 * t + (slot if phase == 1 else 4 + 4 * q + slot)
        step = 1 if slot % 2 == 0 else -1
        return axis, sem, step, "all" if slot < 2 else ("lo" if slot == 2 else "hi")

    def w_copy(ch, t, phase, q, slot):
        axis, sem, step, part = w_parts(ch, t, phase, q, slot)
        near = 0 if slot < 2 else -step
        src = piece(ch, t, near, 0, part) if phase == 1 else piece(ch, t, LINE[q], near, part)
        return remote(src, src, sem, moved(axis, step))

    def w_recv(ch, t, phase, q, slot):
        axis, sem, step, part = w_parts(ch, t, phase, q, slot)
        far = -step if slot < 2 else 2
        dst = piece(ch, t, far, 0, part) if phase == 1 else piece(ch, t, LINE[q], far, part)
        remote(dst, dst, sem, moved(axis, step)).wait_recv()

    sent = []

    def go(copy):
        copy.start()
        sent.append(copy)

    def w_wave(ch, wave):
        if wave == 0:
            own_w[ch].wait()
            for phase in (1, 2):
                for t in (0, 1):
                    for slot in (0, 1):
                        go(w_copy(ch, t, phase, 0, slot))
        elif wave == 1:
            for t in (0, 1):
                for slot, q in ((0, 1), (1, 2)):
                    w_recv(ch, t, 1, 0, slot)
                    go(w_copy(ch, t, 1, 0, slot + 2))
                    for s in (0, 1):
                        go(w_copy(ch, t, 2, q, s))
        elif wave == 3:
            for t in (0, 1):
                for slot in (2, 3):
                    w_recv(ch, t, 1, 0, slot)
                for s in (0, 1):
                    go(w_copy(ch, t, 2, 3, s))
        else:
            for q in {2: (0,), 4: (1, 2), 5: (3,)}[wave]:
                for t in (0, 1):
                    for slot in (0, 1):
                        w_recv(ch, t, 2, q, slot)
                        go(w_copy(ch, t, 2, q, slot + 2))

    RING_LO = (0, 2, 2, 0, 0, 2)

    def ring_copy(ref, sem, slot):
        step = 1 if slot % 2 == 0 else -1
        near = y if slot < 4 else (y - step + 4) % 4
        part = ref.at[pl.ds(4 * near + RING_LO[slot], 2)]
        return remote(part, part, sem + slot, (dp, peer(step, 0)))

    def ring_recv(ref, sem, slot):
        step = 1 if slot % 2 == 0 else -1
        far = (y - step + 4) % 4 if slot < 4 else (y + 2) % 4
        part = ref.at[pl.ds(4 * far + RING_LO[slot], 2)]
        remote(part, part, sem + slot, (dp, peer(step, 0))).wait_recv()

    def ring_send(ref, sem):
        for slot in range(4):
            go(ring_copy(ref, sem, slot))

    def ring_forward(ref, sem):
        for slot in (0, 1):
            ring_recv(ref, sem, slot)
            go(ring_copy(ref, sem, slot + 4))

    def ring_finish(ref, sem):
        for slot in (2, 3, 4, 5):
            ring_recv(ref, sem, slot)

    def project(ch, rx):
        @pl.loop(0, 4)
        def _(i):
            d = ((x + rx + 4) % 4) * 4 + i
            rows = hid[:, pl.ds(pl.multiple_of(d * 256, 256), 256)]
            for n in range(2):
                span = slice(n * 256, n * 256 + 256)
                qacc[:, span] += dot(rows, wb[ch][d, :, span])

    def query(ch):
        qacc[...] = jnp.zeros_like(qacc)
        for q, rx in ((0, 0), (1, -1), (2, 1)):
            for slot in (2, 3):
                w_recv(ch, 0, 2, q, slot)
            project(ch, rx)
        for slot in (2, 3):
            w_recv(ch, 0, 2, 3, slot)
            for q in range(4):
                w_recv(ch, 1, 2, q, slot)
        project(ch, 2)
        qg[ch][pl.ds(4 * y, 4)] = qacc[...].astype(BF16).reshape(4, BLOCK, 512)
        ring_send(qg[ch], S_Q + 6 * ch)

    def span256(k):
        return pl.ds(pl.multiple_of(k * 256, 256), 256)

    def feats(k):
        return pl.ds(pl.multiple_of(k * 1024, 1024), 1024)

    def tokens(s):
        return pl.ds(pl.multiple_of(s * 128, 128), 128)

    own_hid_rows = hid.at[tokens(c)]
    hidden_out = []

    def send_hidden():
        for dy in (1, 3, 2):
            to = peer(dy, 0)
            go(remote(own_hid_rows.at[:, feats(to // 2)], hs.at[tokens(seq)], S_HS + dy, (dp, to)))
        hs[span256(y), :] = hid[:, feats(y)]

    def forward_hidden():
        for dy in (1, 3, 2):
            frm = peer(-dy, 0)
            ref = hs.at[tokens(frm)]
            remote(ref, ref, S_HS + dy, (dp, frm)).wait_recv()
            hidden_out.append(remote(ref, ref, S_HF + dy, (dp, sibling)))
            hidden_out[-1].start()

    def slot_of(s, core):
        shard = 2 * y + core
        block, row, other = jnp.int32(0), jnp.int32(0), jnp.int32(0)
        for j in range(4):
            here = ids_s[s, j // 2, j % 2]
            hit = here // 4 == shard
            block = jnp.where(hit, j // 2, block)
            row = jnp.where(hit, here % 4, row)
            other = jnp.where(hit, ids_s[s, j // 2, 1 - j % 2], other)
        return 2 * s + block, 4 * core + row, other

    def diagonal(a, b):
        none = jnp.zeros((BLOCK, HEAD), BF16)
        return jnp.concatenate(
            [jnp.concatenate([a, none], axis=1), jnp.concatenate([none, b], axis=1)], axis=0
        )

    def operands(ch, e, b0, k0, b1, k1):
        lanes = slice(e * HEAD, e * HEAD + HEAD)
        far = slice(ch * 512 + e * HEAD, ch * 512 + e * HEAD + HEAD)
        kk = jnp.concatenate([kc[ch][k0, :, lanes], kc[ch][k1, :, lanes]], axis=1)
        vv = jnp.concatenate([vc[ch][k0, :, lanes], vc[ch][k1, :, lanes]], axis=1)
        qq = diagonal(qg[ch][b0, :, lanes], qg[ch][b1, :, lanes])
        dd = diagonal(gg[b0, :, far], gg[b1, :, far])
        return lanes, kk, vv, qq, dd

    def first_pass(ch):
        @pl.loop(0, 8)
        def _(s):
            b0, k0, _o0 = slot_of(s, 0)
            b1, k1, _o1 = slot_of(s, 1)
            for e in range(4):
                _, kk, vv, qq, dd = operands(ch, e, b0, k0, b1, k1)
                scores = dot(kk, qq, ((1,), (1,))) * SCALE
                d_probs = dot(vv, dd, ((1,), (1,)))
                peak = jnp.max(scores, axis=0, keepdims=True)
                expo = jnp.exp(scores - peak)
                total = jnp.sum(expo, axis=0, keepdims=True)
                st_buf[4 * s + e] = scores
                dp_buf[4 * s + e] = d_probs
                stat[ch][y, s, e:e + 1] = peak + jnp.log(total)
                stat[ch][y, s, 4 + e:5 + e] = jnp.sum(expo * d_probs, axis=0, keepdims=True) / total
        for dy in (1, 3, 2):
            go(remote(stat[ch].at[y], stat[ch].at[y], S_ST + 4 * ch + dy, (dp, peer(dy, 0))))

    def wait_stats(ch):
        for dy in (1, 3, 2):
            frm = peer(-dy, 0)
            ref = stat[ch].at[frm // 2]
            remote(ref, ref, S_ST + 4 * ch + dy, (dp, frm)).wait_recv()

    def second_pass(ch):
        left = lax.broadcasted_iota(jnp.int32, (8, 128), 1) < BLOCK

        @pl.loop(0, 8)
        def _(s):
            b0, k0, o0 = slot_of(s, 0)
            b1, k1, o1 = slot_of(s, 1)
            theirs0 = stat[ch][o0 // 8, s]
            theirs1 = stat[ch][o1 // 8, s]
            turned0 = jnp.concatenate([theirs0[:, BLOCK:], theirs0[:, :BLOCK]], axis=1)
            turned1 = jnp.concatenate([theirs1[:, BLOCK:], theirs1[:, :BLOCK]], axis=1)
            theirs0 = jnp.where((o0 // 4) % 2 == 0, theirs0, turned0)
            theirs1 = jnp.where((o1 // 4) % 2 == 1, theirs1, turned1)
            theirs = jnp.where(left, theirs0, theirs1)
            ours = stat[ch][y, s]
            top = jnp.maximum(ours[:4], theirs[:4])
            whole = top + jnp.log(jnp.exp(ours[:4] - top) + jnp.exp(theirs[:4] - top))
            delta = jnp.exp(ours[:4] - whole) * ours[4:] + jnp.exp(theirs[:4] - whole) * theirs[4:]
            for e in range(4):
                lanes, kk, _, _, _ = operands(ch, e, b0, k0, b1, k1)
                probs = jnp.exp(st_buf[4 * s + e] - whole[e:e + 1])
                low = probs.astype(BF16)
                d_scores = (probs * (dp_buf[4 * s + e] - delta[e:e + 1]) * SCALE).astype(BF16)
                dq = dot(d_scores, kk, ((0,), (0,))).astype(BF16)
                sd[ch][2 * s, :, lanes] = dq[:BLOCK, :HEAD]
                sd[ch][2 * s + 1, :, lanes] = dq[BLOCK:, HEAD:]
                low_buf[4 * s + e] = low
                ds_buf[4 * s + e] = d_scores

    def third_pass(ch):
        @pl.loop(0, 8)
        def _(s):
            b0, k0, _o0 = slot_of(s, 0)
            b1, k1, _o1 = slot_of(s, 1)
            for e in range(4):
                lanes, _, vv, qq, dd = operands(ch, e, b0, k0, b1, k1)
                low, d_scores = low_buf[4 * s + e], ds_buf[4 * s + e]
                att = dot(low, vv, ((0,), (0,))).astype(BF16)
                sa[ch][2 * s, :, lanes] = att[:BLOCK, :HEAD]
                sa[ch][2 * s + 1, :, lanes] = att[BLOCK:, HEAD:]
                dk = dot(d_scores, qq).astype(BF16)
                dv = dot(low, dd).astype(BF16)
                for i in range(2):
                    ck[2 * s + i, :, lanes] = dk[:, i * HEAD:(i + 1) * HEAD]
                    cv[2 * s + i, :, lanes] = dv[:, i * HEAD:(i + 1) * HEAD]

    def give_back(ch, kind):
        src, dst = ((sd, rd), (sa, ra))[kind]
        for dy in (1, 3, 2) if kind == 0 else (2, 1, 3):
            to = peer(dy, 0)
            go(remote(
                src[ch].at[pl.ds(4 * (to // 2), 4)], dst[ch].at[pl.ds(4 * y, 4)],
                S_RET + 8 * kind + 4 * ch + dy, (dp, to),
            ))
        dst[ch][pl.ds(4 * y, 4)] = src[ch][pl.ds(4 * y, 4)]

    def take_back(ch, kind):
        src, dst = ((sd, rd), (sa, ra))[kind]
        for dy in (1, 3, 2):
            frm = peer(-dy, 0)
            ref = dst[ch].at[pl.ds(4 * (frm // 2), 4)]
            remote(ref, ref, S_RET + 8 * kind + 4 * ch + dy, (dp, frm)).wait_recv()
        for block in range(4):
            core, u = block // 2, block % 2
            total = jnp.zeros((BLOCK, 512), F32)
            for j in range(2):
                name = ids_s[2 * y + core, u, j]
                total += dst[ch][(name // 8) * 4 + core * 2 + (name // 4) % 2].astype(F32)
            if kind == 0:
                dqg[ch][4 * y + block] = total.astype(BF16)
            else:
                att_s[block * BLOCK:(block + 1) * BLOCK, ch * 512:(ch + 1) * 512] = total.astype(BF16)

    def sum_kv(ch):
        @pl.loop(0, 8)
        def _(row):
            at = []
            for s in range(8):
                one = jnp.int32(SLOTS)
                for j in range(4):
                    one = jnp.where(ids_s[s, j // 2, j % 2] == 8 * y + row, 2 * s + row // 4, one)
                at.append(one)
            for src, dst in ((ck, dks), (cv, dvs)):
                for e in range(4):
                    lanes = slice(e * HEAD, e * HEAD + HEAD)
                    total = src[at[0], :, lanes].astype(F32)
                    for s in range(1, 8):
                        total += src[at[s], :, lanes].astype(F32)
                    dst[row, :, ch * 512 + e * HEAD:ch * 512 + (e + 1) * HEAD] = total.astype(BF16)

    def wq_grad(k):
        ch, pair = k // 2, k % 2
        both = dqg[ch][:, :, pair * 256:pair * 256 + 256].reshape(1024, 256)
        for m in range(4):
            hs[m * 256:m * 256 + 256, k * 256:k * 256 + 256] = dot(
                ht[m * 256:m * 256 + 256, :], both
            ).astype(BF16)

    def r1_copy(core, ch, b):
        src = hs.at[pl.ds(core * 512, 512), pl.ds((4 * ch + b) * HEAD, HEAD)]
        slot, part, dest = z, 2 * c + ch, x * 4 + b
        dst = r1.at[slot, part]
        sem = ssem.at[S_R1 + core * 8 + ch * 4 + b]
        own = jnp.logical_and(dest == dp, c == core)
        return src, dst, sem, rsem.at[S_R1 + slot * 4 + part], (dest, y * 2 + core), own

    def r1_start(core, ch, b):
        src, dst, s_sem, r_sem, dest, own = r1_copy(core, ch, b)

        @pl.when(own)
        def _():
            pltpu.make_async_copy(src, dst, s_sem).start()

        @pl.when(jnp.logical_not(own))
        def _():
            pltpu.make_async_remote_copy(
                src_ref=src, dst_ref=dst, send_sem=s_sem, recv_sem=r_sem, device_id=dest, device_id_type=MESH
            ).start()

    def r1_wait(core, ch, b):
        src, dst, s_sem, r_sem, dest, own = r1_copy(core, ch, b)

        @pl.when(own)
        def _():
            pltpu.make_async_copy(src, dst, s_sem).wait()

        @pl.when(jnp.logical_not(own))
        def _():
            pltpu.make_async_remote_copy(
                src_ref=src, dst_ref=dst, send_sem=s_sem, recv_sem=r_sem, device_id=dest, device_id_type=MESH
            ).wait_send()

    def wq_send(k):
        wq_grad(k)
        for b in (2 * (k % 2), 2 * (k % 2) + 1):
            for core in range(2):
                r1_start(core, k // 2, b)

    w_wave(0, 0)
    own_hid.wait()
    go(remote(own_hid_rows, own_hid_rows, S_HID, (dp, sibling)))
    go(remote(grads.at[:, :, wide(1 - c)], gg.at[own_blocks], S_DO, (dp, sibling)))
    for j, (dy, dc) in enumerate(others):
        go(remote(idv, idg.at[seq], S_ID + j, (dp, peer(dy, dc))))
    for i, (src, dst) in enumerate(((keys, kc), (values, vc))):
        for ch in range(2):
            go(remote(src.at[:, :, chunk(1 - c, ch)], dst[ch].at[own_rows], S_KV + 2 * i + ch, (dp, sibling)))
    w_wave(0, 1)
    their_blocks = gg.at[pl.ds(4 * y + 2 * (1 - c), 2)]
    remote(their_blocks, their_blocks, S_DO, (dp, sibling)).wait_recv()
    own_do.wait()
    ring_send(gg, S_GG)
    w_wave(0, 2)
    w_wave(0, 3)
    w_wave(1, 0)
    other_rows = hid.at[tokens(1 - c)]
    remote(other_rows, other_rows, S_HID, (dp, sibling)).wait_recv()
    w_wave(0, 4)
    ring_forward(gg, S_GG)
    w_wave(0, 5)
    for j, (dy, dc) in enumerate(others):
        frm = peer(-dy, -dc + 2)
        remote(idv, idg.at[frm], S_ID + j, (dp, frm)).wait_recv()
    idg[seq] = idv[...]
    to_smem = local(idg, ids_s, 8)
    to_smem.start()
    to_smem.wait()
    query(0)
    w_wave(1, 1)
    w_wave(1, 2)
    ck[SLOTS] = jnp.zeros((NLEN, 512), BF16)
    cv[SLOTS] = jnp.zeros((NLEN, 512), BF16)
    for copy in own_kv:
        copy.wait()
    their_rows = pl.ds(4 * (1 - c), 4)
    for i, dst in enumerate((kc, vc)):
        for ch in range(2):
            ref = dst[ch].at[their_rows]
            remote(ref, ref, S_KV + 2 * i + ch, (dp, sibling)).wait_recv()
    ring_forward(qg[0], S_Q)
    send_hidden()
    w_wave(1, 3)
    w_wave(1, 4)
    ring_finish(gg, S_GG)
    ring_finish(qg[0], S_Q)
    first_pass(0)
    w_wave(1, 5)
    def dh_add(ch, first):
        @pl.loop(0, 16)
        def _(d):
            for core, buf in ((1 - c, dhs), (c, dho)):
                rows = dqg[ch][pl.ds(4 * y + 2 * core, 2)].reshape(128, 512)
                part = dot(rows, wb[ch][d], ((1,), (1,)))
                if first:
                    buf[:, span256(d)] = part
                else:
                    buf[:, span256(d)] += part

    query(1)
    wait_stats(0)
    second_pass(0)
    ring_forward(qg[1], S_Q + 6)
    give_back(0, 0)
    third_pass(0)
    sum_kv(0)
    ring_finish(qg[1], S_Q + 6)
    first_pass(1)
    take_back(0, 0)
    ring_send(dqg[0], S_DQ)
    wait_stats(1)
    second_pass(1)
    give_back(1, 0)
    forward_hidden()
    ring_forward(dqg[0], S_DQ)
    third_pass(1)
    for dy in (1, 3, 2):
        frm = peer(-dy, 1)
        ref = hs.at[tokens(frm)]
        remote(ref, ref, S_HF + dy, (dp, sibling)).wait_recv()

    @pl.loop(0, 4)
    def _(m):
        ht[span256(m), :] = jnp.transpose(hs[:, span256(m)])

    for copy in hidden_out:
        copy.wait_send()
    dh_add(0, True)
    take_back(1, 0)
    ring_send(dqg[1], S_DQ + 6)
    ring_finish(dqg[0], S_DQ)
    wq_send(0)
    ring_forward(dqg[1], S_DQ + 6)
    give_back(0, 1)
    give_back(1, 1)
    wq_send(1)
    sum_kv(1)
    their_kv = []
    for i, (src, dst) in enumerate(((dks, dk_out), (dvs, dv_out))):
        go(remote(src.at[their_rows], dst.at[:, :, wide(c)], S_DKV + i, (dp, sibling)))
        their_kv.append(remote(src.at[their_rows], dst.at[:, :, wide(1 - c)], S_DKV + i, (dp, sibling)))
    own_kv_out = [
        local(src.at[own_rows], dst.at[:, :, wide(c)], 9 + i)
        for i, (src, dst) in enumerate(((dks, dk_out), (dvs, dv_out)))
    ]
    for copy in own_kv_out:
        copy.start()
    ring_finish(dqg[1], S_DQ + 6)
    wq_send(2)
    wq_send(3)
    dh_add(1, False)
    dh_copy = remote(dhs, dhr, S_DH, (dp, sibling))
    go(dh_copy)

    for core in range(2):
        for ch in range(2):
            for b in range(4):
                r1_wait(core, ch, b)

    @pl.loop(0, 16)
    def _(k):
        @pl.when(jnp.logical_not(jnp.logical_and(k // 4 == z, (k % 4) // 2 == c)))
        def _():
            ref = r1.at[k // 4, k % 4]
            pltpu.make_async_remote_copy(
                src_ref=ref, dst_ref=ref, send_sem=ssem.at[S_R1], recv_sem=rsem.at[S_R1 + k],
                device_id=(dp, sibling), device_id_type=MESH,
            ).wait_recv()

    def r2_copy(step):
        to = (x + step) % 4
        return remote(r1s.at[to], r2.at[step], S_R2 + step, (to * 4 + z, seq))

    for step in (1, 3, 2, 0):
        to = (x + step) % 4
        total = r1[0, to].astype(F32)
        for k in range(1, 4):
            total += r1[k, to].astype(F32)
        if step:
            r1s[to] = total.astype(BF16)
            go(r2_copy(step))
        else:
            dwq_s[...] = total
    take_back(0, 1)
    dh_copy.wait_recv()
    dh_s[...] = (dho[...] + dhr[...]).astype(BF16)
    late_out = [local(dh_s, dh_out, 12), local(dwq_s, dwq_out, 13)]
    late_out[0].start()
    for step in (1, 3, 2):
        r2_copy(step).wait_recv()
        dwq_s[...] += r2[step].astype(F32)
    late_out[1].start()
    take_back(1, 1)
    own_att = local(att_s.at[tokens(c)], att_out.at[:, wide(c)], 11)
    own_att.start()
    go(remote(att_s.at[tokens(1 - c)], att_out.at[:, wide(c)], S_ATT, (dp, sibling)))

    own_att.wait()
    for copy in late_out:
        copy.wait()
    remote(att_s.at[tokens(1 - c)], att_out.at[:, wide(1 - c)], S_ATT, (dp, sibling)).wait_recv()
    for copy in own_kv_out:
        copy.wait()
    for copy in their_kv:
        copy.wait_recv()
    for copy in sent:
        copy.wait_send()


FINISH_PARTS = 4


def finish(
    att_in, dh_in, dwq_in, dk_in, dv_in, att_out, dh_out, dwq_out, dk_out, dv_out,
    att, dh, dwq, dk, dv, dk_wide, dv_wide, in_sem, out_sem,
):
    rows = 512 // FINISH_PARTS
    loads, stores = [], []
    for k in range(FINISH_PARTS):
        span = pl.ds(k * rows, rows)
        for t, (src, dst) in enumerate(((dk_in, dk), (dv_in, dv))):
            loads.append(pltpu.make_async_copy(src.at[span], dst.at[span], in_sem.at[2 * k + t]))
    small = ((att_in, att, att_out), (dh_in, dh, dh_out), (dwq_in, dwq, dwq_out))
    for t, (src, mid, _) in enumerate(small):
        loads.append(pltpu.make_async_copy(src, mid, in_sem.at[2 * FINISH_PARTS + t]))
    for load in loads:
        load.start()
    for k in range(FINISH_PARTS):
        span = pl.ds(k * rows, rows)
        for t, (narrow, wide, dst) in enumerate(((dk, dk_wide, dk_out), (dv, dv_wide, dv_out))):
            loads[2 * k + t].wait()
            wide[span, :] = narrow[span, :].astype(F32)
            stores.append(pltpu.make_async_copy(wide.at[span], dst.at[span], out_sem.at[2 * k + t]))
            stores[-1].start()
    for t, (_, mid, dst) in enumerate(small):
        loads[2 * FINISH_PARTS + t].wait()
        stores.append(pltpu.make_async_copy(mid, dst, out_sem.at[2 * FINISH_PARTS + t]))
        stores[-1].start()
    for store in stores:
        store.wait()


def on_device(hidden, w_query, nbr_keys, nbr_values, nbr_ids, d_attended):
    vmem = pltpu.VMEM
    anywhere = pl.BlockSpec(memory_space=pl.ANY)
    in_vmem = pl.BlockSpec(memory_space=pltpu.VMEM)
    attended, d_hidden, d_wq, d_keys, d_values = pl.pallas_call(
        kernel,
        out_shape=(
            jax.ShapeDtypeStruct((128, 2048), BF16),
            jax.ShapeDtypeStruct((128, 4096), BF16),
            jax.ShapeDtypeStruct((512, 128), F32),
            jax.ShapeDtypeStruct((4, 128, 2048), BF16),
            jax.ShapeDtypeStruct((4, 128, 2048), BF16),
        ),
        in_specs=[anywhere, anywhere, anywhere, anywhere, in_vmem, anywhere],
        out_specs=[anywhere] * 5,
        scratch_shapes=[
            vmem((256, 4096), BF16),
            *[vmem((16, 256, 512), BF16)] * 2,
            *[vmem((8, 128, 512), BF16)] * 4,
            vmem((16, 64, 1024), BF16),
            *[vmem((16, 64, 512), BF16)] * 2,
            vmem((256, 512), F32),
            vmem((1024, 1024), BF16),
            vmem((1024, 1024), BF16),
            vmem((32, 128, 128), F32),
            vmem((32, 128, 128), F32),
            vmem((32, 128, 128), BF16),
            vmem((32, 128, 128), BF16),
            *[vmem((4, 8, 8, 128), F32)] * 2,
            *[vmem((SLOTS, 64, 512), BF16)] * 8,
            *[vmem((SLOTS + 1, 128, 512), BF16)] * 2,
            *[vmem((8, 128, 1024), BF16)] * 2,
            vmem((256, 1024), BF16),
            *[vmem((16, 64, 512), BF16)] * 2,
            vmem((4, 4, 512, 128), BF16),
            vmem((4, 512, 128), BF16),
            vmem((4, 512, 128), BF16),
            vmem((128, 4096), F32),
            vmem((128, 4096), F32),
            vmem((128, 4096), F32),
            vmem((128, 4096), BF16),
            vmem((512, 128), F32),
            vmem((8, 128), jnp.int32),
            vmem((8, 8, 128), jnp.int32),
            pltpu.SMEM((8, 8, 128), jnp.int32),
            pltpu.SemaphoreType.DMA((N_SEMS,)),
            pltpu.SemaphoreType.DMA((N_SEMS,)),
        ],
        compiler_params=pltpu.CompilerParams(
            collective_id=0, has_side_effects=True, vmem_limit_bytes=62 * 2**20
        ),
        name="group_attention",
    )(hidden, w_query, nbr_keys, nbr_values, nbr_ids, d_attended.reshape(2, 64, 2048))
    parts = (attended, d_hidden, d_wq, d_keys.reshape(512, 2048), d_values.reshape(512, 2048))
    kinds = (BF16, BF16, F32, F32, F32)
    attended, d_hidden, d_wq, d_keys, d_values = pl.pallas_call(
        finish,
        out_shape=[jax.ShapeDtypeStruct(p.shape, kind) for p, kind in zip(parts, kinds)],
        in_specs=[anywhere] * 5,
        out_specs=[anywhere] * 5,
        scratch_shapes=[
            *[vmem(p.shape, p.dtype) for p in parts],
            *[vmem((512, 2048), F32)] * 2,
            *[pltpu.SemaphoreType.DMA((2 * FINISH_PARTS + 3,))] * 2,
        ],
        compiler_params=pltpu.CompilerParams(vmem_limit_bytes=60 * 2**20),
        name="finish",
    )(*parts)
    return attended, d_hidden, d_wq, d_keys.reshape(4, 128, 2048), d_values.reshape(4, 128, 2048)


def solution(mesh):
    placed = (
        P(("dp", "seq"), None),
        P("dp", None),
        P(("dp", "seq"), None, None),
        P(("dp", "seq"), None, None),
        P(("dp", "seq"), None),
        P(("dp", "seq"), None),
    )
    return jax.shard_map(
        on_device,
        mesh=mesh,
        in_specs=placed,
        out_specs=(
            P(("dp", "seq"), None),
            P(("dp", "seq"), None),
            P("seq", "dp"),
            P(("dp", "seq"), None, None),
            P(("dp", "seq"), None, None),
        ),
        check_vma=False,
    )
```
